32 devices in a mesh: space: 8 (over y, x, core), vel: 4 (over z).
Axes of the slice: x: 2, y: 2, z: 4, core: 2. Of those that a mesh axis runs over, the one named last changes fastest.
Arguments:
- dist: float32 [512, 64, 4096], P('space', None, 'vel'), as said below
- cell_kind: int32 [512, 64], P('space'), may hold values from 0 to 2, as said below
- normal_code: int32 [512, 64], P('space'), may hold values from 0 to 3
- wall_temp: float32 [512, 64], P('space'), may hold values from 0.8 to 1.25
Outputs:
- evolved: float32 [512, 64, 4096], P('space', None, 'vel')
- wall_flux: float32 [512, 64], P('space', 'vel')
The draws below stay inside these ranges and needn't reach their ends.
Inputs may be any that keep to these rules, and one draw needn't show every extreme that they name: `cell_kind`: 0 is a gas cell, 1 a solid wall cell, 2 an evaporating meniscus cell. `normal_code`: normal into the gas: 0 rising rows, 1 falling rows, 2 rising columns, 3 falling columns; used only where cell_kind is not 0. `dist`: every population is positive.
All inputs are finite; a program needn't handle non-finite values.
Results may differ from the reference program's by a relative error of at most 0.0003.
Values sent between devices are 32-bit elements; how exact they have to be, the bound alone decides.
No kernel may reach another device: no remote copies, remote signals or barrier semaphores. Data moves between devices by JAX's collectives and lax.ppermute only.
A program may use at most 128 MiB of HBM per device.

```python
import math
import jax
import jax.numpy as jnp
from jax import lax

STRIP_SITES = 64
NQ = 16
STEPS = 4
STRIP_LINES = 512
NV = 4096


LIMIT = 5.0


def speed_grid(points, levels):
    spacing = 2.0 * LIMIT / levels
    first = points % levels
    second = points // levels % levels
    third = points // (levels * levels)
    picks = ((first + third) % levels, (second + third) % levels, (first + second + third) % levels)
    return tuple((-LIMIT + (pick.astype(jnp.float32) + 0.5) * spacing for pick in picks))


def draw_dist(key, part):
    key = jax.random.fold_in(key, 11)
    stochastic_seeds = jax.random.split(key, 4)
    particle_count_field = jnp.exp(jax.random.uniform(stochastic_seeds[0], (STRIP_LINES, STRIP_SITES, 1), jnp.float32, math.log(0.5), math.log(2.0)))
    drift = jax.random.uniform(stochastic_seeds[1], (3, STRIP_LINES, STRIP_SITES, 1), jnp.float32, -0.3, 0.3)
    cellwise_warmth = jnp.exp(jax.random.uniform(stochastic_seeds[2], (STRIP_LINES, STRIP_SITES, 1), jnp.float32, math.log(0.7), math.log(1.4)))
    jagged_interface = jax.random.uniform(stochastic_seeds[3], (STRIP_LINES, STRIP_SITES, NV), jnp.float32, 0.7, 1.4)
    speeds = speed_grid(jnp.arange(NV, dtype=jnp.int32), NQ)
    self_product = (speeds[0][None, None, :] - drift[0]) ** 2 + (speeds[1][None, None, :] - drift[1]) ** 2 + (speeds[2][None, None, :] - drift[2]) ** 2
    return particle_count_field * cellwise_warmth ** (-1.5) * jnp.exp(-self_product / (2.0 * cellwise_warmth)) * jagged_interface


def draw_cell_kind(key, part):
    key = jax.random.fold_in(key, 23)
    value = jax.random.randint(key, (STRIP_LINES, STRIP_SITES), 0, 8)
    return jnp.where(value >= 3, 0, value).astype(jnp.int32)


def with_ends(values, key, low, high):
    longest = values.shape.index(max(values.shape))
    spots = []
    for shift in (0, 1):
        where = [jax.random.randint(jax.random.fold_in(key, axis), (), 0, length) for axis, length in enumerate(values.shape)]
        where[longest] = (where[longest] + shift) % values.shape[longest]
        spots.append(tuple(where))
    return values.at[spots[0]].set(low).at[spots[1]].set(high)


def shard_levels(rng, shape, pieces, smallest, largest):
    loudness = 1.0
    for axis_at, parts in pieces:
        heights = jax.random.uniform(jax.random.fold_in(jax.random.fold_in(rng, 6), axis_at), (parts,), jnp.float32, smallest / len(pieces), largest / len(pieces))
        loudness = loudness * jnp.repeat(jnp.exp(heights), shape[axis_at] // parts).reshape((-1,) + (1,) * (len(shape) - 1 - axis_at))
    return loudness


def setup_inputs(seed: int = 0) -> dict:
    keys = jax.random.split(jax.random.key(seed), 5)
    return {
        "dist": draw_dist(jax.random.fold_in(keys[4], 71), 0),
        "cell_kind": draw_cell_kind(jax.random.fold_in(keys[4], 71), 0),
        "normal_code": with_ends(jax.random.randint(keys[2], (STRIP_LINES, STRIP_SITES), 0, 4), jax.random.fold_in(keys[2], 1), 0, 3).astype(jnp.int32),
        "wall_temp": jnp.clip(jnp.exp(math.log(1.25) - 0.4462871 * jax.random.uniform(keys[3], (STRIP_LINES, STRIP_SITES), jnp.float32) ** shard_levels(keys[3], (STRIP_LINES, STRIP_SITES), ((0, 8),), -0.2, 0.2)), 0.8, 1.25),
    }


LIMIT = 5.0
TIME_STEP = 0.05
SIGMA = 0.8
LATENT = 5.0
PRANDTL = 2.0 / 3.0
SHEAR_EXPONENT = 0.1


def velocity_grid(points, levels):
    spacing = 2.0 * LIMIT / levels
    first = points % levels
    second = (points // levels) % levels
    third = points // (levels * levels)
    picks = ((first + third) % levels, (second + third) % levels, (first + second + third) % levels)
    return tuple(-LIMIT + (pick.astype(jnp.float32) + 0.5) * spacing for pick in picks)


def quad_weight(levels):
    return (2.0 * LIMIT / levels) ** 3 / (2.0 * math.pi) ** 1.5


def moment_table(speeds, weight):
    along_x, along_y, along_z = speeds
    self_product = along_x * along_x + along_y * along_y + along_z * along_z
    listed = [jnp.ones_like(along_x), along_x, along_y, along_z, self_product,
              along_x * along_x, along_y * along_y, along_z * along_z,
              along_x * along_y, along_x * along_z, along_y * along_z,
              along_x * self_product, along_y * self_product, along_z * self_product]
    return jnp.stack(listed) * weight


def project_moments(values, table):
    return jnp.einsum("kv,nv->kn", table, values, precision=lax.Precision.HIGHEST)


def beam_warming(padded, drift, length, axis):
    centre = lax.slice_in_dim(padded, 2, 2 + length, axis=axis)
    below = lax.slice_in_dim(padded, 1, 1 + length, axis=axis)
    below_far = lax.slice_in_dim(padded, 0, length, axis=axis)
    above = lax.slice_in_dim(padded, 3, 3 + length, axis=axis)
    above_far = lax.slice_in_dim(padded, 4, 4 + length, axis=axis)
    ahead = drift > 0
    courant = jnp.abs(drift)
    near = jnp.where(ahead, below, above)
    distant = jnp.where(ahead, below_far, above_far)
    return (centre - 0.5 * courant * (3.0 * centre - 4.0 * near + distant)
            + 0.5 * courant * courant * (centre - 2.0 * near + distant))


def normal_speed(codes, speeds):
    column = codes[:, None]
    along_x = speeds[0][None, :]
    along_y = speeds[1][None, :]
    return jnp.where(column == 0, along_x, jnp.where(column == 1, -along_x,
                     jnp.where(column == 2, along_y, -along_y)))


def wall_mass(incident, norm, kinds, saturated):
    evaporating = jnp.where(kinds == 2.0, 1.0, 0.0)
    boundary = jnp.where(kinds > 0.0, 1.0, 0.0)
    emitted = evaporating * SIGMA * saturated + (1.0 - evaporating * SIGMA) * incident / norm
    return emitted, boundary * (emitted * norm - incident)


def gas_state(hydrodynamic_fields):
    particle_count_field = hydrodynamic_fields[0]
    mean_drift = [hydrodynamic_fields[1] / particle_count_field, hydrodynamic_fields[2] / particle_count_field, hydrodynamic_fields[3] / particle_count_field]
    mean_drift_norm = mean_drift[0] * mean_drift[0] + mean_drift[1] * mean_drift[1] + mean_drift[2] * mean_drift[2]
    cellwise_warmth = (hydrodynamic_fields[4] / particle_count_field - mean_drift_norm) / 3.0
    flow_dot = mean_drift[0] * hydrodynamic_fields[1] + mean_drift[1] * hydrodynamic_fields[2] + mean_drift[2] * hydrodynamic_fields[3]
    second = [[hydrodynamic_fields[5], hydrodynamic_fields[8], hydrodynamic_fields[9]],
              [hydrodynamic_fields[8], hydrodynamic_fields[6], hydrodynamic_fields[10]],
              [hydrodynamic_fields[9], hydrodynamic_fields[10], hydrodynamic_fields[7]]]
    thermal_current = []
    for comp in range(3):
        value = (hydrodynamic_fields[11 + comp]
                 - 2.0 * (mean_drift[0] * second[comp][0] + mean_drift[1] * second[comp][1] + mean_drift[2] * second[comp][2])
                 + mean_drift_norm * hydrodynamic_fields[1 + comp] - mean_drift[comp] * hydrodynamic_fields[4]
                 + 2.0 * mean_drift[comp] * flow_dot - mean_drift[comp] * mean_drift_norm * particle_count_field)
        thermal_current.append(0.5 * value)
    return jnp.stack([particle_count_field] + mean_drift + [cellwise_warmth] + thermal_current)


def relax_shakhov(values, steam_distribution, speeds):
    particle_count_field, mean_drift_first, mean_drift_second, mean_drift_third, cellwise_warmth, thermal_current_first, thermal_current_second, thermal_current_third = [steam_distribution[placement_offset][:, None] for placement_offset in range(8)]
    peculiar_x = speeds[0][None, :] - mean_drift_first
    peculiar_y = speeds[1][None, :] - mean_drift_second
    peculiar_z = speeds[2][None, :] - mean_drift_third
    thermal_motion_norm = peculiar_x * peculiar_x + peculiar_y * peculiar_y + peculiar_z * peculiar_z
    isotropic_stress = particle_count_field * cellwise_warmth
    target_gaussian = particle_count_field * cellwise_warmth ** -1.5 * jnp.exp(-thermal_motion_norm / (2.0 * cellwise_warmth))
    factor = 1.0 + (1.0 - PRANDTL) * (peculiar_x * thermal_current_first + peculiar_y * thermal_current_second + peculiar_z * thermal_current_third) / (
        5.0 * isotropic_stress * cellwise_warmth) * (thermal_motion_norm / cellwise_warmth - 5.0)
    target = target_gaussian * factor
    collision_interval = SHEAR_EXPONENT * cellwise_warmth ** 0.72 / isotropic_stress
    return target + (values - target) * jnp.exp(-TIME_STEP / collision_interval)


def stream_block(block_values, speeds):
    nrows, ncols = block_values.shape[0], block_values.shape[1]
    padded = jnp.pad(block_values, ((2, 2), (0, 0), (0, 0)))
    rowwise = beam_warming(padded, speeds[0] * TIME_STEP, nrows, 0)
    padded = jnp.pad(rowwise, ((0, 0), (2, 2), (0, 0)))
    return beam_warming(padded, speeds[1] * TIME_STEP, ncols, 1)


def reference(dist, cell_kind, normal_code, wall_temp):
    nrows, ncols, nvel = dist.shape
    cell_count = nrows * ncols
    block = min(nvel, 256)
    blocks = nvel // block
    weight = quad_weight(NQ)
    kinds = cell_kind.reshape(cell_count).astype(jnp.float32)
    codes = normal_code.reshape(cell_count)
    wall_flat = wall_temp.reshape(cell_count)
    saturated = jnp.exp(LATENT * (1.0 - 1.0 / wall_flat)) / wall_flat

    def setup(block_no):
        start = (block_no * block).astype(jnp.int32)
        points = start + jnp.arange(block, dtype=jnp.int32)
        speeds = velocity_grid(points, NQ)
        table = moment_table(speeds, weight)
        facing = normal_speed(codes, speeds)
        emit = (kinds[:, None] > 0.0) & (facing > 0.0)
        self_product = speeds[0] * speeds[0] + speeds[1] * speeds[1] + speeds[2] * speeds[2]
        wall_maxwell = wall_flat[:, None] ** -1.5 * jnp.exp(-self_product[None, :] / (2.0 * wall_flat[:, None]))
        return start, speeds, table, facing, emit, wall_maxwell

    def fixed_pass(block_no, carry):
        norm, fixed_moments = carry
        start, speeds, table, facing, emit, wall_maxwell = setup(block_no)
        norm = norm + jnp.sum(jnp.maximum(facing, 0.0) * wall_maxwell, axis=1) * weight
        fixed_moments = fixed_moments + project_moments(jnp.where(emit, wall_maxwell, 0.0), table)
        return norm, fixed_moments

    norm, fixed_moments = lax.fori_loop(0, blocks, fixed_pass,
                                        (jnp.zeros((cell_count,), jnp.float32), jnp.zeros((14, cell_count), jnp.float32)))
    current = dist
    flux = jnp.zeros((cell_count,), jnp.float32)
    for repeat in range(STEPS):
        def first_pass(block_no, carry):
            incident, kept = carry
            start, speeds, table, facing, emit, wall_maxwell = setup(block_no)
            piece = lax.dynamic_slice_in_dim(current, start, block, 2)
            flat = stream_block(piece, speeds).reshape(cell_count, block)
            incident = incident + jnp.sum(jnp.maximum(-facing, 0.0) * flat, axis=1) * weight
            kept = kept + project_moments(jnp.where(emit, 0.0, flat), table)
            return incident, kept

        incident, kept = lax.fori_loop(0, blocks, first_pass,
                                       (jnp.zeros((cell_count,), jnp.float32), jnp.zeros((14, cell_count), jnp.float32)))
        emitted, flux = wall_mass(incident, norm, kinds, saturated)
        steam_distribution = gas_state(kept + emitted[None, :] * fixed_moments)

        def second_pass(block_no, result):
            start, speeds, table, facing, emit, wall_maxwell = setup(block_no)
            piece = lax.dynamic_slice_in_dim(current, start, block, 2)
            flat = stream_block(piece, speeds).reshape(cell_count, block)
            bounded = jnp.where(emit, emitted[:, None] * wall_maxwell, flat)
            fresh = relax_shakhov(bounded, steam_distribution, speeds).reshape(nrows, ncols, block)
            return lax.dynamic_update_slice_in_dim(result, fresh, start, 2)

        current = lax.fori_loop(0, blocks, second_pass, jnp.zeros_like(current))
    return current, flux.reshape(nrows, ncols)
```

```python
import functools
import math

import jax
import jax.numpy as jnp
from jax import lax
from jax.experimental import pallas as pl
from jax.experimental.pallas import tpu as pltpu
from jax.sharding import PartitionSpec as P

NQ = 16
STEPS = 4
LIMIT = 5.0
TIME_STEP = 0.05
SIGMA = 0.8
LATENT = 5.0
PRANDTL = 2.0 / 3.0
SHEAR_EXPONENT = 0.1

SPACING = 2.0 * LIMIT / NQ
HALF = 0.5 * SPACING
WEIGHT = SPACING**3 / (2.0 * math.pi) ** 1.5
LOG2E = math.log2(math.e)
LANES = 128
ROWS = 16
OFF = 1024.0

T_SQ_HI, T_SQ_LO, T_X, T_Y, T_Z, T_ONE = range(6)
P_ONE, P_X, P_Y, P_Z, P_XX, P_YY, P_ZZ, P_XY, P_XZ, P_YZ = range(6, 16)
P_XS, P_YS, P_ZS, P_XSL, P_YSL, P_ZSL = range(16, 22)
W_SQ_HI, W_SQ_LO, W_ONE, W_XP, W_XN, W_YP, W_YN = range(22, 29)
B_E, B_W = 29, 30
PART = 32
COEF = 128

VMEM_LIMIT = 60 * 1024 * 1024


def setup_kernel(span, target_ref, factor_ref, wall_ref, sums_ref, stencil_ref, spread_ref,
                 feature_ref, moment_ref):
    shape = (8, span)
    place = lax.broadcasted_iota(jnp.int32, shape, 1)
    third = lax.axis_index("vel") * (span // WIDE) + place // WIDE
    first = place % NQ
    middle = place // NQ % NQ

    def odd(pick):
        return (2 * (pick % NQ) - (NQ - 1)).astype(jnp.float32)

    x, y, z = odd(first + third), odd(middle), odd(first + middle)
    one = jnp.ones(shape, jnp.float32)
    square = x * x + y * y + z * z
    square_hi = jnp.floor(square * (1.0 / 16.0)) * 16.0
    square_lo = square - square_hi

    def split(v):
        hi = jnp.floor(v * (1.0 / 128.0)) * 128.0
        return hi, v - hi

    xs, xsl = split(x * square)
    ys, ysl = split(y * square)
    zs, zsl = split(z * square)
    xp = jnp.where(x > 0, 1.0, 0.0)
    yp = jnp.where(y > 0, 1.0, 0.0)
    features = [square_hi, square_lo, x, y, z, one,
                one, x, y, z, x * x, y * y, z * z, x * y, x * z, y * z, xs, ys, zs, xsl, ysl, zsl,
                square_hi, square_lo, one, xp, one - xp, yp, one - yp]
    feature_ref[...] = jnp.zeros_like(feature_ref)
    for k, feature in enumerate(features):
        feature_ref[k:k + 1, :] = feature[0:1]
    row = lax.broadcasted_iota(jnp.int32, (PART, span), 0)
    blank = jnp.zeros((COEF - 3 * PART, span), jnp.float32)
    for ref, low, high in ((target_ref, T_SQ_HI, P_ONE), (factor_ref, P_ONE, W_SQ_HI),
                           (wall_ref, W_SQ_HI, B_E)):
        chosen = jnp.where((row >= low) & (row < high), feature_ref[...], 0.0)
        ref[...] = jnp.concatenate([chosen, chosen, chosen, blank], axis=0).astype(jnp.bfloat16)
    quadrants = (xp * yp, xp * (one - yp), (one - xp) * yp, (one - xp) * (one - yp))
    moment = feature_ref[P_ONE:W_SQ_HI, :]
    moment_ref[...] = jnp.zeros_like(moment_ref)
    for k, quadrant in enumerate(quadrants):
        moment_ref[ROWS * k:ROWS * (k + 1), :] = moment * quadrant[0:1]
    for k, speed in enumerate((-x, x, -y, y)):
        moment_ref[4 * ROWS + k:4 * ROWS + k + 1, :] = jnp.maximum(speed, 0.0)[0:1]
    for l in range(span // LANES):
        cut = slice(l * LANES, (l + 1) * LANES)
        sums_ref[cut, :] = moment_ref[:, cut].T.astype(jnp.bfloat16)
    for k, v in enumerate((x, y)):
        courant = jnp.abs(v) * (HALF * TIME_STEP)
        half_square = 0.5 * courant * courant
        for n, value in enumerate((1.0 - 1.5 * courant + half_square, 2.0 * courant - 2.0 * half_square,
                                   half_square - 0.5 * courant, v)):
            stencil_ref[8 * (4 * k + n):8 * (4 * k + n + 1), :] = value
    row = lax.broadcasted_iota(jnp.int32, (COEF, 2 * LANES), 0)
    column = lax.broadcasted_iota(jnp.int32, (COEF, 2 * LANES), 1)
    want = jnp.where(column < LANES, B_E, B_W)
    hit = (row % PART == want) & (row < 3 * PART)
    spread_ref[...] = jnp.where(hit, 1.0, 0.0).astype(jnp.bfloat16)


def setup(span):
    table = jax.ShapeDtypeStruct((COEF, span), jnp.bfloat16)
    return pl.pallas_call(
        functools.partial(setup_kernel, span),
        out_shape=(table, table, table,
                   jax.ShapeDtypeStruct((span, LANES), jnp.bfloat16),
                   jax.ShapeDtypeStruct((64, span), jnp.float32),
                   jax.ShapeDtypeStruct((COEF, 2 * LANES), jnp.bfloat16)),
        out_specs=(pl.BlockSpec(memory_space=pltpu.VMEM),) * 6,
        scratch_shapes=[pltpu.VMEM((PART, span), jnp.float32), pltpu.VMEM((LANES, span), jnp.float32)],
        name="setup",
    )()


def turned(values, l, span, back=False):
    third = lax.axis_index("vel") * (span // WIDE) + l
    shift = NQ * (third % NQ)
    return pltpu.roll(values, (WIDE - shift) % WIDE if back else shift, 1)


def dot(a, b):
    return jnp.dot(a, b, preferred_element_type=jnp.float32)


def state_kernel(groups, with_edges, sums_ref, kind_ref, code_ref, temp_ref, first_ref, last_ref, spread_ref,
                 target_ref, factor_ref, wall_ref, coef_ref, flux_ref, *outer):
    stack_ref = outer[-1]

    def read(k, scale):
        return sums_ref[pl.ds(k, groups, stride=ROWS), :] * (WEIGHT * scale)

    kind = kind_ref[...]
    code = code_ref[...]
    wall = temp_ref[...]
    s0 = s1 = s2 = s3 = jnp.zeros_like(wall)
    inverse = 1.0 / wall
    for j in range(NQ // 2):
        speed = HALF * (2 * j + 1)
        e = jnp.exp(inverse * (-0.5 * speed * speed))
        s0, s1, s2, s3 = s0 + e, s1 + speed * e, s2 + speed**2 * e, s3 + speed**3 * e
    scale = (WEIGHT * 2.0) * inverse * lax.rsqrt(wall)
    norm = 2.0 * scale * s1 * s0 * s0
    f_one = 2.0 * scale * s0 * s0 * s0
    f_nn = 2.0 * scale * s2 * s0 * s0
    f_tt = f_nn
    f_ns = 2.0 * scale * (s3 * s0 * s0 + 2.0 * s1 * s2 * s0)
    saturated = jnp.exp(LATENT * (1.0 - inverse)) * inverse
    incident = read(13, HALF)
    share = jnp.where(kind == 2, SIGMA, 0.0)
    emitted = share * saturated + (1.0 - share) * incident / norm
    boundary = kind > 0
    flux_ref[...] = jnp.where(boundary, emitted * norm - incident, 0.0)
    em = jnp.where(boundary, emitted, 0.0)
    along_x = code < 2
    sign = jnp.where((code == 0) | (code == 2), 1.0, -1.0)
    sx = jnp.where(along_x, sign, 0.0)
    sy = jnp.where(along_x, 0.0, sign)

    rho = read(0, 1.0) + em * f_one
    em_n = em * norm
    em_s = em * f_ns
    mx = read(1, HALF) + sx * em_n
    my = read(2, HALF) + sy * em_n
    mz = read(3, HALF)
    mxx = read(4, HALF**2) + em * f_nn
    myy = read(5, HALF**2) + em * f_tt
    mzz = read(6, HALF**2) + em * f_tt
    mxy = read(7, HALF**2)
    mxz = read(8, HALF**2)
    myz = read(9, HALF**2)
    mxs = read(10, HALF**3) + sx * em_s
    mys = read(11, HALF**3) + sy * em_s
    mzs = read(12, HALF**3)
    msq = mxx + myy + mzz
    per = 1.0 / rho
    ux, uy, uz = mx * per, my * per, mz * per
    uu = ux * ux + uy * uy + uz * uz
    temp = (msq * per - uu) * (1.0 / 3.0)
    dotted = ux * mx + uy * my + uz * mz

    def heat(third, u, m, second):
        return 0.5 * (third - 2.0 * (ux * second[0] + uy * second[1] + uz * second[2]) + uu * m
                      - u * msq + 2.0 * u * dotted - u * uu * rho)

    qx = heat(mxs, ux, mx, (mxx, mxy, mxz))
    qy = heat(mys, uy, my, (mxy, myy, myz))
    qz = heat(mzs, uz, mz, (mxz, myz, mzz))
    pressure = rho * temp
    per_t = 1.0 / temp
    decay = jnp.exp((-TIME_STEP / SHEAR_EXPONENT) * pressure * jnp.exp(-0.72 * jnp.log(temp)))
    amount = (1.0 - decay) * rho * per_t * lax.rsqrt(temp)
    bend = amount * ((1.0 - PRANDTL) / 5.0) * per_t * per_t / pressure
    kappa = (0.5 * LOG2E) * per_t
    qu = qx * ux + qy * uy + qz * uz
    rest = uu - 5.0 * temp
    twice = -2.0 * bend * HALF**2
    kappa_sq = -kappa * HALF**2
    kappa_u = (2.0 * HALF) * kappa
    wall_sq = (-0.5 * LOG2E * HALF**2) * inverse
    bqu = bend * qu * HALF**2
    solid = jnp.where(boundary, OFF, 0.0)
    rows = {
        T_SQ_HI: kappa_sq, T_SQ_LO: kappa_sq,
        T_X: kappa_u * ux, T_Y: kappa_u * uy, T_Z: kappa_u * uz, T_ONE: -kappa * uu,
        P_ONE: amount - bend * qu * rest,
        P_X: bend * HALF * (qx * rest + 2.0 * qu * ux),
        P_Y: bend * HALF * (qy * rest + 2.0 * qu * uy),
        P_Z: bend * HALF * (qz * rest + 2.0 * qu * uz),
        P_XX: twice * qx * ux - bqu, P_YY: twice * qy * uy - bqu, P_ZZ: twice * qz * uz - bqu,
        P_XY: twice * (qx * uy + qy * ux), P_XZ: twice * (qx * uz + qz * ux),
        P_YZ: twice * (qy * uz + qz * uy),
        P_XS: bend * HALF**3 * qx, P_YS: bend * HALF**3 * qy, P_ZS: bend * HALF**3 * qz,
        W_SQ_HI: wall_sq, W_SQ_LO: wall_sq,
        W_ONE: jnp.where(boundary, 0.0, OFF),
        W_XP: jnp.where(code == 1, solid, 0.0), W_XN: jnp.where(code == 0, solid, 0.0),
        W_YP: jnp.where(code == 3, solid, 0.0), W_YN: jnp.where(code == 2, solid, 0.0),
        B_E: decay, B_W: em * decay * inverse * lax.rsqrt(wall),
    }
    rows[P_XSL], rows[P_YSL], rows[P_ZSL] = rows[P_XS], rows[P_YS], rows[P_ZS]
    zero = jnp.zeros_like(wall)
    for k in range(PART):
        value = rows.get(k)
        for part in range(3):
            if value is None:
                stack_ref[pl.ds(part * PART + k, groups, stride=COEF), :] = zero
                continue
            hi = value.astype(jnp.bfloat16).astype(jnp.float32)
            stack_ref[pl.ds(part * PART + k, groups, stride=COEF), :] = hi
            value = value - hi
    blank = jnp.zeros((COEF - 3 * PART, LANES), jnp.float32)

    def turn(g, carry):
        start = pl.multiple_of(g * COEF, COEF)
        block = jnp.concatenate([stack_ref[pl.ds(start, 3 * PART), :], blank], axis=0)
        coef_ref[pl.ds(start, LANES), :] = block.T.astype(jnp.bfloat16)
        return carry

    lax.fori_loop(0, groups, turn, 0, unroll=4)
    if not with_edges:
        return
    low_ref, high_ref = outer[:2]
    size = low_ref.shape[0]
    for flat_ref, start, out_ref in ((first_ref, 0, low_ref), (last_ref, groups * LANES - size, high_ref)):
        coef = coef_ref[start:start + size, :]
        even = dot(coef, spread_ref[...])
        for l in range(flat_ref.shape[1] // WIDE):
            columns = slice(l * WIDE, (l + 1) * WIDE)
            out_ref[:, columns] = relaxed(coef, even, flat_ref[:, columns], target_ref[:, columns],
                                          factor_ref[:, columns], wall_ref[:, columns])


def state(with_edges, sums, kind, code, temp, flat, spread, tables, ncols):
    groups = kind.shape[0]
    cells, span = flat.shape
    size = 2 * ncols
    last = cells // size - 1
    whole = pl.BlockSpec(memory_space=pltpu.VMEM)
    out_shape = (jax.ShapeDtypeStruct((cells, COEF), jnp.bfloat16),
                 jax.ShapeDtypeStruct((groups, LANES), jnp.float32))
    if with_edges:
        out_shape += (jax.ShapeDtypeStruct((size, span), jnp.float32),) * 2
    return pl.pallas_call(
        functools.partial(state_kernel, groups, with_edges),
        grid=(1,),
        out_shape=out_shape,
        in_specs=[whole] * 4 + [pl.BlockSpec((size, span), lambda i: (0, 0)),
                                pl.BlockSpec((size, span), lambda i: (last, 0))] + [whole] * 4,
        out_specs=(whole,) * len(out_shape),
        scratch_shapes=[pltpu.VMEM((groups * COEF, LANES), jnp.float32)],
        compiler_params=pltpu.CompilerParams(vmem_limit_bytes=VMEM_LIMIT),
        name="state",
    )(sums, kind, code, temp, flat, flat, spread, *tables)


CELLS = 256
WIDE = 256


def relaxed(coef, even, flat, target, factor, wall):
    exponent = dot(coef, target)
    factor = dot(coef, factor)
    wall = dot(coef, wall)
    decay, amount = even[:, :LANES], even[:, LANES:]
    parts = []
    for h in range(WIDE // LANES):
        cut = slice(h * LANES, (h + 1) * LANES)
        bounded = jnp.where(wall[:, cut] > 0.0, flat[:, cut] * decay, amount * jnp.exp2(wall[:, cut]))
        parts.append(bounded + jnp.exp2(exponent[:, cut]) * factor[:, cut])
    return jnp.concatenate(parts, axis=1)


def relax_tiles(cells, spread_ref, tables, coef_ref, even_ref, flat_ref, store):
    target_ref, factor_ref, wall_ref = tables
    span = flat_ref.shape[1]

    def block(b, carry):
        start = pl.multiple_of(b * CELLS, CELLS)
        coef = coef_ref[pl.ds(start, CELLS), :]
        even_ref[...] = dot(coef, spread_ref[...])
        for l in range(span // WIDE):
            columns = slice(l * WIDE, (l + 1) * WIDE)
            store(start, l, relaxed(coef, even_ref, flat_ref[pl.ds(start, CELLS), columns],
                                    target_ref[:, columns], factor_ref[:, columns], wall_ref[:, columns]))
        return carry

    lax.fori_loop(0, cells // CELLS, block, 0)


PAD = 8


def main_kernel(relax, exact, blocks, rows, ncols, flat_ref, coef_ref, low_ref, high_ref, kind_ref, code_ref,
                spread_ref, target_ref, factor_ref, wall_ref, sums_ref, stencil_ref,
                out_ref, parts_ref, field_ref, even_ref, strip_ref, half_ref):
    i = pl.program_id(0)
    block = rows * ncols
    span = flat_ref.shape[1]
    edge = 2 * ncols

    @pl.when(i == 0)
    def _():
        for l in range(span // WIDE):
            columns = slice(l * WIDE, (l + 1) * WIDE)
            for ref, start in ((low_ref, 0), (high_ref, edge + blocks * block)):
                values = ref[:, columns]
                field_ref[pl.ds(start, edge), columns] = values if relax else turned(values, l, span)
        strip_ref[...] = jnp.zeros_like(strip_ref)

    @pl.when(i < blocks)
    def _():
        base = edge + i * block

        def store(start, l, values):
            columns = slice(l * WIDE, (l + 1) * WIDE)
            field_ref[pl.ds(pl.multiple_of(base + start, edge), values.shape[0]), columns] = values

        if relax:
            relax_tiles(block, spread_ref, (target_ref, factor_ref, wall_ref), coef_ref, even_ref,
                        flat_ref, store)
        else:
            for l in range(span // WIDE):
                for start in range(0, block, edge):
                    store(start, l, turned(flat_ref[start:start + edge, l * WIDE:(l + 1) * WIDE], l, span))

    @pl.when(i > 0)
    def _():
        base = (i - 1) * block
        nothing = jnp.minimum(i, 0)

        def lanes(l, carry):
            for h in range(WIDE // LANES):
                columns = pl.ds(pl.multiple_of(l * WIDE, WIDE) + h * LANES, LANES)
                table = stencil_ref[:, columns]
                x0, x1, x2, vx, y0, y1, y2, vy = (table[8 * k:8 * k + 8][None] for k in range(8))
                x_up = jnp.broadcast_to(vx > 0, (ncols // 8, 8, LANES))
                ahead = 1 if h == 0 else -1

                def field(k):
                    start = pl.multiple_of(base + k * ncols, ncols)
                    return field_ref[pl.ds(start, ncols), columns].reshape(ncols // 8, 8, LANES)

                for r in range(rows):
                    near = jnp.where(x_up, field(r + 1), field(r + 3))
                    far = jnp.where(x_up, field(r), field(r + 4))
                    rowwise = x0 * field(r + 2) + x1 * near + x2 * far
                    slot = h * rows + r
                    strip_ref[slot, PAD:PAD + ncols, :] = rowwise.reshape(ncols, LANES)

                    def strip(k):
                        return strip_ref[slot, pl.ds(nothing + PAD + k, ncols), :].reshape(ncols // 8, 8, LANES)

                    value = y0 * rowwise + y1 * strip(ahead) + y2 * strip(2 * ahead)
                    value = value.reshape(ncols, LANES)
                    cut = slice(r * ncols, (r + 1) * ncols)
                    out_ref[cut, columns] = value
                    upper = value.astype(jnp.bfloat16)
                    half_ref[0, cut, columns] = upper
                    if exact:
                        half_ref[1, cut, columns] = (value - upper.astype(jnp.float32)).astype(jnp.bfloat16)
            return carry

        lax.fori_loop(0, span // WIDE, lanes, 0)
        table = dot(half_ref[0], sums_ref[...])
        if exact:
            table = table + dot(half_ref[1], sums_ref[...])
        for g in range(block // LANES):
            total = table[g * LANES:(g + 1) * LANES, :].T
            group = (i - 1) * (block // LANES) + g
            kind = kind_ref[pl.ds(group, 1), :]
            code = code_ref[pl.ds(group, 1), :]
            gas = kind == 0

            def keep(*codes):
                hit = (code == codes[0]) | (code == codes[1])
                return jnp.where(gas | jnp.logical_not(hit), 1.0, 0.0)

            kept = (keep(0, 2) * total[0:16] + keep(0, 3) * total[16:32]
                    + keep(1, 2) * total[32:48] + keep(1, 3) * total[48:64])
            incident = jnp.where(code == 0, total[64:65], jnp.where(code == 1, total[65:66], jnp.where(
                code == 2, total[66:67], total[67:68])))
            parts_ref[pl.ds(pl.multiple_of(group * ROWS, ROWS), ROWS), :] = jnp.concatenate(
                [kept[0:10], kept[10:13] + kept[13:16], incident, jnp.zeros((2, LANES), jnp.float32)], axis=0)


def advance(relax, exact, flat, coef, low, high, kind, code, spread, tables, sums, stencil, ncols):
    cells, span = flat.shape
    rows = 8
    block = rows * ncols
    blocks = cells // block
    groups = cells // LANES
    whole = pl.BlockSpec(memory_space=pltpu.VMEM)
    return pl.pallas_call(
        functools.partial(main_kernel, relax, exact, blocks, rows, ncols),
        grid=(blocks + 1,),
        out_shape=(jax.ShapeDtypeStruct((cells, span), jnp.float32),
                   jax.ShapeDtypeStruct((groups * ROWS, LANES), jnp.float32)),
        in_specs=[pl.BlockSpec((block, span), lambda i: (jnp.minimum(i, blocks - 1), 0)),
                  pl.BlockSpec((block, COEF), lambda i: (jnp.minimum(i, blocks - 1), 0)),
                  whole, whole, whole, whole, whole, whole, whole, whole, whole, whole],
        out_specs=(pl.BlockSpec((block, span), lambda i: (jnp.maximum(i - 1, 0), 0)), whole),
        scratch_shapes=[pltpu.VMEM((cells + 4 * ncols, span), jnp.float32),
                        pltpu.VMEM((CELLS, 2 * LANES), jnp.float32),
                        pltpu.VMEM((WIDE // LANES * rows, ncols + 2 * PAD, LANES), jnp.float32),
                        pltpu.VMEM((1 + exact, block, span), jnp.bfloat16)],
        compiler_params=pltpu.CompilerParams(vmem_limit_bytes=VMEM_LIMIT),
        name="advance" if relax else "transport",
    )(flat, coef, low, high, kind, code, spread, *tables, sums, stencil)


def last_kernel(flat_ref, coef_ref, spread_ref, target_ref, factor_ref, wall_ref, out_ref, even_ref):
    span = flat_ref.shape[1]

    def store(start, l, values):
        out_ref[pl.ds(start, CELLS), l * WIDE:(l + 1) * WIDE] = turned(values, l, span, back=True)

    relax_tiles(flat_ref.shape[0], spread_ref, (target_ref, factor_ref, wall_ref), coef_ref, even_ref,
                flat_ref, store)


def finish(flat, coef, spread, tables, ncols):
    cells, span = flat.shape
    block = 8 * ncols
    whole = pl.BlockSpec(memory_space=pltpu.VMEM)
    return pl.pallas_call(
        last_kernel,
        grid=(cells // block,),
        out_shape=jax.ShapeDtypeStruct((cells, span), jnp.float32),
        in_specs=[pl.BlockSpec((block, span), lambda i: (i, 0)),
                  pl.BlockSpec((block, COEF), lambda i: (i, 0)),
                  whole, whole, whole, whole],
        out_specs=pl.BlockSpec((block, span), lambda i: (i, 0)),
        scratch_shapes=[pltpu.VMEM((CELLS, 2 * LANES), jnp.float32)],
        compiler_params=pltpu.CompilerParams(vmem_limit_bytes=VMEM_LIMIT),
        name="finish",
    )(flat, coef, spread, *tables)


def exchange(first, last):
    size = lax.axis_size("space")
    up = [(i, (i + 1) % size) for i in range(size - 1)]
    down = [(j, i) for i, j in up]
    return lax.ppermute(last, "space", up), lax.ppermute(first, "space", down)


def total(parts):
    count = lax.axis_size("vel")
    rows = parts.shape[0] // count
    pieces = parts.reshape(count, rows, LANES)
    swapped = lax.all_to_all(pieces, "vel", 0, 0)
    own = jnp.sum(swapped, axis=0)
    spread = lax.all_to_all(jnp.broadcast_to(own[None], (count, rows, LANES)), "vel", 0, 0)
    return spread.reshape(count * rows, LANES)


def shards(dist, cell_kind, normal_code, wall_temp):
    nrows, ncols, span = dist.shape
    cells = nrows * ncols
    groups = cells // LANES
    kind = cell_kind.reshape(groups, LANES)
    code = normal_code.reshape(groups, LANES)
    temp = wall_temp.reshape(groups, LANES)
    flat = dist.reshape(cells, span)
    target, factor, wall, sums, stencil, spread = setup(span)
    tables = (target, factor, wall)
    edge = 2 * ncols
    coef = jnp.zeros((cells, COEF), jnp.bfloat16)
    low, high = flat[:edge], flat[cells - edge:]
    for step in range(STEPS):
        final = step == STEPS - 1
        low, high = exchange(low, high)
        flat, parts = advance(step > 0, final, flat, coef, low, high, kind, code, spread, tables, sums, stencil, ncols)
        coef, flux, *ends = state(not final, total(parts), kind, code, temp, flat, spread, tables, ncols)
        if not final:
            low, high = ends
    current = finish(flat, coef, spread, tables, ncols)
    columns = ncols // lax.axis_size("vel")
    own_flux = lax.dynamic_slice_in_dim(flux.reshape(nrows, ncols), lax.axis_index("vel") * columns, columns, 1)
    return current.reshape(nrows, ncols, span), own_flux


def solution(mesh):
    placed = (P("space", None, "vel"), P("space", None), P("space", None), P("space", None))
    return jax.shard_map(
        shards,
        mesh=mesh,
        in_specs=placed,
        out_specs=(P("space", None, "vel"), P("space", "vel")),
        check_vma=False,
    )
```

```python
import functools
import math

import jax
import jax.numpy as jnp
from jax import lax
from jax.experimental import pallas as pl
from jax.experimental.pallas import tpu as pltpu
from jax.sharding import PartitionSpec as P

NQ = 16
STEPS = 4
LIMIT = 5.0
TIME_STEP = 0.05
SIGMA = 0.8
LATENT = 5.0
PRANDTL = 2.0 / 3.0
SHEAR_EXPONENT = 0.1

SPACING = 2.0 * LIMIT / NQ
HALF = 0.5 * SPACING
WEIGHT = SPACING**3 / (2.0 * math.pi) ** 1.5
LOG2E = math.log2(math.e)
LANES = 128
MOMENTS = 16
ROWS = 14
GAS = 10
OFF = 1024.0

T_SQ_HI, T_SQ_LO, T_X, T_Y, T_Z, T_ONE = range(6)
P_ONE, P_X, P_Y, P_Z, P_XX, P_YY, P_ZZ, P_XY, P_XZ, P_YZ = range(6, 16)
P_XS, P_YS, P_ZS, P_XSL, P_YSL, P_ZSL = range(16, 22)
W_SQ_HI, W_SQ_LO, W_ONE, W_XP, W_XN, W_YP, W_YN = range(22, 29)
B_E, B_W = 29, 30
PART = 32
COEF = 2 * PART
STRIDE = COEF + 1

VMEM_LIMIT = 60 * 1024 * 1024


def setup_kernel(span, target_ref, factor_ref, wall_ref, sums_ref, stencil_ref, spread_ref,
                 feature_ref, moment_ref):
    shape = (8, span)
    place = lax.broadcasted_iota(jnp.int32, shape, 1)
    third = lax.axis_index("vel") * (span // WIDE) + place // WIDE
    first = place % NQ
    middle = place // NQ % NQ

    def odd(pick):
        return (2 * (pick % NQ) - (NQ - 1)).astype(jnp.float32)

    x, y, z = odd(first + third), odd(middle), odd(first + middle)
    one = jnp.ones(shape, jnp.float32)
    square = x * x + y * y + z * z
    square_hi = jnp.floor(square * (1.0 / 16.0)) * 16.0
    square_lo = square - square_hi

    def split(v):
        hi = jnp.floor(v * (1.0 / 128.0)) * 128.0
        return hi, v - hi

    xs, xsl = split(x * square)
    ys, ysl = split(y * square)
    zs, zsl = split(z * square)
    xp = jnp.where(x > 0, 1.0, 0.0)
    yp = jnp.where(y > 0, 1.0, 0.0)
    features = [square_hi, square_lo, x, y, z, one,
                one, x, y, z, x * x, y * y, z * z, x * y, x * z, y * z, xs, ys, zs, xsl, ysl, zsl,
                square_hi, square_lo, one, xp, one - xp, yp, one - yp]
    feature_ref[...] = jnp.zeros_like(feature_ref)
    for k, feature in enumerate(features):
        feature_ref[k:k + 1, :] = feature[0:1]
    row = lax.broadcasted_iota(jnp.int32, (PART, span), 0)
    for ref, low, high in ((target_ref, T_SQ_HI, P_ONE), (factor_ref, P_ONE, W_SQ_HI),
                           (wall_ref, W_SQ_HI, B_E)):
        chosen = jnp.where((row >= low) & (row < high), feature_ref[...], 0.0)
        ref[...] = jnp.concatenate([chosen, chosen], axis=0).astype(jnp.bfloat16)
    quadrants = (xp * yp, xp * (one - yp), (one - xp) * yp, (one - xp) * (one - yp))
    moment = feature_ref[P_ONE:W_SQ_HI, :]
    moment_ref[...] = jnp.zeros_like(moment_ref)
    for k, quadrant in enumerate(quadrants):
        moment_ref[MOMENTS * k:MOMENTS * (k + 1), :] = moment * quadrant[0:1]
    for k, speed in enumerate((-x, x, -y, y)):
        moment_ref[4 * MOMENTS + k:4 * MOMENTS + k + 1, :] = jnp.maximum(speed, 0.0)[0:1]
    for l in range(span // LANES):
        cut = slice(l * LANES, (l + 1) * LANES)
        sums_ref[cut, :] = moment_ref[:, cut].T.astype(jnp.bfloat16)
    for k, v in enumerate((x, y)):
        courant = jnp.abs(v) * (HALF * TIME_STEP)
        half_square = 0.5 * courant * courant
        for n, value in enumerate((1.0 - 1.5 * courant + half_square, 2.0 * courant - 2.0 * half_square,
                                   half_square - 0.5 * courant, v)):
            stencil_ref[8 * (4 * k + n):8 * (4 * k + n + 1), :] = value
    row = lax.broadcasted_iota(jnp.int32, (COEF, 2 * LANES), 0)
    column = lax.broadcasted_iota(jnp.int32, (COEF, 2 * LANES), 1)
    want = jnp.where(column < LANES, B_E, B_W)
    hit = row % PART == want
    spread_ref[...] = jnp.where(hit, 1.0, 0.0).astype(jnp.bfloat16)


def setup(span):
    table = jax.ShapeDtypeStruct((COEF, span), jnp.bfloat16)
    return pl.pallas_call(
        functools.partial(setup_kernel, span),
        out_shape=(table, table, table,
                   jax.ShapeDtypeStruct((span, LANES), jnp.bfloat16),
                   jax.ShapeDtypeStruct((64, span), jnp.float32),
                   jax.ShapeDtypeStruct((COEF, 2 * LANES), jnp.bfloat16)),
        out_specs=(pl.BlockSpec(memory_space=pltpu.VMEM),) * 6,
        scratch_shapes=[pltpu.VMEM((PART, span), jnp.float32), pltpu.VMEM((LANES, span), jnp.float32)],
        name="setup",
    )()


def turned(values, l, span, back=False):
    third = lax.axis_index("vel") * (span // WIDE) + l
    shift = NQ * (third % NQ)
    return pltpu.roll(values, (WIDE - shift) % WIDE if back else shift, 1)


def dot(a, b):
    return jnp.dot(a, b, preferred_element_type=jnp.float32)


def gas_kernel(count, size, *refs):
    part_refs = refs[:count]
    kind_ref, code_ref, temp_ref, out_ref = refs[count:]
    mine = pl.ds(pl.multiple_of(lax.axis_index("vel") * size, size), size)

    def read(k, scale):
        value = part_refs[0][pl.ds(k, size, stride=ROWS), :]
        for ref in part_refs[1:]:
            value = value + ref[pl.ds(k, size, stride=ROWS), :]
        return value * (WEIGHT * scale)

    kind = kind_ref[mine, :]
    code = code_ref[mine, :]
    wall = temp_ref[mine, :]
    s0 = s1 = s2 = s3 = jnp.zeros_like(wall)
    inverse = 1.0 / wall
    for j in range(NQ // 2):
        speed = HALF * (2 * j + 1)
        e = jnp.exp(inverse * (-0.5 * speed * speed))
        s0, s1, s2, s3 = s0 + e, s1 + speed * e, s2 + speed**2 * e, s3 + speed**3 * e
    scale = (WEIGHT * 2.0) * inverse * lax.rsqrt(wall)
    norm = 2.0 * scale * s1 * s0 * s0
    f_one = 2.0 * scale * s0 * s0 * s0
    f_nn = 2.0 * scale * s2 * s0 * s0
    f_tt = f_nn
    f_ns = 2.0 * scale * (s3 * s0 * s0 + 2.0 * s1 * s2 * s0)
    saturated = jnp.exp(LATENT * (1.0 - inverse)) * inverse
    incident = read(13, HALF)
    share = jnp.where(kind == 2, SIGMA, 0.0)
    emitted = share * saturated + (1.0 - share) * incident / norm
    boundary = kind > 0
    flux = jnp.where(boundary, emitted * norm - incident, 0.0)
    em = jnp.where(boundary, emitted, 0.0)
    along_x = code < 2
    sign = jnp.where((code == 0) | (code == 2), 1.0, -1.0)
    sx = jnp.where(along_x, sign, 0.0)
    sy = jnp.where(along_x, 0.0, sign)

    rho = read(0, 1.0) + em * f_one
    em_n = em * norm
    em_s = em * f_ns
    mx = read(1, HALF) + sx * em_n
    my = read(2, HALF) + sy * em_n
    mz = read(3, HALF)
    mxx = read(4, HALF**2) + em * f_nn
    myy = read(5, HALF**2) + em * f_tt
    mzz = read(6, HALF**2) + em * f_tt
    mxy = read(7, HALF**2)
    mxz = read(8, HALF**2)
    myz = read(9, HALF**2)
    mxs = read(10, HALF**3) + sx * em_s
    mys = read(11, HALF**3) + sy * em_s
    mzs = read(12, HALF**3)
    msq = mxx + myy + mzz
    per = 1.0 / rho
    ux, uy, uz = mx * per, my * per, mz * per
    uu = ux * ux + uy * uy + uz * uz
    temp = (msq * per - uu) * (1.0 / 3.0)
    dotted = ux * mx + uy * my + uz * mz

    def heat(third, u, m, second):
        return 0.5 * (third - 2.0 * (ux * second[0] + uy * second[1] + uz * second[2]) + uu * m
                      - u * msq + 2.0 * u * dotted - u * uu * rho)

    qx = heat(mxs, ux, mx, (mxx, mxy, mxz))
    qy = heat(mys, uy, my, (mxy, myy, myz))
    qz = heat(mzs, uz, mz, (mxz, myz, mzz))
    for k, value in enumerate((rho, ux, uy, uz, temp, qx, qy, qz, em, flux)):
        out_ref[k * size:(k + 1) * size, :] = value


def gas(parts, kind, code, temp):
    size = parts[0].shape[0] // ROWS
    whole = pl.BlockSpec(memory_space=pltpu.VMEM)
    return pl.pallas_call(
        functools.partial(gas_kernel, len(parts), size),
        out_shape=jax.ShapeDtypeStruct((GAS * size, LANES), jnp.float32),
        in_specs=[whole] * (len(parts) + 3),
        out_specs=whole,
        name="gas",
    )(*parts, kind, code, temp)


def state_kernel(count, groups, with_edges, *refs):
    piece_refs = refs[:count]
    kind_ref, code_ref, temp_ref, *refs = refs[count:]
    if with_edges:
        first_ref, last_ref, spread_ref, target_ref, factor_ref, wall_ref, coef_ref, low_ref, high_ref, *refs = refs
    else:
        coef_ref, flux_ref, *refs = refs
    stack_ref, field_ref = refs
    size = groups // count
    me = lax.axis_index("vel")
    for away, ref in enumerate(piece_refs):
        owner = lax.rem(me + (count - away), count)
        for k in range(GAS):
            field_ref[k, pl.ds(pl.multiple_of(owner * size, size), size), :] = ref[k * size:(k + 1) * size, :]
    kind = kind_ref[...]
    code = code_ref[...]
    wall = temp_ref[...]
    rho, ux, uy, uz, temp, qx, qy, qz, em, flux = (field_ref[k] for k in range(GAS))
    if not with_edges:
        flux_ref[...] = flux
    inverse = 1.0 / wall
    uu = ux * ux + uy * uy + uz * uz
    boundary = kind > 0
    pressure = rho * temp
    per_t = 1.0 / temp
    decay = jnp.exp((-TIME_STEP / SHEAR_EXPONENT) * pressure * jnp.exp(-0.72 * jnp.log(temp)))
    amount = (1.0 - decay) * rho * per_t * lax.rsqrt(temp)
    bend = amount * ((1.0 - PRANDTL) / 5.0) * per_t * per_t / pressure
    kappa = (0.5 * LOG2E) * per_t
    qu = qx * ux + qy * uy + qz * uz
    rest = uu - 5.0 * temp
    twice = -2.0 * bend * HALF**2
    kappa_sq = -kappa * HALF**2
    kappa_u = (2.0 * HALF) * kappa
    wall_sq = (-0.5 * LOG2E * HALF**2) * inverse
    bqu = bend * qu * HALF**2
    solid = jnp.where(boundary, OFF, 0.0)
    rows = {
        T_SQ_HI: kappa_sq, T_SQ_LO: kappa_sq,
        T_X: kappa_u * ux, T_Y: kappa_u * uy, T_Z: kappa_u * uz, T_ONE: -kappa * uu,
        P_ONE: amount - bend * qu * rest,
        P_X: bend * HALF * (qx * rest + 2.0 * qu * ux),
        P_Y: bend * HALF * (qy * rest + 2.0 * qu * uy),
        P_Z: bend * HALF * (qz * rest + 2.0 * qu * uz),
        P_XX: twice * qx * ux - bqu, P_YY: twice * qy * uy - bqu, P_ZZ: twice * qz * uz - bqu,
        P_XY: twice * (qx * uy + qy * ux), P_XZ: twice * (qx * uz + qz * ux),
        P_YZ: twice * (qy * uz + qz * uy),
        P_XS: bend * HALF**3 * qx, P_YS: bend * HALF**3 * qy, P_ZS: bend * HALF**3 * qz,
        W_SQ_HI: wall_sq, W_SQ_LO: wall_sq,
        W_ONE: jnp.where(boundary, 0.0, OFF),
        W_XP: jnp.where(code == 1, solid, 0.0), W_XN: jnp.where(code == 0, solid, 0.0),
        W_YP: jnp.where(code == 3, solid, 0.0), W_YN: jnp.where(code == 2, solid, 0.0),
        B_E: decay, B_W: em * decay * inverse * lax.rsqrt(wall),
    }
    rows[P_XSL], rows[P_YSL], rows[P_ZSL] = rows[P_XS], rows[P_YS], rows[P_ZS]
    zero = jnp.zeros_like(wall)
    for k in range(PART):
        value = rows.get(k)
        for part in range(2):
            if value is None:
                stack_ref[pl.ds(part * PART + k, groups, stride=STRIDE), :] = zero
                continue
            hi = value.astype(jnp.bfloat16).astype(jnp.float32)
            stack_ref[pl.ds(part * PART + k, groups, stride=STRIDE), :] = hi
            value = value - hi

    def turn(g, carry):
        block = stack_ref[pl.ds(g * STRIDE, COEF), :]
        coef_ref[pl.ds(pl.multiple_of(g * LANES, LANES), LANES), :] = block.T.astype(jnp.bfloat16)
        return carry

    lax.fori_loop(0, groups, turn, 0, unroll=8)
    if not with_edges:
        return
    size = low_ref.shape[0]
    for flat_ref, start, out_ref in ((first_ref, 0, low_ref), (last_ref, groups * LANES - size, high_ref)):
        coef = coef_ref[start:start + size, :]
        even = dot(coef, spread_ref[...])
        for l in range(flat_ref.shape[1] // WIDE):
            columns = slice(l * WIDE, (l + 1) * WIDE)
            out_ref[:, columns] = relaxed(coef, even, flat_ref[:, columns], target_ref[:, columns],
                                          factor_ref[:, columns], wall_ref[:, columns])


def state(with_edges, pieces, kind, code, temp, flat, spread, tables, ncols):
    groups = kind.shape[0]
    cells, span = flat.shape
    size = 2 * ncols
    last = cells // size - 1
    whole = pl.BlockSpec(memory_space=pltpu.VMEM)
    operands = [*pieces, kind, code, temp]
    in_specs = [whole] * len(operands)
    out_shape = (jax.ShapeDtypeStruct((cells, COEF), jnp.bfloat16),)
    if with_edges:
        operands += [flat, flat, spread, *tables]
        in_specs += [pl.BlockSpec((size, span), lambda i: (0, 0)),
                     pl.BlockSpec((size, span), lambda i: (last, 0))] + [whole] * 4
        out_shape += (jax.ShapeDtypeStruct((size, span), jnp.float32),) * 2
    else:
        out_shape += (jax.ShapeDtypeStruct((groups, LANES), jnp.float32),)
    return pl.pallas_call(
        functools.partial(state_kernel, len(pieces), groups, with_edges),
        grid=(1,),
        out_shape=out_shape,
        in_specs=in_specs,
        out_specs=(whole,) * len(out_shape),
        scratch_shapes=[pltpu.VMEM((groups * STRIDE + 7, LANES), jnp.float32),
                        pltpu.VMEM((GAS, groups, LANES), jnp.float32)],
        compiler_params=pltpu.CompilerParams(vmem_limit_bytes=VMEM_LIMIT),
        name="state",
    )(*operands)


CELLS = 256
WIDE = 256


def relaxed(coef, even, flat, target, factor, wall):
    exponent = dot(coef, target)
    factor = dot(coef, factor)
    wall = dot(coef, wall)
    decay, amount = even[:, :LANES], even[:, LANES:]
    parts = []
    for h in range(WIDE // LANES):
        cut = slice(h * LANES, (h + 1) * LANES)
        bounded = jnp.where(wall[:, cut] > 0.0, flat[:, cut] * decay, amount * jnp.exp2(wall[:, cut]))
        parts.append(bounded + jnp.exp2(exponent[:, cut]) * factor[:, cut])
    return jnp.concatenate(parts, axis=1)


def relax_tiles(cells, spread_ref, tables, coef_ref, even_ref, flat_ref, store):
    target_ref, factor_ref, wall_ref = tables
    span = flat_ref.shape[1]

    def block(b, carry):
        start = pl.multiple_of(b * CELLS, CELLS)
        coef = coef_ref[pl.ds(start, CELLS), :]
        even_ref[...] = dot(coef, spread_ref[...])
        for l in range(span // WIDE):
            columns = slice(l * WIDE, (l + 1) * WIDE)
            store(start, l, relaxed(coef, even_ref, flat_ref[pl.ds(start, CELLS), columns],
                                    target_ref[:, columns], factor_ref[:, columns], wall_ref[:, columns]))
        return carry

    lax.fori_loop(0, cells // CELLS, block, 0)


PAD = 8
BLOCK = 8


def transport(exact, field_ref, base, ncols, group, kind_ref, code_ref, sums_ref, stencil_ref,
              out_ref, parts_ref, strip_ref, half_ref):
    span = out_ref.shape[1]
    nothing = jnp.minimum(pl.program_id(0), 0)
    table = None
    for l in range(span // WIDE):
        for h in range(WIDE // LANES):
            columns = slice(l * WIDE + h * LANES, l * WIDE + (h + 1) * LANES)
            x0, x1, x2, vx, y0, y1, y2, vy = (stencil_ref[8 * k:8 * k + 8, columns][None] for k in range(8))
            x_up = jnp.broadcast_to(vx > 0, (ncols // 8, 8, LANES))
            ahead = 1 if h == 0 else -1

            def field(k):
                start = pl.multiple_of(base + k * ncols, ncols)
                return field_ref[pl.ds(start, ncols), columns].reshape(ncols // 8, 8, LANES)

            for r in range(BLOCK):
                near = jnp.where(x_up, field(r + 1), field(r + 3))
                far = jnp.where(x_up, field(r), field(r + 4))
                rowwise = x0 * field(r + 2) + x1 * near + x2 * far
                slot = h * BLOCK + r
                strip_ref[slot, PAD:PAD + ncols, :] = rowwise.reshape(ncols, LANES)

                def strip(k):
                    return strip_ref[slot, pl.ds(nothing + PAD + k, ncols), :].reshape(ncols // 8, 8, LANES)

                value = y0 * rowwise + y1 * strip(ahead) + y2 * strip(2 * ahead)
                value = value.reshape(ncols, LANES)
                cut = slice(r * ncols, (r + 1) * ncols)
                out_ref[cut, columns] = value
                upper = value.astype(jnp.bfloat16)
                half_ref[0, cut, columns] = upper
                if exact:
                    half_ref[1, cut, columns] = (value - upper.astype(jnp.float32)).astype(jnp.bfloat16)
        columns = slice(l * WIDE, (l + 1) * WIDE)
        for k in range(1 + exact):
            term = dot(half_ref[k, :, columns], sums_ref[columns, :])
            table = term if table is None else table + term
    for g in range(BLOCK * ncols // LANES):
        total = table[g * LANES:(g + 1) * LANES, :].T
        kind = kind_ref[pl.ds(group + g, 1), :]
        code = code_ref[pl.ds(group + g, 1), :]
        gas = kind == 0

        def keep(*codes):
            hit = (code == codes[0]) | (code == codes[1])
            return jnp.where(gas | jnp.logical_not(hit), 1.0, 0.0)

        kept = (keep(0, 2) * total[0:16] + keep(0, 3) * total[16:32]
                + keep(1, 2) * total[32:48] + keep(1, 3) * total[48:64])
        incident = jnp.where(code == 0, total[64:65], jnp.where(code == 1, total[65:66], jnp.where(
            code == 2, total[66:67], total[67:68])))
        parts_ref[pl.ds((group + g) * ROWS, ROWS), :] = jnp.concatenate(
            [kept[0:10], kept[10:13] + kept[13:16], incident], axis=0)


def inner_kernel(relax, exact, ncols, flat_ref, coef_ref, kind_ref, code_ref,
                 spread_ref, target_ref, factor_ref, wall_ref, sums_ref, stencil_ref,
                 out_ref, parts_ref, head_ref, tail_ref, field_ref, even_ref, strip_ref, half_ref):
    i = pl.program_id(0)
    block = BLOCK * ncols
    span = flat_ref.shape[1]
    edge = 2 * ncols
    base = i * block

    @pl.when(i == 0)
    def _():
        strip_ref[...] = jnp.zeros_like(strip_ref)

    def store(start, l, values):
        columns = slice(l * WIDE, (l + 1) * WIDE)
        field_ref[pl.ds(pl.multiple_of(base + start, edge), values.shape[0]), columns] = values

    if relax:
        relax_tiles(block, spread_ref, (target_ref, factor_ref, wall_ref), coef_ref, even_ref,
                    flat_ref, store)
    else:
        for l in range(span // WIDE):
            for start in range(0, block, edge):
                store(start, l, turned(flat_ref[start:start + edge, l * WIDE:(l + 1) * WIDE], l, span))

    @pl.when(i > 1)
    def _():
        transport(exact, field_ref, base - block - edge, ncols, (i - 1) * (block // LANES), kind_ref, code_ref,
                  sums_ref, stencil_ref, out_ref, parts_ref, strip_ref, half_ref)

    @pl.when(i == pl.num_programs(0) - 1)
    def _():
        size = head_ref.shape[0]
        head_ref[...] = field_ref[:size, :]
        tail_ref[...] = field_ref[field_ref.shape[0] - size:, :]


def outer_kernel(relax, exact, blocks, ncols, count, flat_ref, given_ref, head_ref, tail_ref, low_ref, high_ref,
                 kind_ref, code_ref, sums_ref, stencil_ref, out_ref, *refs):
    slot_refs = refs[:count]
    parts_ref, field_ref, strip_ref, half_ref = refs[count:]
    i = pl.program_id(0)
    block = BLOCK * ncols
    edge = 2 * ncols
    size = head_ref.shape[0]
    span = out_ref.shape[1]

    def halo(ref, start):
        for l in range(span // WIDE):
            columns = slice(l * WIDE, (l + 1) * WIDE)
            values = ref[:, columns]
            field_ref[start:start + edge, columns] = values if relax else turned(values, l, span)

    @pl.when(i == 0)
    def _():
        strip_ref[...] = jnp.zeros_like(strip_ref)
        parts_ref[...] = given_ref[...]
        halo(low_ref, 0)
        field_ref[edge:, :] = head_ref[...]

    @pl.when(i == 1)
    def _():
        field_ref[:size, :] = tail_ref[...]
        halo(high_ref, size)

    transport(exact, field_ref, 0, ncols, i * ((blocks - 1) * (block // LANES)), kind_ref, code_ref,
              sums_ref, stencil_ref, out_ref, parts_ref, strip_ref, half_ref)

    @pl.when(i == 1)
    def _():
        me = lax.axis_index("vel")
        rows = slot_refs[0].shape[0]
        for away, ref in enumerate(slot_refs):
            owner = lax.rem(me + away, count)
            ref[...] = parts_ref[pl.ds(pl.multiple_of(owner * rows, 4), rows), :]


def inner(relax, exact, flat, coef, kind, code, spread, tables, sums, stencil, ncols):
    cells, span = flat.shape
    block = BLOCK * ncols
    blocks = cells // block
    groups = cells // LANES
    whole = pl.BlockSpec(memory_space=pltpu.VMEM)
    end = jax.ShapeDtypeStruct(((BLOCK + 2) * ncols, span), jnp.float32)
    return pl.pallas_call(
        functools.partial(inner_kernel, relax, exact, ncols),
        grid=(blocks,),
        out_shape=(jax.ShapeDtypeStruct((cells, span), jnp.float32),
                   jax.ShapeDtypeStruct((groups * ROWS, LANES), jnp.float32), end, end),
        in_specs=[pl.BlockSpec((block, span), lambda i: (i, 0)),
                  pl.BlockSpec((block, COEF), lambda i: (i, 0))] + [whole] * 8,
        out_specs=(pl.BlockSpec((block, span), lambda i: (jnp.maximum(i - 1, 1), 0)), whole, whole, whole),
        scratch_shapes=[pltpu.VMEM((cells, span), jnp.float32),
                        pltpu.VMEM((CELLS, 2 * LANES), jnp.float32),
                        pltpu.VMEM((WIDE // LANES * BLOCK, ncols + 2 * PAD, LANES), jnp.float32),
                        pltpu.VMEM((1 + exact, block, span), jnp.bfloat16)],
        compiler_params=pltpu.CompilerParams(vmem_limit_bytes=VMEM_LIMIT),
        cost_estimate=pl.CostEstimate(flops=12 * cells * span * COEF, bytes_accessed=8 * cells * span,
                                      transcendentals=2 * cells * span),
        name="inner" if relax else "inner_first",
    )(flat, coef, kind, code, spread, *tables, sums, stencil)


def outer(relax, exact, flat, parts, head, tail, low, high, kind, code, sums, stencil, ncols):
    cells, span = flat.shape
    block = BLOCK * ncols
    blocks = cells // block
    count = lax.axis_size("vel")
    whole = pl.BlockSpec(memory_space=pltpu.VMEM)
    slot = jax.ShapeDtypeStruct((parts.shape[0] // count, LANES), jnp.float32)
    flat, *slots = pl.pallas_call(
        functools.partial(outer_kernel, relax, exact, blocks, ncols, count),
        grid=(2,),
        out_shape=(jax.ShapeDtypeStruct((cells, span), jnp.float32),) + (slot,) * count,
        in_specs=[pl.BlockSpec(memory_space=pl.ANY)] + [whole] * 9,
        out_specs=(pl.BlockSpec((block, span), lambda i: (i * (blocks - 1), 0)),) + (whole,) * count,
        scratch_shapes=[pltpu.VMEM(parts.shape, jnp.float32),
                        pltpu.VMEM(((BLOCK + 4) * ncols, span), jnp.float32),
                        pltpu.VMEM((WIDE // LANES * BLOCK, ncols + 2 * PAD, LANES), jnp.float32),
                        pltpu.VMEM((1 + exact, block, span), jnp.bfloat16)],
        input_output_aliases={0: 0},
        compiler_params=pltpu.CompilerParams(vmem_limit_bytes=VMEM_LIMIT),
        name="outer" if relax else "outer_first",
    )(flat, parts, head, tail, low, high, kind, code, sums, stencil)
    return flat, slots


def last_kernel(flat_ref, coef_ref, spread_ref, target_ref, factor_ref, wall_ref, out_ref, even_ref):
    span = flat_ref.shape[1]

    def store(start, l, values):
        out_ref[pl.ds(start, CELLS), l * WIDE:(l + 1) * WIDE] = turned(values, l, span, back=True)

    relax_tiles(flat_ref.shape[0], spread_ref, (target_ref, factor_ref, wall_ref), coef_ref, even_ref,
                flat_ref, store)


def finish(flat, coef, spread, tables, ncols):
    cells, span = flat.shape
    block = 8 * ncols
    whole = pl.BlockSpec(memory_space=pltpu.VMEM)
    return pl.pallas_call(
        last_kernel,
        grid=(cells // block,),
        out_shape=jax.ShapeDtypeStruct((cells, span), jnp.float32),
        in_specs=[pl.BlockSpec((block, span), lambda i: (i, 0)),
                  pl.BlockSpec((block, COEF), lambda i: (i, 0)),
                  whole, whole, whole, whole],
        out_specs=pl.BlockSpec((block, span), lambda i: (i, 0)),
        scratch_shapes=[pltpu.VMEM((CELLS, 2 * LANES), jnp.float32)],
        compiler_params=pltpu.CompilerParams(vmem_limit_bytes=VMEM_LIMIT),
        name="finish",
    )(flat, coef, spread, *tables)


def exchange(first, last):
    size = lax.axis_size("space")
    up = [(i, (i + 1) % size) for i in range(size - 1)]
    down = [(j, i) for i, j in up]
    return lax.ppermute(last, "space", up), lax.ppermute(first, "space", down)


def swap(slots):
    count = len(slots)
    return [slots[0]] + [lax.ppermute(slots[k], "vel", [(i, (i + k) % count) for i in range(count)])
                         for k in range(1, count)]


def shards(dist, cell_kind, normal_code, wall_temp):
    nrows, ncols, span = dist.shape
    cells = nrows * ncols
    groups = cells // LANES
    kind = cell_kind.reshape(groups, LANES)
    code = normal_code.reshape(groups, LANES)
    temp = wall_temp.reshape(groups, LANES)
    flat = dist.reshape(cells, span)
    target, factor, wall, sums, stencil, spread = setup(span)
    tables = (target, factor, wall)
    edge = 2 * ncols
    coef = jnp.zeros((cells, COEF), jnp.bfloat16)
    low, high = flat[:edge], flat[cells - edge:]
    for step in range(STEPS):
        final = step == STEPS - 1
        low, high = exchange(low, high)
        flat, parts, head, tail = inner(step > 0, final, flat, coef, kind, code, spread, tables, sums, stencil, ncols)
        flat, slots = outer(step > 0, final, flat, parts, head, tail, low, high, kind, code, sums, stencil, ncols)
        own = gas(swap(slots), kind, code, temp)
        coef, *others = state(not final, swap([own] * len(slots)), kind, code, temp, flat, spread, tables, ncols)
        if not final:
            low, high = others
    flux = others[0]
    current = finish(flat, coef, spread, tables, ncols)
    columns = ncols // lax.axis_size("vel")
    own_flux = lax.dynamic_slice_in_dim(flux.reshape(nrows, ncols), lax.axis_index("vel") * columns, columns, 1)
    return current.reshape(nrows, ncols, span), own_flux


def solution(mesh):
    placed = (P("space", None, "vel"), P("space", None), P("space", None), P("space", None))
    return jax.shard_map(
        shards,
        mesh=mesh,
        in_specs=placed,
        out_specs=(P("space", None, "vel"), P("space", "vel")),
        check_vma=False,
    )
```

```python
import functools
import math

import jax
import jax.numpy as jnp
from jax import lax
from jax.experimental import pallas as pl
from jax.experimental.pallas import tpu as pltpu
from jax.sharding import PartitionSpec as P

NQ = 16
STEPS = 4
LIMIT = 5.0
TIME_STEP = 0.05
SIGMA = 0.8
LATENT = 5.0
PRANDTL = 2.0 / 3.0
SHEAR_EXPONENT = 0.1

SPACING = 2.0 * LIMIT / NQ
HALF = 0.5 * SPACING
WEIGHT = SPACING**3 / (2.0 * math.pi) ** 1.5
LOG2E = math.log2(math.e)
LANES = 128
MOMENTS = 16
ROWS = 14
GAS = 10
OFF = 1024.0

T_SQ_HI, T_SQ_LO, T_X, T_Y, T_Z, T_ONE = range(6)
P_ONE, P_X, P_Y, P_Z, P_XX, P_YY, P_ZZ, P_XY, P_XZ, P_YZ = range(6, 16)
P_XS, P_YS, P_ZS, P_XSL, P_YSL, P_ZSL = range(16, 22)
W_SQ_HI, W_SQ_LO, W_ONE, W_XP, W_XN, W_YP, W_YN = range(22, 29)
B_E, B_W = 29, 30
PART = 32
COEF = 2 * PART
STRIDE = COEF + 1

VMEM_LIMIT = 60 * 1024 * 1024


def setup_kernel(span, target_ref, factor_ref, wall_ref, sums_ref, stencil_ref, spread_ref,
                 feature_ref, moment_ref):
    shape = (8, span)
    place = lax.broadcasted_iota(jnp.int32, shape, 1)
    third = lax.axis_index("vel") * (span // WIDE) + place // WIDE
    first = place % NQ
    middle = place // NQ % NQ

    def odd(pick):
        return (2 * (pick % NQ) - (NQ - 1)).astype(jnp.float32)

    x, y, z = odd(first + third), odd(middle), odd(first + middle)
    one = jnp.ones(shape, jnp.float32)
    square = x * x + y * y + z * z
    square_hi = jnp.floor(square * (1.0 / 16.0)) * 16.0
    square_lo = square - square_hi

    def split(v):
        hi = jnp.floor(v * (1.0 / 128.0)) * 128.0
        return hi, v - hi

    xs, xsl = split(x * square)
    ys, ysl = split(y * square)
    zs, zsl = split(z * square)
    xp = jnp.where(x > 0, 1.0, 0.0)
    yp = jnp.where(y > 0, 1.0, 0.0)
    features = [square_hi, square_lo, x, y, z, one,
                one, x, y, z, x * x, y * y, z * z, x * y, x * z, y * z, xs, ys, zs, xsl, ysl, zsl,
                square_hi, square_lo, one, xp, one - xp, yp, one - yp]
    feature_ref[...] = jnp.zeros_like(feature_ref)
    for k, feature in enumerate(features):
        feature_ref[k:k + 1, :] = feature[0:1]
    row = lax.broadcasted_iota(jnp.int32, (PART, span), 0)
    for ref, low, high in ((target_ref, T_SQ_HI, P_ONE), (factor_ref, P_ONE, W_SQ_HI),
                           (wall_ref, W_SQ_HI, B_E)):
        chosen = jnp.where((row >= low) & (row < high), feature_ref[...], 0.0)
        ref[...] = jnp.concatenate([chosen, chosen], axis=0).astype(jnp.bfloat16)
    quadrants = (xp * yp, xp * (one - yp), (one - xp) * yp, (one - xp) * (one - yp))
    moment = feature_ref[P_ONE:W_SQ_HI, :]
    moment_ref[...] = jnp.zeros_like(moment_ref)
    for k, quadrant in enumerate(quadrants):
        moment_ref[MOMENTS * k:MOMENTS * (k + 1), :] = moment * quadrant[0:1]
    for k, speed in enumerate((-x, x, -y, y)):
        moment_ref[4 * MOMENTS + k:4 * MOMENTS + k + 1, :] = jnp.maximum(speed, 0.0)[0:1]
    for l in range(span // LANES):
        cut = slice(l * LANES, (l + 1) * LANES)
        sums_ref[cut, :] = moment_ref[:, cut].T.astype(jnp.bfloat16)
    for k, v in enumerate((x, y)):
        courant = jnp.abs(v) * (HALF * TIME_STEP)
        half_square = 0.5 * courant * courant
        for n, value in enumerate((1.0 - 1.5 * courant + half_square, 2.0 * courant - 2.0 * half_square,
                                   half_square - 0.5 * courant, v)):
            stencil_ref[8 * (4 * k + n):8 * (4 * k + n + 1), :] = value
    row = lax.broadcasted_iota(jnp.int32, (COEF, 2 * LANES), 0)
    column = lax.broadcasted_iota(jnp.int32, (COEF, 2 * LANES), 1)
    want = jnp.where(column < LANES, B_E, B_W)
    hit = row % PART == want
    spread_ref[...] = jnp.where(hit, 1.0, 0.0).astype(jnp.bfloat16)


def setup(span):
    table = jax.ShapeDtypeStruct((COEF, span), jnp.bfloat16)
    return pl.pallas_call(
        functools.partial(setup_kernel, span),
        out_shape=(table, table, table,
                   jax.ShapeDtypeStruct((span, LANES), jnp.bfloat16),
                   jax.ShapeDtypeStruct((64, span), jnp.float32),
                   jax.ShapeDtypeStruct((COEF, 2 * LANES), jnp.bfloat16)),
        out_specs=(pl.BlockSpec(memory_space=pltpu.VMEM),) * 6,
        scratch_shapes=[pltpu.VMEM((PART, span), jnp.float32), pltpu.VMEM((LANES, span), jnp.float32)],
        name="setup",
    )()


def turned(values, l, span, back=False):
    third = lax.axis_index("vel") * (span // WIDE) + l
    shift = NQ * (third % NQ)
    return pltpu.roll(values, (WIDE - shift) % WIDE if back else shift, 1)


def dot(a, b):
    return jnp.dot(a, b, preferred_element_type=jnp.float32)


def gas_kernel(count, size, *refs):
    part_refs = refs[:count]
    kind_ref, code_ref, temp_ref, out_ref = refs[count:]
    mine = pl.ds(pl.multiple_of(lax.axis_index("vel") * size, size), size)

    def read(k, scale):
        value = part_refs[0][pl.ds(k, size, stride=ROWS), :]
        for ref in part_refs[1:]:
            value = value + ref[pl.ds(k, size, stride=ROWS), :]
        return value * (WEIGHT * scale)

    kind = kind_ref[mine, :]
    code = code_ref[mine, :]
    wall = temp_ref[mine, :]
    s0 = s1 = s2 = s3 = jnp.zeros_like(wall)
    inverse = 1.0 / wall
    for j in range(NQ // 2):
        speed = HALF * (2 * j + 1)
        e = jnp.exp(inverse * (-0.5 * speed * speed))
        s0, s1, s2, s3 = s0 + e, s1 + speed * e, s2 + speed**2 * e, s3 + speed**3 * e
    scale = (WEIGHT * 2.0) * inverse * lax.rsqrt(wall)
    norm = 2.0 * scale * s1 * s0 * s0
    f_one = 2.0 * scale * s0 * s0 * s0
    f_nn = 2.0 * scale * s2 * s0 * s0
    f_tt = f_nn
    f_ns = 2.0 * scale * (s3 * s0 * s0 + 2.0 * s1 * s2 * s0)
    saturated = jnp.exp(LATENT * (1.0 - inverse)) * inverse
    incident = read(13, HALF)
    share = jnp.where(kind == 2, SIGMA, 0.0)
    emitted = share * saturated + (1.0 - share) * incident / norm
    boundary = kind > 0
    flux = jnp.where(boundary, emitted * norm - incident, 0.0)
    em = jnp.where(boundary, emitted, 0.0)
    along_x = code < 2
    sign = jnp.where((code == 0) | (code == 2), 1.0, -1.0)
    sx = jnp.where(along_x, sign, 0.0)
    sy = jnp.where(along_x, 0.0, sign)

    rho = read(0, 1.0) + em * f_one
    em_n = em * norm
    em_s = em * f_ns
    mx = read(1, HALF) + sx * em_n
    my = read(2, HALF) + sy * em_n
    mz = read(3, HALF)
    mxx = read(4, HALF**2) + em * f_nn
    myy = read(5, HALF**2) + em * f_tt
    mzz = read(6, HALF**2) + em * f_tt
    mxy = read(7, HALF**2)
    mxz = read(8, HALF**2)
    myz = read(9, HALF**2)
    mxs = read(10, HALF**3) + sx * em_s
    mys = read(11, HALF**3) + sy * em_s
    mzs = read(12, HALF**3)
    msq = mxx + myy + mzz
    per = 1.0 / rho
    ux, uy, uz = mx * per, my * per, mz * per
    uu = ux * ux + uy * uy + uz * uz
    temp = (msq * per - uu) * (1.0 / 3.0)
    dotted = ux * mx + uy * my + uz * mz

    def heat(third, u, m, second):
        return 0.5 * (third - 2.0 * (ux * second[0] + uy * second[1] + uz * second[2]) + uu * m
                      - u * msq + 2.0 * u * dotted - u * uu * rho)

    qx = heat(mxs, ux, mx, (mxx, mxy, mxz))
    qy = heat(mys, uy, my, (mxy, myy, myz))
    qz = heat(mzs, uz, mz, (mxz, myz, mzz))
    for k, value in enumerate((rho, ux, uy, uz, temp, qx, qy, qz, em, flux)):
        out_ref[k * size:(k + 1) * size, :] = value


def gas(parts, kind, code, temp):
    size = parts[0].shape[0] // ROWS
    whole = pl.BlockSpec(memory_space=pltpu.VMEM)
    return pl.pallas_call(
        functools.partial(gas_kernel, len(parts), size),
        out_shape=jax.ShapeDtypeStruct((GAS * size, LANES), jnp.float32),
        in_specs=[whole] * (len(parts) + 3),
        out_specs=whole,
        name="gas",
    )(*parts, kind, code, temp)


def state_kernel(count, groups, with_edges, *refs):
    piece_refs = refs[:count]
    kind_ref, code_ref, temp_ref, *refs = refs[count:]
    if with_edges:
        first_ref, last_ref, spread_ref, target_ref, factor_ref, wall_ref, coef_ref, low_ref, high_ref, *refs = refs
    else:
        coef_ref, flux_ref, *refs = refs
    stack_ref, field_ref = refs
    size = groups // count
    me = lax.axis_index("vel")
    for away, ref in enumerate(piece_refs):
        owner = lax.rem(me + (count - away), count)
        for k in range(GAS):
            field_ref[k, pl.ds(pl.multiple_of(owner * size, size), size), :] = ref[k * size:(k + 1) * size, :]
    kind = kind_ref[...]
    code = code_ref[...]
    wall = temp_ref[...]
    rho, ux, uy, uz, temp, qx, qy, qz, em, flux = (field_ref[k] for k in range(GAS))
    if not with_edges:
        flux_ref[...] = flux
    inverse = 1.0 / wall
    uu = ux * ux + uy * uy + uz * uz
    boundary = kind > 0
    pressure = rho * temp
    per_t = 1.0 / temp
    decay = jnp.exp((-TIME_STEP / SHEAR_EXPONENT) * pressure * jnp.exp(-0.72 * jnp.log(temp)))
    amount = (1.0 - decay) * rho * per_t * lax.rsqrt(temp)
    bend = amount * ((1.0 - PRANDTL) / 5.0) * per_t * per_t / pressure
    kappa = (0.5 * LOG2E) * per_t
    qu = qx * ux + qy * uy + qz * uz
    rest = uu - 5.0 * temp
    twice = -2.0 * bend * HALF**2
    kappa_sq = -kappa * HALF**2
    kappa_u = (2.0 * HALF) * kappa
    wall_sq = (-0.5 * LOG2E * HALF**2) * inverse
    bqu = bend * qu * HALF**2
    solid = jnp.where(boundary, OFF, 0.0)
    rows = {
        T_SQ_HI: kappa_sq, T_SQ_LO: kappa_sq,
        T_X: kappa_u * ux, T_Y: kappa_u * uy, T_Z: kappa_u * uz, T_ONE: -kappa * uu,
        P_ONE: amount - bend * qu * rest,
        P_X: bend * HALF * (qx * rest + 2.0 * qu * ux),
        P_Y: bend * HALF * (qy * rest + 2.0 * qu * uy),
        P_Z: bend * HALF * (qz * rest + 2.0 * qu * uz),
        P_XX: twice * qx * ux - bqu, P_YY: twice * qy * uy - bqu, P_ZZ: twice * qz * uz - bqu,
        P_XY: twice * (qx * uy + qy * ux), P_XZ: twice * (qx * uz + qz * ux),
        P_YZ: twice * (qy * uz + qz * uy),
        P_XS: bend * HALF**3 * qx, P_YS: bend * HALF**3 * qy, P_ZS: bend * HALF**3 * qz,
        W_SQ_HI: wall_sq, W_SQ_LO: wall_sq,
        W_ONE: jnp.where(boundary, 0.0, OFF),
        W_XP: jnp.where(code == 1, solid, 0.0), W_XN: jnp.where(code == 0, solid, 0.0),
        W_YP: jnp.where(code == 3, solid, 0.0), W_YN: jnp.where(code == 2, solid, 0.0),
        B_E: decay, B_W: em * decay * inverse * lax.rsqrt(wall),
    }
    rows[P_XSL], rows[P_YSL], rows[P_ZSL] = rows[P_XS], rows[P_YS], rows[P_ZS]
    zero = jnp.zeros_like(wall)
    for k in range(PART):
        value = rows.get(k)
        for part in range(2):
            if value is None:
                stack_ref[pl.ds(part * PART + k, groups, stride=STRIDE), :] = zero
                continue
            hi = value.astype(jnp.bfloat16).astype(jnp.float32)
            stack_ref[pl.ds(part * PART + k, groups, stride=STRIDE), :] = hi
            value = value - hi

    def turn(g, carry):
        block = stack_ref[pl.ds(g * STRIDE, COEF), :]
        coef_ref[pl.ds(pl.multiple_of(g * LANES, LANES), LANES), :] = block.T.astype(jnp.bfloat16)
        return carry

    lax.fori_loop(0, groups, turn, 0, unroll=8)
    if not with_edges:
        return
    size = low_ref.shape[0]
    for flat_ref, start, out_ref in ((first_ref, 0, low_ref), (last_ref, groups * LANES - size, high_ref)):
        coef = coef_ref[start:start + size, :]
        even = dot(coef, spread_ref[...])
        for l in range(flat_ref.shape[1] // WIDE):
            columns = slice(l * WIDE, (l + 1) * WIDE)
            out_ref[:, columns] = relaxed(coef, even, flat_ref[:, columns], target_ref[:, columns],
                                          factor_ref[:, columns], wall_ref[:, columns])


def state(with_edges, pieces, kind, code, temp, flat, spread, tables, ncols):
    groups = kind.shape[0]
    cells, span = flat.shape
    size = 2 * ncols
    last = cells // size - 1
    whole = pl.BlockSpec(memory_space=pltpu.VMEM)
    operands = [*pieces, kind, code, temp]
    in_specs = [whole] * len(operands)
    out_shape = (jax.ShapeDtypeStruct((cells, COEF), jnp.bfloat16),)
    if with_edges:
        operands += [flat, flat, spread, *tables]
        in_specs += [pl.BlockSpec((size, span), lambda i: (0, 0)),
                     pl.BlockSpec((size, span), lambda i: (last, 0))] + [whole] * 4
        out_shape += (jax.ShapeDtypeStruct((size, span), jnp.float32),) * 2
    else:
        out_shape += (jax.ShapeDtypeStruct((groups, LANES), jnp.float32),)
    return pl.pallas_call(
        functools.partial(state_kernel, len(pieces), groups, with_edges),
        grid=(1,),
        out_shape=out_shape,
        in_specs=in_specs,
        out_specs=(whole,) * len(out_shape),
        scratch_shapes=[pltpu.VMEM((groups * STRIDE + 7, LANES), jnp.float32),
                        pltpu.VMEM((GAS, groups, LANES), jnp.float32)],
        compiler_params=pltpu.CompilerParams(vmem_limit_bytes=VMEM_LIMIT),
        name="state",
    )(*operands)


CELLS = 512
WIDE = 256


def relaxed(coef, even, flat, target, factor, wall):
    exponent = dot(coef, target)
    factor = dot(coef, factor)
    wall = dot(coef, wall)
    decay, amount = even[:, :LANES], even[:, LANES:]
    parts = []
    for h in range(WIDE // LANES):
        cut = slice(h * LANES, (h + 1) * LANES)
        bounded = jnp.where(wall[:, cut] > 0.0, flat[:, cut] * decay, amount * jnp.exp2(wall[:, cut]))
        parts.append(bounded + jnp.exp2(exponent[:, cut]) * factor[:, cut])
    return jnp.concatenate(parts, axis=1)


def relax_tiles(cells, spread_ref, tables, coef_ref, even_ref, flat_ref, store):
    target_ref, factor_ref, wall_ref = tables
    span = flat_ref.shape[1]

    def block(b, carry):
        start = pl.multiple_of(b * CELLS, CELLS)
        coef = coef_ref[pl.ds(start, CELLS), :]
        even_ref[...] = dot(coef, spread_ref[...])
        for l in range(span // WIDE):
            columns = slice(l * WIDE, (l + 1) * WIDE)
            store(start, l, relaxed(coef, even_ref, flat_ref[pl.ds(start, CELLS), columns],
                                    target_ref[:, columns], factor_ref[:, columns], wall_ref[:, columns]))
        return carry

    lax.fori_loop(0, cells // CELLS, block, 0)


PAD = 8
BLOCK = 8


def transport(exact, rows, field_ref, base, ncols, group, kind_ref, code_ref, sums_ref, stencil_ref,
              out_ref, parts_ref, strip_ref, half_ref):
    span = out_ref.shape[1]
    nothing = jnp.minimum(pl.program_id(0), 0)
    shape = (ncols // 8, 8, LANES)
    table = None
    for l in range(span // WIDE):
        for h in range(WIDE // LANES):
            columns = slice(l * WIDE + h * LANES, l * WIDE + (h + 1) * LANES)
            x0, x1, x2, vx, y0, y1, y2, _ = (stencil_ref[8 * k:8 * k + 8, columns][None] for k in range(8))
            x_up = jnp.broadcast_to(vx > 0, shape)
            ahead = 1 if h == 0 else -1

            def field(k):
                start = pl.multiple_of(base + k * ncols, ncols)
                return field_ref[pl.ds(start, ncols), columns].reshape(shape)

            window = [field(k) for k in range(4)]
            for r in range(rows):
                window.append(field(r + 4))
                near = jnp.where(x_up, window[1], window[3])
                far = jnp.where(x_up, window[0], window[4])
                rowwise = x0 * window[2] + x1 * near + x2 * far
                window = window[1:]
                slot = h * BLOCK + r
                strip_ref[slot, PAD:PAD + ncols, :] = rowwise.reshape(ncols, LANES)

                def strip(k):
                    return strip_ref[slot, pl.ds(nothing + PAD + k, ncols), :].reshape(shape)

                value = y0 * rowwise + y1 * strip(ahead) + y2 * strip(2 * ahead)
                value = value.reshape(ncols, LANES)
                cut = slice(r * ncols, (r + 1) * ncols)
                out_ref[cut, columns] = value
                upper = value.astype(jnp.bfloat16)
                half_ref[0, cut, columns] = upper
                if exact:
                    half_ref[1, cut, columns] = (value - upper.astype(jnp.float32)).astype(jnp.bfloat16)
        columns = slice(l * WIDE, (l + 1) * WIDE)
        for k in range(1 + exact):
            term = dot(half_ref[k, :, columns], sums_ref[columns, :])
            table = term if table is None else table + term
    for g in range(rows * ncols // LANES):
        total = table[g * LANES:(g + 1) * LANES, :].T
        kind = kind_ref[pl.ds(group + g, 1), :]
        code = code_ref[pl.ds(group + g, 1), :]
        gas = kind == 0

        def keep(*codes):
            hit = (code == codes[0]) | (code == codes[1])
            return jnp.where(gas | jnp.logical_not(hit), 1.0, 0.0)

        kept = (keep(0, 2) * total[0:16] + keep(0, 3) * total[16:32]
                + keep(1, 2) * total[32:48] + keep(1, 3) * total[48:64])
        incident = jnp.where(code == 0, total[64:65], jnp.where(code == 1, total[65:66], jnp.where(
            code == 2, total[66:67], total[67:68])))
        parts_ref[pl.ds((group + g) * ROWS, ROWS), :] = jnp.concatenate(
            [kept[0:10], kept[10:13] + kept[13:16], incident], axis=0)


END = 2


def inner_kernel(relax, exact, blocks, ncols, flat_ref, kind_ref, code_ref, sums_ref, stencil_ref, *refs):
    if relax:
        coef_ref, spread_ref, target_ref, factor_ref, wall_ref, *refs = refs
    out_ref, parts_ref, head_ref, tail_ref, field_ref, even_ref, strip_ref, half_ref = refs
    i = pl.program_id(0)
    block = BLOCK * ncols
    span = flat_ref.shape[1]
    edge = END * ncols

    @pl.when(i == 0)
    def _():
        strip_ref[...] = jnp.zeros_like(strip_ref)
        blank = jnp.zeros((edge, span), jnp.float32)
        field_ref[:edge, :] = blank
        field_ref[field_ref.shape[0] - edge:, :] = blank

    @pl.when(i < blocks)
    def _():
        base = edge + i * block

        def store(start, l, values):
            columns = slice(l * WIDE, (l + 1) * WIDE)
            field_ref[pl.ds(pl.multiple_of(base + start, edge), values.shape[0]), columns] = values

        if relax:
            relax_tiles(block, spread_ref, (target_ref, factor_ref, wall_ref), coef_ref, even_ref,
                        flat_ref, store)
        else:
            for l in range(span // WIDE):
                for start in range(0, block, edge):
                    store(start, l, turned(flat_ref[start:start + edge, l * WIDE:(l + 1) * WIDE], l, span))

    @pl.when(i > 0)
    def _():
        transport(exact, BLOCK, field_ref, (i - 1) * block, ncols, (i - 1) * (block // LANES), kind_ref, code_ref,
                  sums_ref, stencil_ref, out_ref, parts_ref, strip_ref, half_ref)

    @pl.when(i == blocks)
    def _():
        size = head_ref.shape[0]
        last = field_ref.shape[0] - edge
        head_ref[...] = field_ref[edge:edge + size, :]
        tail_ref[...] = field_ref[last - size:last, :]


def outer_kernel(relax, exact, ncols, count, flat_ref, given_ref, head_ref, tail_ref, low_ref, high_ref,
                 kind_ref, code_ref, sums_ref, stencil_ref, out_ref, *refs):
    slot_refs = refs[:count]
    parts_ref, field_ref, strip_ref, half_ref = refs[count:]
    i = pl.program_id(0)
    edge = END * ncols
    size = head_ref.shape[0]
    span = out_ref.shape[1]
    groups = parts_ref.shape[0] // ROWS

    def halo(ref, start):
        for l in range(span // WIDE):
            columns = slice(l * WIDE, (l + 1) * WIDE)
            values = ref[:, columns]
            field_ref[start:start + edge, columns] = values if relax else turned(values, l, span)

    @pl.when(i == 0)
    def _():
        strip_ref[...] = jnp.zeros_like(strip_ref)
        parts_ref[...] = given_ref[...]
        halo(low_ref, 0)
        field_ref[edge:, :] = head_ref[...]

    @pl.when(i == 1)
    def _():
        field_ref[:size, :] = tail_ref[...]
        halo(high_ref, size)

    transport(exact, END, field_ref, 0, ncols, i * (groups - edge // LANES), kind_ref, code_ref,
              sums_ref, stencil_ref, out_ref, parts_ref, strip_ref, half_ref)

    @pl.when(i == 1)
    def _():
        me = lax.axis_index("vel")
        rows = slot_refs[0].shape[0]
        for away, ref in enumerate(slot_refs):
            owner = lax.rem(me + away, count)
            ref[...] = parts_ref[pl.ds(pl.multiple_of(owner * rows, 4), rows), :]


def inner(relax, exact, flat, coef, kind, code, spread, tables, sums, stencil, ncols):
    cells, span = flat.shape
    block = BLOCK * ncols
    blocks = cells // block
    groups = cells // LANES
    whole = pl.BlockSpec(memory_space=pltpu.VMEM)
    end = jax.ShapeDtypeStruct((2 * END * ncols, span), jnp.float32)
    operands = [flat, kind, code, sums, stencil]
    in_specs = [pl.BlockSpec((block, span), lambda i: (jnp.minimum(i, blocks - 1), 0))] + [whole] * 4
    if relax:
        operands += [coef, spread, *tables]
        in_specs += [pl.BlockSpec((block, COEF), lambda i: (jnp.minimum(i, blocks - 1), 0))] + [whole] * 4
    return pl.pallas_call(
        functools.partial(inner_kernel, relax, exact, blocks, ncols),
        grid=(blocks + 1,),
        out_shape=(jax.ShapeDtypeStruct((cells, span), jnp.float32),
                   jax.ShapeDtypeStruct((groups * ROWS, LANES), jnp.float32), end, end),
        in_specs=in_specs,
        out_specs=(pl.BlockSpec((block, span), lambda i: (jnp.maximum(i - 1, 0), 0)), whole, whole, whole),
        scratch_shapes=[pltpu.VMEM((cells + 2 * END * ncols, span), jnp.float32),
                        pltpu.VMEM((CELLS, 2 * LANES), jnp.float32),
                        pltpu.VMEM((WIDE // LANES * BLOCK, ncols + 2 * PAD, LANES), jnp.float32),
                        pltpu.VMEM((1 + exact, block, span), jnp.bfloat16)],
        compiler_params=pltpu.CompilerParams(vmem_limit_bytes=VMEM_LIMIT),
        cost_estimate=pl.CostEstimate(flops=12 * cells * span * COEF, bytes_accessed=8 * cells * span,
                                      transcendentals=2 * cells * span),
        name="inner" if relax else "inner_first",
    )(*operands)


def outer(relax, exact, flat, parts, head, tail, low, high, kind, code, sums, stencil, ncols):
    cells, span = flat.shape
    edge = END * ncols
    last = cells // edge - 1
    count = lax.axis_size("vel")
    whole = pl.BlockSpec(memory_space=pltpu.VMEM)
    slot = jax.ShapeDtypeStruct((parts.shape[0] // count, LANES), jnp.float32)
    flat, *slots = pl.pallas_call(
        functools.partial(outer_kernel, relax, exact, ncols, count),
        grid=(2,),
        out_shape=(jax.ShapeDtypeStruct((cells, span), jnp.float32),) + (slot,) * count,
        in_specs=[pl.BlockSpec(memory_space=pl.ANY)] + [whole] * 9,
        out_specs=(pl.BlockSpec((edge, span), lambda i: (i * last, 0)),) + (whole,) * count,
        scratch_shapes=[pltpu.VMEM(parts.shape, jnp.float32),
                        pltpu.VMEM((3 * edge, span), jnp.float32),
                        pltpu.VMEM((WIDE // LANES * BLOCK, ncols + 2 * PAD, LANES), jnp.float32),
                        pltpu.VMEM((1 + exact, edge, span), jnp.bfloat16)],
        input_output_aliases={0: 0},
        compiler_params=pltpu.CompilerParams(vmem_limit_bytes=VMEM_LIMIT),
        name="outer" if relax else "outer_first",
    )(flat, parts, head, tail, low, high, kind, code, sums, stencil)
    return flat, slots


def last_kernel(flat_ref, coef_ref, spread_ref, target_ref, factor_ref, wall_ref, out_ref, even_ref):
    span = flat_ref.shape[1]

    def store(start, l, values):
        out_ref[pl.ds(start, CELLS), l * WIDE:(l + 1) * WIDE] = turned(values, l, span, back=True)

    relax_tiles(flat_ref.shape[0], spread_ref, (target_ref, factor_ref, wall_ref), coef_ref, even_ref,
                flat_ref, store)


def finish(flat, coef, spread, tables, ncols):
    cells, span = flat.shape
    block = 8 * ncols
    whole = pl.BlockSpec(memory_space=pltpu.VMEM)
    return pl.pallas_call(
        last_kernel,
        grid=(cells // block,),
        out_shape=jax.ShapeDtypeStruct((cells, span), jnp.float32),
        in_specs=[pl.BlockSpec((block, span), lambda i: (i, 0)),
                  pl.BlockSpec((block, COEF), lambda i: (i, 0)),
                  whole, whole, whole, whole],
        out_specs=pl.BlockSpec((block, span), lambda i: (i, 0)),
        scratch_shapes=[pltpu.VMEM((CELLS, 2 * LANES), jnp.float32)],
        compiler_params=pltpu.CompilerParams(vmem_limit_bytes=VMEM_LIMIT),
        name="finish",
    )(flat, coef, spread, *tables)


def exchange(first, last):
    size = lax.axis_size("space")
    up = [(i, (i + 1) % size) for i in range(size - 1)]
    down = [(j, i) for i, j in up]
    return lax.ppermute(last, "space", up), lax.ppermute(first, "space", down)


def swap(slots):
    count = len(slots)
    return [slots[0]] + [lax.ppermute(slots[k], "vel", [(i, (i + k) % count) for i in range(count)])
                         for k in range(1, count)]


def shards(dist, cell_kind, normal_code, wall_temp):
    nrows, ncols, span = dist.shape
    cells = nrows * ncols
    groups = cells // LANES
    kind = cell_kind.reshape(groups, LANES)
    code = normal_code.reshape(groups, LANES)
    temp = wall_temp.reshape(groups, LANES)
    flat = dist.reshape(cells, span)
    target, factor, wall, sums, stencil, spread = setup(span)
    tables = (target, factor, wall)
    edge = 2 * ncols
    coef = None
    low, high = flat[:edge], flat[cells - edge:]
    for step in range(STEPS):
        final = step == STEPS - 1
        low, high = exchange(low, high)
        flat, parts, head, tail = inner(step > 0, final, flat, coef, kind, code, spread, tables, sums, stencil, ncols)
        flat, slots = outer(step > 0, final, flat, parts, head, tail, low, high, kind, code, sums, stencil, ncols)
        own = gas(swap(slots), kind, code, temp)
        coef, *others = state(not final, swap([own] * len(slots)), kind, code, temp, flat, spread, tables, ncols)
        if not final:
            low, high = others
    flux = others[0]
    current = finish(flat, coef, spread, tables, ncols)
    columns = ncols // lax.axis_size("vel")
    own_flux = lax.dynamic_slice_in_dim(flux.reshape(nrows, ncols), lax.axis_index("vel") * columns, columns, 1)
    return current.reshape(nrows, ncols, span), own_flux


def solution(mesh):
    placed = (P("space", None, "vel"), P("space", None), P("space", None), P("space", None))
    return jax.shard_map(
        shards,
        mesh=mesh,
        in_specs=placed,
        out_specs=(P("space", None, "vel"), P("space", "vel")),
        check_vma=False,
    )
```

```python
import functools
import math

import jax
import jax.numpy as jnp
from jax import lax
from jax.experimental import pallas as pl
from jax.experimental.pallas import tpu as pltpu
from jax.sharding import PartitionSpec as P

NQ = 16
STEPS = 4
LIMIT = 5.0
TIME_STEP = 0.05
SIGMA = 0.8
LATENT = 5.0
PRANDTL = 2.0 / 3.0
SHEAR_EXPONENT = 0.1

SPACING = 2.0 * LIMIT / NQ
HALF = 0.5 * SPACING
WEIGHT = SPACING**3 / (2.0 * math.pi) ** 1.5
LOG2E = math.log2(math.e)
LANES = 128
MOMENTS = 16
ROWS = 14
GAS = 10
OFF = 1024.0

T_SQ_HI, T_SQ_LO, T_X, T_Y, T_Z, T_ONE = range(6)
P_ONE, P_X, P_Y, P_Z, P_XX, P_YY, P_ZZ, P_XY, P_XZ, P_YZ = range(6, 16)
P_XS, P_YS, P_ZS, P_XSL, P_YSL, P_ZSL = range(16, 22)
W_SQ_HI, W_SQ_LO, W_ONE, W_XP, W_XN, W_YP, W_YN = range(22, 29)
B_E, B_W = 29, 30
PART = 32
COEF = 2 * PART
STRIDE = COEF + 1

VMEM_LIMIT = 60 * 1024 * 1024


def setup_kernel(span, target_ref, factor_ref, wall_ref, sums_ref, stencil_ref, spread_ref,
                 feature_ref, moment_ref):
    shape = (8, span)
    place = lax.broadcasted_iota(jnp.int32, shape, 1)
    third = lax.axis_index("vel") * (span // WIDE) + place // WIDE
    first = place % NQ
    middle = place // NQ % NQ

    def odd(pick):
        return (2 * (pick % NQ) - (NQ - 1)).astype(jnp.float32)

    x, y, z = odd(first + third), odd(middle), odd(first + middle)
    one = jnp.ones(shape, jnp.float32)
    square = x * x + y * y + z * z
    square_hi = jnp.floor(square * (1.0 / 16.0)) * 16.0
    square_lo = square - square_hi

    def split(v):
        hi = jnp.floor(v * (1.0 / 128.0)) * 128.0
        return hi, v - hi

    xs, xsl = split(x * square)
    ys, ysl = split(y * square)
    zs, zsl = split(z * square)
    xp = jnp.where(x > 0, 1.0, 0.0)
    yp = jnp.where(y > 0, 1.0, 0.0)
    features = [square_hi, square_lo, x, y, z, one,
                one, x, y, z, x * x, y * y, z * z, x * y, x * z, y * z, xs, ys, zs, xsl, ysl, zsl,
                square_hi, square_lo, one, xp, one - xp, yp, one - yp]
    feature_ref[...] = jnp.zeros_like(feature_ref)
    for k, feature in enumerate(features):
        feature_ref[k:k + 1, :] = feature[0:1]
    row = lax.broadcasted_iota(jnp.int32, (PART, span), 0)
    for ref, low, high in ((target_ref, T_SQ_HI, P_ONE), (factor_ref, P_ONE, W_SQ_HI),
                           (wall_ref, W_SQ_HI, B_E)):
        chosen = jnp.where((row >= low) & (row < high), feature_ref[...], 0.0)
        ref[...] = jnp.concatenate([chosen, chosen], axis=0).astype(jnp.bfloat16)
    quadrants = (xp * yp, xp * (one - yp), (one - xp) * yp, (one - xp) * (one - yp))
    moment = feature_ref[P_ONE:W_SQ_HI, :]
    moment_ref[...] = jnp.zeros_like(moment_ref)
    for k, quadrant in enumerate(quadrants):
        moment_ref[MOMENTS * k:MOMENTS * (k + 1), :] = moment * quadrant[0:1]
    for k, speed in enumerate((-x, x, -y, y)):
        moment_ref[4 * MOMENTS + k:4 * MOMENTS + k + 1, :] = jnp.maximum(speed, 0.0)[0:1]
    for l in range(span // LANES):
        cut = slice(l * LANES, (l + 1) * LANES)
        sums_ref[cut, :] = moment_ref[:, cut].T.astype(jnp.bfloat16)
    for k, v in enumerate((x, y)):
        courant = jnp.abs(v) * (HALF * TIME_STEP)
        half_square = 0.5 * courant * courant
        for n, value in enumerate((1.0 - 1.5 * courant + half_square, 2.0 * courant - 2.0 * half_square,
                                   half_square - 0.5 * courant, v)):
            stencil_ref[8 * (4 * k + n):8 * (4 * k + n + 1), :] = value
    row = lax.broadcasted_iota(jnp.int32, (COEF, 2 * LANES), 0)
    column = lax.broadcasted_iota(jnp.int32, (COEF, 2 * LANES), 1)
    want = jnp.where(column < LANES, B_E, B_W)
    hit = row % PART == want
    spread_ref[...] = jnp.where(hit, 1.0, 0.0).astype(jnp.bfloat16)


def setup(span):
    table = jax.ShapeDtypeStruct((COEF, span), jnp.bfloat16)
    return pl.pallas_call(
        functools.partial(setup_kernel, span),
        out_shape=(table, table, table,
                   jax.ShapeDtypeStruct((span, LANES), jnp.bfloat16),
                   jax.ShapeDtypeStruct((64, span), jnp.float32),
                   jax.ShapeDtypeStruct((COEF, 2 * LANES), jnp.bfloat16)),
        out_specs=(pl.BlockSpec(memory_space=pltpu.VMEM),) * 6,
        scratch_shapes=[pltpu.VMEM((PART, span), jnp.float32), pltpu.VMEM((LANES, span), jnp.float32)],
        name="setup",
    )()


def turned(values, l, span, back=False):
    third = lax.axis_index("vel") * (span // WIDE) + l
    shift = NQ * (third % NQ)
    return pltpu.roll(values, (WIDE - shift) % WIDE if back else shift, 1)


def dot(a, b):
    return jnp.dot(a, b, preferred_element_type=jnp.float32)


def gas_kernel(count, size, *refs):
    part_refs = refs[:count]
    kind_ref, code_ref, temp_ref, out_ref = refs[count:]
    mine = pl.ds(pl.multiple_of(lax.axis_index("vel") * size, size), size)

    def read(k, scale):
        value = part_refs[0][pl.ds(k, size, stride=ROWS), :]
        for ref in part_refs[1:]:
            value = value + ref[pl.ds(k, size, stride=ROWS), :]
        return value * (WEIGHT * scale)

    kind = kind_ref[mine, :]
    code = code_ref[mine, :]
    wall = temp_ref[mine, :]
    s0 = s1 = s2 = s3 = jnp.zeros_like(wall)
    inverse = 1.0 / wall
    for j in range(NQ // 2):
        speed = HALF * (2 * j + 1)
        e = jnp.exp(inverse * (-0.5 * speed * speed))
        s0, s1, s2, s3 = s0 + e, s1 + speed * e, s2 + speed**2 * e, s3 + speed**3 * e
    scale = (WEIGHT * 2.0) * inverse * lax.rsqrt(wall)
    norm = 2.0 * scale * s1 * s0 * s0
    f_one = 2.0 * scale * s0 * s0 * s0
    f_nn = 2.0 * scale * s2 * s0 * s0
    f_tt = f_nn
    f_ns = 2.0 * scale * (s3 * s0 * s0 + 2.0 * s1 * s2 * s0)
    saturated = jnp.exp(LATENT * (1.0 - inverse)) * inverse
    incident = read(13, HALF)
    share = jnp.where(kind == 2, SIGMA, 0.0)
    emitted = share * saturated + (1.0 - share) * incident / norm
    boundary = kind > 0
    flux = jnp.where(boundary, emitted * norm - incident, 0.0)
    em = jnp.where(boundary, emitted, 0.0)
    along_x = code < 2
    sign = jnp.where((code == 0) | (code == 2), 1.0, -1.0)
    sx = jnp.where(along_x, sign, 0.0)
    sy = jnp.where(along_x, 0.0, sign)

    rho = read(0, 1.0) + em * f_one
    em_n = em * norm
    em_s = em * f_ns
    mx = read(1, HALF) + sx * em_n
    my = read(2, HALF) + sy * em_n
    mz = read(3, HALF)
    mxx = read(4, HALF**2) + em * f_nn
    myy = read(5, HALF**2) + em * f_tt
    mzz = read(6, HALF**2) + em * f_tt
    mxy = read(7, HALF**2)
    mxz = read(8, HALF**2)
    myz = read(9, HALF**2)
    mxs = read(10, HALF**3) + sx * em_s
    mys = read(11, HALF**3) + sy * em_s
    mzs = read(12, HALF**3)
    msq = mxx + myy + mzz
    per = 1.0 / rho
    ux, uy, uz = mx * per, my * per, mz * per
    uu = ux * ux + uy * uy + uz * uz
    temp = (msq * per - uu) * (1.0 / 3.0)
    dotted = ux * mx + uy * my + uz * mz

    def heat(third, u, m, second):
        return 0.5 * (third - 2.0 * (ux * second[0] + uy * second[1] + uz * second[2]) + uu * m
                      - u * msq + 2.0 * u * dotted - u * uu * rho)

    qx = heat(mxs, ux, mx, (mxx, mxy, mxz))
    qy = heat(mys, uy, my, (mxy, myy, myz))
    qz = heat(mzs, uz, mz, (mxz, myz, mzz))
    for k, value in enumerate((rho, ux, uy, uz, temp, qx, qy, qz, em, flux)):
        out_ref[k * size:(k + 1) * size, :] = value


def gas(parts, kind, code, temp):
    size = parts[0].shape[0] // ROWS
    whole = pl.BlockSpec(memory_space=pltpu.VMEM)
    return pl.pallas_call(
        functools.partial(gas_kernel, len(parts), size),
        out_shape=jax.ShapeDtypeStruct((GAS * size, LANES), jnp.float32),
        in_specs=[whole] * (len(parts) + 3),
        out_specs=whole,
        name="gas",
    )(*parts, kind, code, temp)


def state_kernel(count, groups, with_edges, *refs):
    piece_refs = refs[:count]
    kind_ref, code_ref, temp_ref, *refs = refs[count:]
    if with_edges:
        first_ref, last_ref, spread_ref, target_ref, factor_ref, wall_ref, coef_ref, low_ref, high_ref, *refs = refs
    else:
        coef_ref, flux_ref, *refs = refs
    stack_ref, field_ref = refs
    size = groups // count
    me = lax.axis_index("vel")
    for away, ref in enumerate(piece_refs):
        owner = lax.rem(me + (count - away), count)
        for k in range(GAS):
            field_ref[k, pl.ds(pl.multiple_of(owner * size, size), size), :] = ref[k * size:(k + 1) * size, :]
    kind = kind_ref[...]
    code = code_ref[...]
    wall = temp_ref[...]
    rho, ux, uy, uz, temp, qx, qy, qz, em, flux = (field_ref[k] for k in range(GAS))
    if not with_edges:
        flux_ref[...] = flux
    inverse = 1.0 / wall
    uu = ux * ux + uy * uy + uz * uz
    boundary = kind > 0
    pressure = rho * temp
    per_t = 1.0 / temp
    decay = jnp.exp((-TIME_STEP / SHEAR_EXPONENT) * pressure * jnp.exp(-0.72 * jnp.log(temp)))
    amount = (1.0 - decay) * rho * per_t * lax.rsqrt(temp)
    bend = amount * ((1.0 - PRANDTL) / 5.0) * per_t * per_t / pressure
    kappa = (0.5 * LOG2E) * per_t
    qu = qx * ux + qy * uy + qz * uz
    rest = uu - 5.0 * temp
    twice = -2.0 * bend * HALF**2
    kappa_sq = -kappa * HALF**2
    kappa_u = (2.0 * HALF) * kappa
    wall_sq = (-0.5 * LOG2E * HALF**2) * inverse
    bqu = bend * qu * HALF**2
    solid = jnp.where(boundary, OFF, 0.0)
    rows = {
        T_SQ_HI: kappa_sq, T_SQ_LO: kappa_sq,
        T_X: kappa_u * ux, T_Y: kappa_u * uy, T_Z: kappa_u * uz, T_ONE: -kappa * uu,
        P_ONE: amount - bend * qu * rest,
        P_X: bend * HALF * (qx * rest + 2.0 * qu * ux),
        P_Y: bend * HALF * (qy * rest + 2.0 * qu * uy),
        P_Z: bend * HALF * (qz * rest + 2.0 * qu * uz),
        P_XX: twice * qx * ux - bqu, P_YY: twice * qy * uy - bqu, P_ZZ: twice * qz * uz - bqu,
        P_XY: twice * (qx * uy + qy * ux), P_XZ: twice * (qx * uz + qz * ux),
        P_YZ: twice * (qy * uz + qz * uy),
        P_XS: bend * HALF**3 * qx, P_YS: bend * HALF**3 * qy, P_ZS: bend * HALF**3 * qz,
        W_SQ_HI: wall_sq, W_SQ_LO: wall_sq,
        W_ONE: jnp.where(boundary, 0.0, OFF),
        W_XP: jnp.where(code == 1, solid, 0.0), W_XN: jnp.where(code == 0, solid, 0.0),
        W_YP: jnp.where(code == 3, solid, 0.0), W_YN: jnp.where(code == 2, solid, 0.0),
        B_E: decay, B_W: em * decay * inverse * lax.rsqrt(wall),
    }
    rows[P_XSL], rows[P_YSL], rows[P_ZSL] = rows[P_XS], rows[P_YS], rows[P_ZS]
    zero = jnp.zeros_like(wall)
    for k in range(PART):
        value = rows.get(k)
        for part in range(2):
            if value is None:
                stack_ref[pl.ds(part * PART + k, groups, stride=STRIDE), :] = zero
                continue
            hi = value.astype(jnp.bfloat16).astype(jnp.float32)
            stack_ref[pl.ds(part * PART + k, groups, stride=STRIDE), :] = hi
            value = value - hi

    def turn(g, carry):
        block = stack_ref[pl.ds(g * STRIDE, COEF), :]
        coef_ref[pl.ds(pl.multiple_of(g * LANES, LANES), LANES), :] = block.T.astype(jnp.bfloat16)
        return carry

    lax.fori_loop(0, groups, turn, 0, unroll=8)
    if not with_edges:
        return
    size = low_ref.shape[0]
    for flat_ref, start, out_ref in ((first_ref, 0, low_ref), (last_ref, groups * LANES - size, high_ref)):
        coef = coef_ref[start:start + size, :]
        even = dot(coef, spread_ref[...])
        for l in range(flat_ref.shape[1] // WIDE):
            columns = slice(l * WIDE, (l + 1) * WIDE)
            out_ref[:, columns] = relaxed(coef, even, flat_ref[:, columns], target_ref[:, columns],
                                          factor_ref[:, columns], wall_ref[:, columns])


def state(with_edges, pieces, kind, code, temp, flat, spread, tables, ncols):
    groups = kind.shape[0]
    cells, span = flat.shape
    size = 2 * ncols
    last = cells // size - 1
    whole = pl.BlockSpec(memory_space=pltpu.VMEM)
    operands = [*pieces, kind, code, temp]
    in_specs = [whole] * len(operands)
    out_shape = (jax.ShapeDtypeStruct((cells, COEF), jnp.bfloat16),)
    if with_edges:
        operands += [flat, flat, spread, *tables]
        in_specs += [pl.BlockSpec((size, span), lambda i: (0, 0)),
                     pl.BlockSpec((size, span), lambda i: (last, 0))] + [whole] * 4
        out_shape += (jax.ShapeDtypeStruct((size, span), jnp.float32),) * 2
    else:
        out_shape += (jax.ShapeDtypeStruct((groups, LANES), jnp.float32),)
    return pl.pallas_call(
        functools.partial(state_kernel, len(pieces), groups, with_edges),
        grid=(1,),
        out_shape=out_shape,
        in_specs=in_specs,
        out_specs=(whole,) * len(out_shape),
        scratch_shapes=[pltpu.VMEM((groups * STRIDE + 7, LANES), jnp.float32),
                        pltpu.VMEM((GAS, groups, LANES), jnp.float32)],
        compiler_params=pltpu.CompilerParams(vmem_limit_bytes=VMEM_LIMIT),
        name="state",
    )(*operands)


WIDE = 256


def relaxed(coef, even, flat, target, factor, wall):
    exponent = dot(coef, target)
    factor = dot(coef, factor)
    wall = dot(coef, wall)
    decay, amount = even[:, :LANES], even[:, LANES:]
    parts = []
    for h in range(WIDE // LANES):
        cut = slice(h * LANES, (h + 1) * LANES)
        bounded = jnp.where(wall[:, cut] > 0.0, flat[:, cut] * decay, amount * jnp.exp2(wall[:, cut]))
        parts.append(bounded + jnp.exp2(exponent[:, cut]) * factor[:, cut])
    return jnp.concatenate(parts, axis=1)


def relax_chunk(l, tables, coef_ref, even_ref, flat_ref):
    target_ref, factor_ref, wall_ref = tables
    columns = slice(l * WIDE, (l + 1) * WIDE)
    return relaxed(coef_ref[...], even_ref, flat_ref[:, columns],
                   target_ref[:, columns], factor_ref[:, columns], wall_ref[:, columns])


PAD = 8
BLOCK = 8


def transport_chunk(exact, rows, l, row, ncols, stencil_ref, out_ref, strip_ref, half_ref):
    nothing = jnp.minimum(pl.program_id(0), 0)
    shape = (ncols // 8, 8, LANES)
    for h in range(WIDE // LANES):
        columns = slice(l * WIDE + h * LANES, l * WIDE + (h + 1) * LANES)
        x0, x1, x2, vx, y0, y1, y2, _ = (stencil_ref[8 * k:8 * k + 8, columns][None] for k in range(8))
        x_up = jnp.broadcast_to(vx > 0, shape)
        ahead = 1 if h == 0 else -1

        def field(k):
            ref, start = row(k - 2)
            return ref[start:start + ncols, columns].reshape(shape)

        window = [field(k) for k in range(4)]
        for r in range(rows):
            window.append(field(r + 4))
            near = jnp.where(x_up, window[1], window[3])
            far = jnp.where(x_up, window[0], window[4])
            rowwise = x0 * window[2] + x1 * near + x2 * far
            window = window[1:]
            slot = h * BLOCK + r
            strip_ref[slot, PAD:PAD + ncols, :] = rowwise.reshape(ncols, LANES)

            def strip(k):
                return strip_ref[slot, pl.ds(nothing + PAD + k, ncols), :].reshape(shape)

            value = y0 * rowwise + y1 * strip(ahead) + y2 * strip(2 * ahead)
            value = value.reshape(ncols, LANES)
            cut = slice(r * ncols, (r + 1) * ncols)
            out_ref[cut, columns] = value
            upper = value.astype(jnp.bfloat16)
            half_ref[0, cut, columns] = upper
            if exact:
                half_ref[1, cut, columns] = (value - upper.astype(jnp.float32)).astype(jnp.bfloat16)


def chunk_sums(exact, l, table, sums_ref, half_ref):
    columns = slice(l * WIDE, (l + 1) * WIDE)
    for k in range(1 + exact):
        term = dot(half_ref[k, :, columns], sums_ref[columns, :])
        table = term if table is None else table + term
    return table


def moments(rows, table, ncols, group, kind_ref, code_ref, parts_ref):
    for g in range(rows * ncols // LANES):
        total = table[g * LANES:(g + 1) * LANES, :].T
        kind = kind_ref[pl.ds(group + g, 1), :]
        code = code_ref[pl.ds(group + g, 1), :]
        gas = kind == 0

        def keep(*codes):
            hit = (code == codes[0]) | (code == codes[1])
            return jnp.where(gas | jnp.logical_not(hit), 1.0, 0.0)

        kept = (keep(0, 2) * total[0:16] + keep(0, 3) * total[16:32]
                + keep(1, 2) * total[32:48] + keep(1, 3) * total[48:64])
        incident = jnp.where(code == 0, total[64:65], jnp.where(code == 1, total[65:66], jnp.where(
            code == 2, total[66:67], total[67:68])))
        parts_ref[pl.ds((group + g) * ROWS, ROWS), :] = jnp.concatenate(
            [kept[0:10], kept[10:13] + kept[13:16], incident], axis=0)


END = 2


DEPTH = 4
LAG = 2


def inner_kernel(relax, exact, blocks, ncols, flat_ref, kind_ref, code_ref, sums_ref, stencil_ref, *refs):
    if relax:
        coef_ref, spread_ref, *tables = refs[:5]
        refs = refs[5:]
    out_ref, parts_ref, head_ref, tail_ref = refs[:4]
    field_refs = refs[4:4 + DEPTH]
    even_ref, strip_ref, half_ref = refs[4 + DEPTH:]
    i = pl.program_id(0)
    block = BLOCK * ncols
    span = flat_ref.shape[1]

    @pl.when(i == 0)
    def _():
        strip_ref[...] = jnp.zeros_like(strip_ref)

    def work(place, relaxing, moving):
        new_ref = field_refs[place]
        old_ref, here_ref, next_ref = (field_refs[(place + k) % DEPTH] for k in (1, 2, 3))

        def row(k):
            ref = old_ref if k < 0 else next_ref if k >= BLOCK else here_ref
            return ref, k % BLOCK * ncols

        if relaxing and relax:
            even_ref[...] = dot(coef_ref[...], spread_ref[...])
        table = None
        for l in range(span // WIDE):
            if relaxing:
                columns = slice(l * WIDE, (l + 1) * WIDE)
                if relax:
                    new_ref[:, columns] = relax_chunk(l, tables, coef_ref, even_ref, flat_ref)
                else:
                    for start in range(0, block, 2 * ncols):
                        cut = slice(start, start + 2 * ncols)
                        new_ref[cut, columns] = turned(flat_ref[cut, columns], l, span)
            if moving:
                transport_chunk(exact, BLOCK, l, row, ncols, stencil_ref, out_ref, strip_ref, half_ref)
                table = chunk_sums(exact, l, table, sums_ref, half_ref)
        if moving:
            moments(BLOCK, table, ncols, (i - LAG) * (block // LANES), kind_ref, code_ref, parts_ref)

    for place in range(min(LAG, blocks)):
        pl.when(i == place)(functools.partial(work, place, True, False))
    for place in range(DEPTH):
        if place < blocks:
            pl.when((i >= LAG) & (i < blocks) & (i % DEPTH == place))(functools.partial(work, place, True, True))
    for last in range(blocks, blocks + LAG):
        pl.when(i == last)(functools.partial(work, last % DEPTH, False, True))

    size = head_ref.shape[0]

    @pl.when(i == 0)
    def _():
        head_ref[...] = field_refs[0][:size, :]

    @pl.when(i == blocks)
    def _():
        tail_ref[...] = field_refs[(blocks - 1) % DEPTH][block - size:, :]


def outer_kernel(relax, exact, ncols, count, flat_ref, given_ref, head_ref, tail_ref, low_ref, high_ref,
                 kind_ref, code_ref, sums_ref, stencil_ref, out_ref, *refs):
    slot_refs = refs[:count]
    parts_ref, field_ref, strip_ref, half_ref = refs[count:]
    i = pl.program_id(0)
    edge = END * ncols
    size = head_ref.shape[0]
    span = out_ref.shape[1]
    groups = parts_ref.shape[0] // ROWS

    def halo(ref, start):
        for l in range(span // WIDE):
            columns = slice(l * WIDE, (l + 1) * WIDE)
            values = ref[:, columns]
            field_ref[start:start + edge, columns] = values if relax else turned(values, l, span)

    @pl.when(i == 0)
    def _():
        strip_ref[...] = jnp.zeros_like(strip_ref)
        parts_ref[...] = given_ref[...]
        halo(low_ref, 0)
        field_ref[edge:, :] = head_ref[...]

    @pl.when(i == 1)
    def _():
        field_ref[:size, :] = tail_ref[...]
        halo(high_ref, size)

    def row(k):
        return field_ref, (k + END) * ncols

    table = None
    for l in range(span // WIDE):
        transport_chunk(exact, END, l, row, ncols, stencil_ref, out_ref, strip_ref, half_ref)
        table = chunk_sums(exact, l, table, sums_ref, half_ref)
    moments(END, table, ncols, i * (groups - edge // LANES), kind_ref, code_ref, parts_ref)

    @pl.when(i == 1)
    def _():
        me = lax.axis_index("vel")
        rows = slot_refs[0].shape[0]
        for away, ref in enumerate(slot_refs):
            owner = lax.rem(me + away, count)
            ref[...] = parts_ref[pl.ds(pl.multiple_of(owner * rows, 4), rows), :]


def inner(relax, exact, flat, coef, kind, code, spread, tables, sums, stencil, ncols):
    cells, span = flat.shape
    block = BLOCK * ncols
    blocks = cells // block
    groups = cells // LANES
    whole = pl.BlockSpec(memory_space=pltpu.VMEM)
    end = jax.ShapeDtypeStruct((2 * END * ncols, span), jnp.float32)
    operands = [flat, kind, code, sums, stencil]
    in_specs = [pl.BlockSpec((block, span), lambda i: (jnp.minimum(i, blocks - 1), 0))] + [whole] * 4
    if relax:
        operands += [coef, spread, *tables]
        in_specs += [pl.BlockSpec((block, COEF), lambda i: (jnp.minimum(i, blocks - 1), 0))] + [whole] * 4
    return pl.pallas_call(
        functools.partial(inner_kernel, relax, exact, blocks, ncols),
        grid=(blocks + LAG,),
        out_shape=(jax.ShapeDtypeStruct((cells, span), jnp.float32),
                   jax.ShapeDtypeStruct((groups * ROWS, LANES), jnp.float32), end, end),
        in_specs=in_specs,
        out_specs=(pl.BlockSpec((block, span), lambda i: (jnp.maximum(i - LAG, 0), 0)), whole, whole, whole),
        scratch_shapes=[pltpu.VMEM((block, span), jnp.float32)] * DEPTH + [
                        pltpu.VMEM((block, 2 * LANES), jnp.float32),
                        pltpu.VMEM((WIDE // LANES * BLOCK, ncols + 2 * PAD, LANES), jnp.float32),
                        pltpu.VMEM((1 + exact, block, span), jnp.bfloat16)],
        compiler_params=pltpu.CompilerParams(vmem_limit_bytes=VMEM_LIMIT),
        cost_estimate=pl.CostEstimate(flops=12 * cells * span * COEF, bytes_accessed=8 * cells * span,
                                      transcendentals=2 * cells * span),
        name="inner" if relax else "inner_first",
    )(*operands)


def outer(relax, exact, flat, parts, head, tail, low, high, kind, code, sums, stencil, ncols):
    cells, span = flat.shape
    edge = END * ncols
    last = cells // edge - 1
    count = lax.axis_size("vel")
    whole = pl.BlockSpec(memory_space=pltpu.VMEM)
    slot = jax.ShapeDtypeStruct((parts.shape[0] // count, LANES), jnp.float32)
    flat, *slots = pl.pallas_call(
        functools.partial(outer_kernel, relax, exact, ncols, count),
        grid=(2,),
        out_shape=(jax.ShapeDtypeStruct((cells, span), jnp.float32),) + (slot,) * count,
        in_specs=[pl.BlockSpec(memory_space=pl.ANY)] + [whole] * 9,
        out_specs=(pl.BlockSpec((edge, span), lambda i: (i * last, 0)),) + (whole,) * count,
        scratch_shapes=[pltpu.VMEM(parts.shape, jnp.float32),
                        pltpu.VMEM((3 * edge, span), jnp.float32),
                        pltpu.VMEM((WIDE // LANES * BLOCK, ncols + 2 * PAD, LANES), jnp.float32),
                        pltpu.VMEM((1 + exact, edge, span), jnp.bfloat16)],
        input_output_aliases={0: 0},
        compiler_params=pltpu.CompilerParams(vmem_limit_bytes=VMEM_LIMIT),
        name="outer" if relax else "outer_first",
    )(flat, parts, head, tail, low, high, kind, code, sums, stencil)
    return flat, slots


def last_kernel(flat_ref, coef_ref, spread_ref, target_ref, factor_ref, wall_ref, out_ref, even_ref):
    span = flat_ref.shape[1]
    even_ref[...] = dot(coef_ref[...], spread_ref[...])
    for l in range(span // WIDE):
        values = relax_chunk(l, (target_ref, factor_ref, wall_ref), coef_ref, even_ref, flat_ref)
        out_ref[:, l * WIDE:(l + 1) * WIDE] = turned(values, l, span, back=True)


def finish(flat, coef, spread, tables, ncols):
    cells, span = flat.shape
    block = 8 * ncols
    whole = pl.BlockSpec(memory_space=pltpu.VMEM)
    return pl.pallas_call(
        last_kernel,
        grid=(cells // block,),
        out_shape=jax.ShapeDtypeStruct((cells, span), jnp.float32),
        in_specs=[pl.BlockSpec((block, span), lambda i: (i, 0)),
                  pl.BlockSpec((block, COEF), lambda i: (i, 0)),
                  whole, whole, whole, whole],
        out_specs=pl.BlockSpec((block, span), lambda i: (i, 0)),
        scratch_shapes=[pltpu.VMEM((block, 2 * LANES), jnp.float32)],
        compiler_params=pltpu.CompilerParams(vmem_limit_bytes=VMEM_LIMIT),
        name="finish",
    )(flat, coef, spread, *tables)


def exchange(first, last):
    size = lax.axis_size("space")
    up = [(i, (i + 1) % size) for i in range(size - 1)]
    down = [(j, i) for i, j in up]
    return lax.ppermute(last, "space", up), lax.ppermute(first, "space", down)


def swap(slots):
    count = len(slots)
    return [slots[0]] + [lax.ppermute(slots[k], "vel", [(i, (i + k) % count) for i in range(count)])
                         for k in range(1, count)]


def shards(dist, cell_kind, normal_code, wall_temp):
    nrows, ncols, span = dist.shape
    cells = nrows * ncols
    groups = cells // LANES
    kind = cell_kind.reshape(groups, LANES)
    code = normal_code.reshape(groups, LANES)
    temp = wall_temp.reshape(groups, LANES)
    flat = dist.reshape(cells, span)
    target, factor, wall, sums, stencil, spread = setup(span)
    tables = (target, factor, wall)
    edge = 2 * ncols
    coef = None
    low, high = flat[:edge], flat[cells - edge:]
    for step in range(STEPS):
        final = step == STEPS - 1
        low, high = exchange(low, high)
        flat, parts, head, tail = inner(step > 0, final, flat, coef, kind, code, spread, tables, sums, stencil, ncols)
        flat, slots = outer(step > 0, final, flat, parts, head, tail, low, high, kind, code, sums, stencil, ncols)
        own = gas(swap(slots), kind, code, temp)
        coef, *others = state(not final, swap([own] * len(slots)), kind, code, temp, flat, spread, tables, ncols)
        if not final:
            low, high = others
    flux = others[0]
    current = finish(flat, coef, spread, tables, ncols)
    columns = ncols // lax.axis_size("vel")
    own_flux = lax.dynamic_slice_in_dim(flux.reshape(nrows, ncols), lax.axis_index("vel") * columns, columns, 1)
    return current.reshape(nrows, ncols, span), own_flux


def solution(mesh):
    placed = (P("space", None, "vel"), P("space", None), P("space", None), P("space", None))
    return jax.shard_map(
        shards,
        mesh=mesh,
        in_specs=placed,
        out_specs=(P("space", None, "vel"), P("space", "vel")),
        check_vma=False,
    )
```

```python
import functools
import math

import jax
import jax.numpy as jnp
from jax import lax
from jax.experimental import pallas as pl
from jax.experimental.pallas import tpu as pltpu
from jax.sharding import PartitionSpec as P

NQ = 16
STEPS = 4
LIMIT = 5.0
TIME_STEP = 0.05
SIGMA = 0.8
LATENT = 5.0
PRANDTL = 2.0 / 3.0
SHEAR_EXPONENT = 0.1

SPACING = 2.0 * LIMIT / NQ
HALF = 0.5 * SPACING
WEIGHT = SPACING**3 / (2.0 * math.pi) ** 1.5
LOG2E = math.log2(math.e)
LANES = 128
MOMENTS = 16
ROWS = 14
GAS = 10
OFF = 1024.0

T_SQ_HI, T_SQ_LO, T_X, T_Y, T_Z, T_ONE = range(6)
P_ONE, P_X, P_Y, P_Z, P_XX, P_YY, P_ZZ, P_XY, P_XZ, P_YZ = range(6, 16)
P_XS, P_YS, P_ZS, P_XSL, P_YSL, P_ZSL = range(16, 22)
W_SQ_HI, W_SQ_LO, W_ONE, W_XP, W_XN, W_YP, W_YN = range(22, 29)
B_E, B_W = 29, 30
PART = 32
COEF = 2 * PART
STRIDE = COEF + 1

VMEM_LIMIT = 44 * 1024 * 1024
SMALL_LIMIT = 24 * 1024 * 1024


def setup_kernel(span, kind_in_ref, code_in_ref, temp_in_ref, kind_ref, code_ref, temp_ref, target_ref, factor_ref, wall_ref, sums_ref, stencil_ref, spread_ref,
                 feature_ref, moment_ref):
    for in_ref, ref in ((kind_in_ref, kind_ref), (code_in_ref, code_ref), (temp_in_ref, temp_ref)):
        ncols = in_ref.shape[1]
        joined = LANES // ncols
        for k in range(joined):
            ref[:, k * ncols:(k + 1) * ncols] = in_ref[pl.ds(k, ref.shape[0], stride=joined), :]
    shape = (8, span)
    place = lax.broadcasted_iota(jnp.int32, shape, 1)
    third = lax.axis_index("vel") * (span // WIDE) + place // WIDE
    first = place % NQ
    middle = place // NQ % NQ

    def odd(pick):
        return (2 * (pick % NQ) - (NQ - 1)).astype(jnp.float32)

    x, y, z = odd(first + third), odd(middle), odd(first + middle)
    one = jnp.ones(shape, jnp.float32)
    square = x * x + y * y + z * z
    square_hi = jnp.floor(square * (1.0 / 16.0)) * 16.0
    square_lo = square - square_hi

    def split(v):
        hi = jnp.floor(v * (1.0 / 128.0)) * 128.0
        return hi, v - hi

    xs, xsl = split(x * square)
    ys, ysl = split(y * square)
    zs, zsl = split(z * square)
    xp = jnp.where(x > 0, 1.0, 0.0)
    yp = jnp.where(y > 0, 1.0, 0.0)
    features = [square_hi, square_lo, x, y, z, one,
                one, x, y, z, x * x, y * y, z * z, x * y, x * z, y * z, xs, ys, zs, xsl, ysl, zsl,
                square_hi, square_lo, one, xp, one - xp, yp, one - yp]
    feature_ref[...] = jnp.zeros_like(feature_ref)
    for k, feature in enumerate(features):
        feature_ref[k:k + 1, :] = feature[0:1]
    row = lax.broadcasted_iota(jnp.int32, (PART, span), 0)
    for ref, low, high in ((target_ref, T_SQ_HI, P_ONE), (factor_ref, P_ONE, W_SQ_HI),
                           (wall_ref, W_SQ_HI, B_E)):
        chosen = jnp.where((row >= low) & (row < high), feature_ref[...], 0.0)
        ref[...] = jnp.concatenate([chosen, chosen], axis=0).astype(jnp.bfloat16)
    quadrants = (xp * yp, xp * (one - yp), (one - xp) * yp, (one - xp) * (one - yp))
    moment = feature_ref[P_ONE:W_SQ_HI, :]
    moment_ref[...] = jnp.zeros_like(moment_ref)
    for k, quadrant in enumerate(quadrants):
        moment_ref[MOMENTS * k:MOMENTS * (k + 1), :] = moment * quadrant[0:1]
    for k, speed in enumerate((-x, x, -y, y)):
        moment_ref[4 * MOMENTS + k:4 * MOMENTS + k + 1, :] = jnp.maximum(speed, 0.0)[0:1]
    for l in range(span // LANES):
        cut = slice(l * LANES, (l + 1) * LANES)
        sums_ref[cut, :] = moment_ref[:, cut].T.astype(jnp.bfloat16)
    for k, v in enumerate((x, y)):
        courant = jnp.abs(v) * (HALF * TIME_STEP)
        half_square = 0.5 * courant * courant
        for n, value in enumerate((1.0 - 1.5 * courant + half_square, 2.0 * courant - 2.0 * half_square,
                                   half_square - 0.5 * courant, v)):
            stencil_ref[8 * (4 * k + n):8 * (4 * k + n + 1), :] = value
    row = lax.broadcasted_iota(jnp.int32, (COEF, 2 * LANES), 0)
    column = lax.broadcasted_iota(jnp.int32, (COEF, 2 * LANES), 1)
    want = jnp.where(column < LANES, B_E, B_W)
    hit = row % PART == want
    spread_ref[...] = jnp.where(hit, 1.0, 0.0).astype(jnp.bfloat16)


def setup(span, *given):
    groups = given[0].size // LANES
    whole = pl.BlockSpec(memory_space=pltpu.VMEM)
    table = jax.ShapeDtypeStruct((COEF, span), jnp.bfloat16)
    return pl.pallas_call(
        functools.partial(setup_kernel, span),
        out_shape=tuple(jax.ShapeDtypeStruct((groups, LANES), g.dtype) for g in given) + (table, table, table,
                   jax.ShapeDtypeStruct((span, LANES), jnp.bfloat16),
                   jax.ShapeDtypeStruct((64, span), jnp.float32),
                   jax.ShapeDtypeStruct((COEF, 2 * LANES), jnp.bfloat16)),
        in_specs=[whole] * 3,
        out_specs=(whole,) * 9,
        scratch_shapes=[pltpu.VMEM((PART, span), jnp.float32), pltpu.VMEM((LANES, span), jnp.float32)],
        name="setup",
    )(*given)


def turned(values, l, span, back=False):
    third = lax.axis_index("vel") * (span // WIDE) + l
    shift = NQ * (third % NQ)
    return pltpu.roll(values, (WIDE - shift) % WIDE if back else shift, 1)


def dot(a, b):
    return jnp.dot(a, b, preferred_element_type=jnp.float32)


def gas_kernel(count, size, *refs):
    part_refs = refs[:count]
    kind_ref, code_ref, temp_ref, out_ref = refs[count:]
    mine = pl.ds(pl.multiple_of(lax.axis_index("vel") * size, size), size)

    def read(k, scale):
        value = part_refs[0][pl.ds(k, size, stride=ROWS), :]
        for ref in part_refs[1:]:
            value = value + ref[pl.ds(k, size, stride=ROWS), :]
        return value * (WEIGHT * scale)

    kind = kind_ref[mine, :]
    code = code_ref[mine, :]
    wall = temp_ref[mine, :]
    s0 = s1 = s2 = s3 = jnp.zeros_like(wall)
    inverse = 1.0 / wall
    for j in range(NQ // 2):
        speed = HALF * (2 * j + 1)
        e = jnp.exp(inverse * (-0.5 * speed * speed))
        s0, s1, s2, s3 = s0 + e, s1 + speed * e, s2 + speed**2 * e, s3 + speed**3 * e
    scale = (WEIGHT * 2.0) * inverse * lax.rsqrt(wall)
    norm = 2.0 * scale * s1 * s0 * s0
    f_one = 2.0 * scale * s0 * s0 * s0
    f_nn = 2.0 * scale * s2 * s0 * s0
    f_tt = f_nn
    f_ns = 2.0 * scale * (s3 * s0 * s0 + 2.0 * s1 * s2 * s0)
    saturated = jnp.exp(LATENT * (1.0 - inverse)) * inverse
    incident = read(13, HALF)
    share = jnp.where(kind == 2, SIGMA, 0.0)
    emitted = share * saturated + (1.0 - share) * incident / norm
    boundary = kind > 0
    flux = jnp.where(boundary, emitted * norm - incident, 0.0)
    em = jnp.where(boundary, emitted, 0.0)
    along_x = code < 2
    sign = jnp.where((code == 0) | (code == 2), 1.0, -1.0)
    sx = jnp.where(along_x, sign, 0.0)
    sy = jnp.where(along_x, 0.0, sign)

    rho = read(0, 1.0) + em * f_one
    em_n = em * norm
    em_s = em * f_ns
    mx = read(1, HALF) + sx * em_n
    my = read(2, HALF) + sy * em_n
    mz = read(3, HALF)
    mxx = read(4, HALF**2) + em * f_nn
    myy = read(5, HALF**2) + em * f_tt
    mzz = read(6, HALF**2) + em * f_tt
    mxy = read(7, HALF**2)
    mxz = read(8, HALF**2)
    myz = read(9, HALF**2)
    mxs = read(10, HALF**3) + sx * em_s
    mys = read(11, HALF**3) + sy * em_s
    mzs = read(12, HALF**3)
    msq = mxx + myy + mzz
    per = 1.0 / rho
    ux, uy, uz = mx * per, my * per, mz * per
    uu = ux * ux + uy * uy + uz * uz
    temp = (msq * per - uu) * (1.0 / 3.0)
    dotted = ux * mx + uy * my + uz * mz

    def heat(third, u, m, second):
        return 0.5 * (third - 2.0 * (ux * second[0] + uy * second[1] + uz * second[2]) + uu * m
                      - u * msq + 2.0 * u * dotted - u * uu * rho)

    qx = heat(mxs, ux, mx, (mxx, mxy, mxz))
    qy = heat(mys, uy, my, (mxy, myy, myz))
    qz = heat(mzs, uz, mz, (mxz, myz, mzz))
    for k, value in enumerate((rho, ux, uy, uz, temp, qx, qy, qz, em, flux)):
        out_ref[k * size:(k + 1) * size, :] = value


def gas(parts, kind, code, temp):
    size = parts[0].shape[0] // ROWS
    whole = pl.BlockSpec(memory_space=pltpu.VMEM)
    return pl.pallas_call(
        functools.partial(gas_kernel, len(parts), size),
        out_shape=jax.ShapeDtypeStruct((GAS * size, LANES), jnp.float32),
        in_specs=[whole] * (len(parts) + 3),
        out_specs=whole,
        name="gas",
    )(*parts, kind, code, temp)


def state_kernel(count, groups, with_edges, *refs):
    piece_refs = refs[:count]
    kind_ref, code_ref, temp_ref, *refs = refs[count:]
    if with_edges:
        first_ref, last_ref, spread_ref, target_ref, factor_ref, wall_ref, coef_ref, low_ref, high_ref, *refs = refs
    else:
        coef_ref, flux_ref, *refs = refs
    stack_ref, field_ref = refs
    size = groups // count
    me = lax.axis_index("vel")
    for away, ref in enumerate(piece_refs):
        owner = lax.rem(me + (count - away), count)
        for k in range(GAS):
            field_ref[k, pl.ds(pl.multiple_of(owner * size, size), size), :] = ref[k * size:(k + 1) * size, :]
    kind = kind_ref[...]
    code = code_ref[...]
    wall = temp_ref[...]
    rho, ux, uy, uz, temp, qx, qy, qz, em, flux = (field_ref[k] for k in range(GAS))
    if not with_edges:
        flux_ref[...] = flux
    inverse = 1.0 / wall
    uu = ux * ux + uy * uy + uz * uz
    boundary = kind > 0
    pressure = rho * temp
    per_t = 1.0 / temp
    decay = jnp.exp((-TIME_STEP / SHEAR_EXPONENT) * pressure * jnp.exp(-0.72 * jnp.log(temp)))
    amount = (1.0 - decay) * rho * per_t * lax.rsqrt(temp)
    bend = amount * ((1.0 - PRANDTL) / 5.0) * per_t * per_t / pressure
    kappa = (0.5 * LOG2E) * per_t
    qu = qx * ux + qy * uy + qz * uz
    rest = uu - 5.0 * temp
    twice = -2.0 * bend * HALF**2
    kappa_sq = -kappa * HALF**2
    kappa_u = (2.0 * HALF) * kappa
    wall_sq = (-0.5 * LOG2E * HALF**2) * inverse
    bqu = bend * qu * HALF**2
    solid = jnp.where(boundary, OFF, 0.0)
    rows = {
        T_SQ_HI: kappa_sq, T_SQ_LO: kappa_sq,
        T_X: kappa_u * ux, T_Y: kappa_u * uy, T_Z: kappa_u * uz, T_ONE: -kappa * uu,
        P_ONE: amount - bend * qu * rest,
        P_X: bend * HALF * (qx * rest + 2.0 * qu * ux),
        P_Y: bend * HALF * (qy * rest + 2.0 * qu * uy),
        P_Z: bend * HALF * (qz * rest + 2.0 * qu * uz),
        P_XX: twice * qx * ux - bqu, P_YY: twice * qy * uy - bqu, P_ZZ: twice * qz * uz - bqu,
        P_XY: twice * (qx * uy + qy * ux), P_XZ: twice * (qx * uz + qz * ux),
        P_YZ: twice * (qy * uz + qz * uy),
        P_XS: bend * HALF**3 * qx, P_YS: bend * HALF**3 * qy, P_ZS: bend * HALF**3 * qz,
        W_SQ_HI: wall_sq, W_SQ_LO: wall_sq,
        W_ONE: jnp.where(boundary, 0.0, OFF),
        W_XP: jnp.where(code == 1, solid, 0.0), W_XN: jnp.where(code == 0, solid, 0.0),
        W_YP: jnp.where(code == 3, solid, 0.0), W_YN: jnp.where(code == 2, solid, 0.0),
        B_E: decay, B_W: em * decay * inverse * lax.rsqrt(wall),
    }
    rows[P_XSL], rows[P_YSL], rows[P_ZSL] = rows[P_XS], rows[P_YS], rows[P_ZS]
    zero = jnp.zeros_like(wall)
    for k in range(PART):
        value = rows.get(k)
        for part in range(2):
            if value is None:
                stack_ref[pl.ds(part * PART + k, groups, stride=STRIDE), :] = zero
                continue
            hi = value.astype(jnp.bfloat16).astype(jnp.float32)
            stack_ref[pl.ds(part * PART + k, groups, stride=STRIDE), :] = hi
            value = value - hi

    def turn(g, carry):
        block = stack_ref[pl.ds(g * STRIDE, COEF), :]
        coef_ref[pl.ds(pl.multiple_of(g * LANES, LANES), LANES), :] = block.T.astype(jnp.bfloat16)
        return carry

    lax.fori_loop(0, groups, turn, 0, unroll=8)
    if not with_edges:
        return
    size = low_ref.shape[0]
    for flat_ref, start, out_ref in ((first_ref, 0, low_ref), (last_ref, groups * LANES - size, high_ref)):
        coef = coef_ref[start:start + size, :]
        even = dot(coef, spread_ref[...])
        for l in range(flat_ref.shape[1] // WIDE):
            columns = slice(l * WIDE, (l + 1) * WIDE)
            out_ref[:, columns] = relaxed(coef, even, flat_ref[:, columns], target_ref[:, columns],
                                          factor_ref[:, columns], wall_ref[:, columns])


def state(with_edges, pieces, kind, code, temp, first, last, spread, tables):
    groups = kind.shape[0]
    whole = pl.BlockSpec(memory_space=pltpu.VMEM)
    operands = [*pieces, kind, code, temp]
    out_shape = (jax.ShapeDtypeStruct((groups * LANES, COEF), jnp.bfloat16),)
    if with_edges:
        operands += [first, last, spread, *tables]
        out_shape += (jax.ShapeDtypeStruct(first.shape, jnp.float32),) * 2
    else:
        out_shape += (jax.ShapeDtypeStruct((groups, LANES), jnp.float32),)
    return pl.pallas_call(
        functools.partial(state_kernel, len(pieces), groups, with_edges),
        out_shape=out_shape,
        in_specs=[whole] * len(operands),
        out_specs=(whole,) * len(out_shape),
        scratch_shapes=[pltpu.VMEM((groups * STRIDE + 7, LANES), jnp.float32),
                        pltpu.VMEM((GAS, groups, LANES), jnp.float32)],
        compiler_params=pltpu.CompilerParams(vmem_limit_bytes=SMALL_LIMIT),
        name="state",
    )(*operands)


WIDE = 256


def relaxed(coef, even, flat, target, factor, wall):
    exponent = dot(coef, target)
    factor = dot(coef, factor)
    wall = dot(coef, wall)
    decay, amount = even[:, :LANES], even[:, LANES:]
    parts = []
    for h in range(WIDE // LANES):
        cut = slice(h * LANES, (h + 1) * LANES)
        bounded = jnp.where(wall[:, cut] > 0.0, flat[:, cut] * decay, amount * jnp.exp2(wall[:, cut]))
        parts.append(bounded + jnp.exp2(exponent[:, cut]) * factor[:, cut])
    return jnp.concatenate(parts, axis=1)


def relax_block(spread_ref, tables, coef_ref, even_ref, flat_ref, store):
    even_ref[...] = dot(coef_ref[...], spread_ref[...])

    def lane(l, carry):
        columns = pl.ds(pl.multiple_of(l * WIDE, WIDE), WIDE)
        target, factor, wall = (ref[:, columns] for ref in tables)
        store(l, relaxed(coef_ref[...], even_ref, flat_ref[:, columns], target, factor, wall))
        return carry

    lax.fori_loop(0, flat_ref.shape[1] // WIDE, lane, 0)


PAD = 8
BLOCK = 8


def transport(exact, rows, field_ref, base, ncols, group, kind_ref, code_ref, sums_ref, stencil_ref,
              out_ref, parts_ref, strip_ref, half_ref):
    span = out_ref.shape[1]
    nothing = jnp.minimum(lax.axis_index("vel"), 0)
    shape = (ncols // 8, 8, LANES)

    def lanes(l, carry):
        for h in range(WIDE // LANES):
            columns = pl.ds(pl.multiple_of(l * WIDE + h * LANES, LANES), LANES)
            x0, x1, x2, vx, y0, y1, y2, _ = (stencil_ref[8 * k:8 * k + 8, columns][None] for k in range(8))
            x_up = jnp.broadcast_to(vx > 0, shape)
            ahead = 1 if h == 0 else -1

            def field(k):
                start = pl.multiple_of(base + k * ncols, ncols)
                return field_ref[pl.ds(start, ncols), columns].reshape(shape)

            window = [field(k) for k in range(4)]
            for r in range(rows):
                window.append(field(r + 4))
                near = jnp.where(x_up, window[1], window[3])
                far = jnp.where(x_up, window[0], window[4])
                rowwise = x0 * window[2] + x1 * near + x2 * far
                window = window[1:]
                slot = h * BLOCK + r
                strip_ref[slot, PAD:PAD + ncols, :] = rowwise.reshape(ncols, LANES)

                def strip(k):
                    return strip_ref[slot, pl.ds(nothing + PAD + k, ncols), :].reshape(shape)

                value = y0 * rowwise + y1 * strip(ahead) + y2 * strip(2 * ahead)
                value = value.reshape(ncols, LANES)
                cut = slice(r * ncols, (r + 1) * ncols)
                out_ref[cut, columns] = value
                upper = value.astype(jnp.bfloat16)
                half_ref[0, cut, columns] = upper
                if exact:
                    half_ref[1, cut, columns] = (value - upper.astype(jnp.float32)).astype(jnp.bfloat16)
        return carry

    lax.fori_loop(0, span // WIDE, lanes, 0)
    table = dot(half_ref[0], sums_ref[...])
    if exact:
        table = table + dot(half_ref[1], sums_ref[...])
    for g in range(rows * ncols // LANES):
        total = table[g * LANES:(g + 1) * LANES, :].T
        kind = kind_ref[pl.ds(group + g, 1), :]
        code = code_ref[pl.ds(group + g, 1), :]
        gas = kind == 0

        def keep(*codes):
            hit = (code == codes[0]) | (code == codes[1])
            return jnp.where(gas | jnp.logical_not(hit), 1.0, 0.0)

        kept = (keep(0, 2) * total[0:16] + keep(0, 3) * total[16:32]
                + keep(1, 2) * total[32:48] + keep(1, 3) * total[48:64])
        incident = jnp.where(code == 0, total[64:65], jnp.where(code == 1, total[65:66], jnp.where(
            code == 2, total[66:67], total[67:68])))
        parts_ref[pl.ds((group + g) * ROWS, ROWS), :] = jnp.concatenate(
            [kept[0:10], kept[10:13] + kept[13:16], incident], axis=0)


END = 2


def inner_kernel(relax, exact, blocks, ncols, flat_ref, kind_ref, code_ref, sums_ref, stencil_ref, *refs):
    if relax:
        coef_ref, spread_ref, target_ref, factor_ref, wall_ref, *refs = refs
    out_ref, parts_ref, head_ref, tail_ref, field_ref, even_ref, strip_ref, half_ref = refs
    i = pl.program_id(0)
    block = BLOCK * ncols
    span = flat_ref.shape[1]
    edge = END * ncols

    @pl.when(i == 0)
    def _():
        strip_ref[...] = jnp.zeros_like(strip_ref)
        blank = jnp.zeros((edge, span), jnp.float32)
        field_ref[:edge, :] = blank
        field_ref[field_ref.shape[0] - edge:, :] = blank

    @pl.when(i < blocks)
    def _():
        here = pl.ds(pl.multiple_of(edge + i * block, edge), block)

        if relax:
            def store(l, values):
                field_ref[here, pl.ds(pl.multiple_of(l * WIDE, WIDE), WIDE)] = values

            relax_block(spread_ref, (target_ref, factor_ref, wall_ref), coef_ref, even_ref, flat_ref, store)
        else:
            def lane(l, carry):
                columns = pl.ds(pl.multiple_of(l * WIDE, WIDE), WIDE)
                field_ref[here, columns] = turned(flat_ref[:, columns], l, span)
                return carry

            lax.fori_loop(0, span // WIDE, lane, 0)

    @pl.when(i > 0)
    def _():
        transport(exact, BLOCK, field_ref, (i - 1) * block, ncols, (i - 1) * (block // LANES), kind_ref, code_ref,
                  sums_ref, stencil_ref, out_ref, parts_ref, strip_ref, half_ref)

    @pl.when(i == blocks)
    def _():
        size = head_ref.shape[0]
        last = field_ref.shape[0] - edge
        head_ref[...] = field_ref[edge:edge + size, :]
        tail_ref[...] = field_ref[last - size:last, :]


def outer_kernel(relax, exact, ncols, count, flat_ref, given_ref, head_ref, tail_ref, low_ref, high_ref,
                 kind_ref, code_ref, sums_ref, stencil_ref, out_ref, first_ref, last_ref, *refs):
    slot_refs = refs[:count]
    parts_ref, field_ref, strip_ref, half_ref, done_ref = refs[count:]
    edge = END * ncols
    size = head_ref.shape[0]
    span = first_ref.shape[1]
    groups = parts_ref.shape[0] // ROWS
    strip_ref[...] = jnp.zeros_like(strip_ref)
    parts_ref[...] = given_ref[...]

    def halo(ref, start):
        for l in range(span // WIDE):
            columns = slice(l * WIDE, (l + 1) * WIDE)
            values = ref[:, columns]
            field_ref[start:start + edge, columns] = values if relax else turned(values, l, span)

    halo(low_ref, 0)
    field_ref[edge:edge + size, :] = head_ref[...]
    field_ref[edge + size:edge + 2 * size, :] = tail_ref[...]
    halo(high_ref, edge + 2 * size)
    copies = []
    for k, (ref, base, group, start) in enumerate((
            (first_ref, 0, 0, 0), (last_ref, edge + size, groups - edge // LANES, out_ref.shape[0] - edge))):
        transport(exact, END, field_ref, base, ncols, group, kind_ref, code_ref,
                  sums_ref, stencil_ref, ref, parts_ref, strip_ref, half_ref)
        copies.append(pltpu.make_async_copy(ref, out_ref.at[pl.ds(start, edge), :], done_ref.at[k]))
        copies[-1].start()
    me = lax.axis_index("vel")
    rows = slot_refs[0].shape[0]
    for away, ref in enumerate(slot_refs):
        owner = lax.rem(me + away, count)
        ref[...] = parts_ref[pl.ds(pl.multiple_of(owner * rows, 4), rows), :]
    for copy in copies:
        copy.wait()


def inner(relax, exact, flat, coef, kind, code, spread, tables, sums, stencil, ncols):
    cells, span = flat.shape
    block = BLOCK * ncols
    blocks = cells // block
    groups = cells // LANES
    whole = pl.BlockSpec(memory_space=pltpu.VMEM)
    end = jax.ShapeDtypeStruct((2 * END * ncols, span), jnp.float32)
    operands = [flat, kind, code, sums, stencil]
    in_specs = [pl.BlockSpec((block, span), lambda i: (jnp.minimum(i, blocks - 1), 0))] + [whole] * 4
    if relax:
        operands += [coef, spread, *tables]
        in_specs += [pl.BlockSpec((block, COEF), lambda i: (jnp.minimum(i, blocks - 1), 0))] + [whole] * 4
    return pl.pallas_call(
        functools.partial(inner_kernel, relax, exact, blocks, ncols),
        grid=(blocks + 1,),
        out_shape=(jax.ShapeDtypeStruct((cells, span), jnp.float32),
                   jax.ShapeDtypeStruct((groups * ROWS, LANES), jnp.float32), end, end),
        in_specs=in_specs,
        out_specs=(pl.BlockSpec((block, span), lambda i: (jnp.maximum(i - 1, 0), 0)), whole, whole, whole),
        scratch_shapes=[pltpu.VMEM((cells + 2 * END * ncols, span), jnp.float32),
                        pltpu.VMEM((block, 2 * LANES), jnp.float32),
                        pltpu.VMEM((WIDE // LANES * BLOCK, ncols + 2 * PAD, LANES), jnp.float32),
                        pltpu.VMEM((1 + exact, block, span), jnp.bfloat16)],
        compiler_params=pltpu.CompilerParams(vmem_limit_bytes=VMEM_LIMIT),
        cost_estimate=pl.CostEstimate(flops=12 * cells * span * COEF, bytes_accessed=8 * cells * span,
                                      transcendentals=2 * cells * span),
        name="inner" if relax else "inner_first",
    )(*operands)


def outer(relax, exact, flat, parts, head, tail, low, high, kind, code, sums, stencil, ncols):
    cells, span = flat.shape
    edge = END * ncols
    count = lax.axis_size("vel")
    whole = pl.BlockSpec(memory_space=pltpu.VMEM)
    slot = jax.ShapeDtypeStruct((parts.shape[0] // count, LANES), jnp.float32)
    rim = jax.ShapeDtypeStruct((edge, span), jnp.float32)
    flat, first, last, *slots = pl.pallas_call(
        functools.partial(outer_kernel, relax, exact, ncols, count),
        out_shape=(jax.ShapeDtypeStruct((cells, span), jnp.float32), rim, rim) + (slot,) * count,
        in_specs=[pl.BlockSpec(memory_space=pl.ANY)] + [whole] * 9,
        out_specs=(pl.BlockSpec(memory_space=pl.ANY),) + (whole,) * (count + 2),
        scratch_shapes=[pltpu.VMEM(parts.shape, jnp.float32),
                        pltpu.VMEM((6 * edge, span), jnp.float32),
                        pltpu.VMEM((WIDE // LANES * BLOCK, ncols + 2 * PAD, LANES), jnp.float32),
                        pltpu.VMEM((1 + exact, edge, span), jnp.bfloat16),
                        pltpu.SemaphoreType.DMA((2,))],
        input_output_aliases={0: 0},
        compiler_params=pltpu.CompilerParams(vmem_limit_bytes=SMALL_LIMIT),
        name="outer" if relax else "outer_first",
    )(flat, parts, head, tail, low, high, kind, code, sums, stencil)
    return flat, first, last, slots


def last_kernel(flat_ref, coef_ref, spread_ref, target_ref, factor_ref, wall_ref, out_ref, even_ref):
    span = flat_ref.shape[1]

    def store(l, values):
        out_ref[:, pl.ds(pl.multiple_of(l * WIDE, WIDE), WIDE)] = turned(values, l, span, back=True)

    relax_block(spread_ref, (target_ref, factor_ref, wall_ref), coef_ref, even_ref, flat_ref, store)


def finish(flat, coef, spread, tables, ncols):
    cells, span = flat.shape
    block = 8 * ncols
    whole = pl.BlockSpec(memory_space=pltpu.VMEM)
    return pl.pallas_call(
        last_kernel,
        grid=(cells // block,),
        out_shape=jax.ShapeDtypeStruct((cells, span), jnp.float32),
        in_specs=[pl.BlockSpec((block, span), lambda i: (i, 0)),
                  pl.BlockSpec((block, COEF), lambda i: (i, 0)),
                  whole, whole, whole, whole],
        out_specs=pl.BlockSpec((block, span), lambda i: (i, 0)),
        scratch_shapes=[pltpu.VMEM((block, 2 * LANES), jnp.float32)],
        compiler_params=pltpu.CompilerParams(vmem_limit_bytes=VMEM_LIMIT),
        name="finish",
    )(flat, coef, spread, *tables)


def exchange(first, last):
    size = lax.axis_size("space")
    up = [(i, (i + 1) % size) for i in range(size - 1)]
    down = [(j, i) for i, j in up]
    return lax.ppermute(last, "space", up), lax.ppermute(first, "space", down)


def swap(slots):
    count = len(slots)
    return [slots[0]] + [lax.ppermute(slots[k], "vel", [(i, (i + k) % count) for i in range(count)])
                         for k in range(1, count)]


def shards(dist, cell_kind, normal_code, wall_temp):
    nrows, ncols, span = dist.shape
    cells = nrows * ncols
    flat = dist.reshape(cells, span)
    kind, code, temp, target, factor, wall, sums, stencil, spread = setup(span, cell_kind, normal_code, wall_temp)
    tables = (target, factor, wall)
    edge = 2 * ncols
    coef = None
    low, high = flat[:edge], flat[cells - edge:]
    for step in range(STEPS):
        final = step == STEPS - 1
        low, high = exchange(low, high)
        flat, parts, head, tail = inner(step > 0, final, flat, coef, kind, code, spread, tables, sums, stencil, ncols)
        flat, first, last, slots = outer(step > 0, final, flat, parts, head, tail, low, high, kind, code, sums, stencil, ncols)
        own = gas(swap(slots), kind, code, temp)
        coef, *others = state(not final, swap([own] * len(slots)), kind, code, temp, first, last, spread, tables)
        if not final:
            low, high = others
    flux = others[0]
    current = finish(flat, coef, spread, tables, ncols)
    columns = ncols // lax.axis_size("vel")
    own_flux = lax.dynamic_slice_in_dim(flux.reshape(nrows, ncols), lax.axis_index("vel") * columns, columns, 1)
    return current.reshape(nrows, ncols, span), own_flux


def solution(mesh):
    placed = (P("space", None, "vel"), P("space", None), P("space", None), P("space", None))
    return jax.shard_map(
        shards,
        mesh=mesh,
        in_specs=placed,
        out_specs=(P("space", None, "vel"), P("space", "vel")),
        check_vma=False,
    )
```

```python
import functools
import math

import jax
import jax.numpy as jnp
from jax import lax
from jax.experimental import pallas as pl
from jax.experimental.pallas import tpu as pltpu
from jax.sharding import PartitionSpec as P

NQ = 16
STEPS = 4
LIMIT = 5.0
TIME_STEP = 0.05
SIGMA = 0.8
LATENT = 5.0
PRANDTL = 2.0 / 3.0
SHEAR_EXPONENT = 0.1

SPACING = 2.0 * LIMIT / NQ
HALF = 0.5 * SPACING
WEIGHT = SPACING**3 / (2.0 * math.pi) ** 1.5
LOG2E = math.log2(math.e)
LANES = 128
MOMENTS = 16
ROWS = 14
GAS = 10
OFF = 1024.0

T_SQ_HI, T_SQ_LO, T_X, T_Y, T_Z, T_ONE = range(6)
P_ONE, P_X, P_Y, P_Z, P_XX, P_YY, P_ZZ, P_XY, P_XZ, P_YZ = range(6, 16)
P_XS, P_YS, P_ZS, P_XSL, P_YSL, P_ZSL = range(16, 22)
W_SQ_HI, W_SQ_LO, W_ONE, W_XP, W_XN, W_YP, W_YN = range(22, 29)
B_E, B_W = 29, 30
PART = 32
COEF = 2 * PART
STRIDE = COEF + 1

VMEM_LIMIT = 60 * 1024 * 1024
SMALL_LIMIT = 52 * 1024 * 1024


def setup_kernel(span, kind_in_ref, code_in_ref, temp_in_ref, kind_ref, code_ref, temp_ref, target_ref, factor_ref, wall_ref, sums_ref, stencil_ref, spread_ref,
                 feature_ref, moment_ref):
    for in_ref, ref in ((kind_in_ref, kind_ref), (code_in_ref, code_ref), (temp_in_ref, temp_ref)):
        ncols = in_ref.shape[1]
        joined = LANES // ncols
        for k in range(joined):
            ref[:, k * ncols:(k + 1) * ncols] = in_ref[pl.ds(k, ref.shape[0], stride=joined), :]
    shape = (8, span)
    place = lax.broadcasted_iota(jnp.int32, shape, 1)
    third = lax.axis_index("vel") * (span // WIDE) + place // WIDE
    first = place % NQ
    middle = place // NQ % NQ

    def odd(pick):
        return (2 * (pick % NQ) - (NQ - 1)).astype(jnp.float32)

    x, y, z = odd(first + third), odd(middle), odd(first + middle)
    one = jnp.ones(shape, jnp.float32)
    square = x * x + y * y + z * z
    square_hi = jnp.floor(square * (1.0 / 16.0)) * 16.0
    square_lo = square - square_hi

    def split(v):
        hi = jnp.floor(v * (1.0 / 128.0)) * 128.0
        return hi, v - hi

    xs, xsl = split(x * square)
    ys, ysl = split(y * square)
    zs, zsl = split(z * square)
    xp = jnp.where(x > 0, 1.0, 0.0)
    yp = jnp.where(y > 0, 1.0, 0.0)
    features = [square_hi, square_lo, x, y, z, one,
                one, x, y, z, x * x, y * y, z * z, x * y, x * z, y * z, xs, ys, zs, xsl, ysl, zsl,
                square_hi, square_lo, one, xp, one - xp, yp, one - yp]
    feature_ref[...] = jnp.zeros_like(feature_ref)
    for k, feature in enumerate(features):
        feature_ref[k:k + 1, :] = feature[0:1]
    row = lax.broadcasted_iota(jnp.int32, (PART, span), 0)
    for ref, low, high in ((target_ref, T_SQ_HI, P_ONE), (factor_ref, P_ONE, W_SQ_HI),
                           (wall_ref, W_SQ_HI, B_E)):
        chosen = jnp.where((row >= low) & (row < high), feature_ref[...], 0.0)
        ref[...] = jnp.concatenate([chosen, chosen], axis=0).astype(jnp.bfloat16)
    quadrants = (xp * yp, xp * (one - yp), (one - xp) * yp, (one - xp) * (one - yp))
    moment = feature_ref[P_ONE:W_SQ_HI, :]
    moment_ref[...] = jnp.zeros_like(moment_ref)
    for k, quadrant in enumerate(quadrants):
        moment_ref[MOMENTS * k:MOMENTS * (k + 1), :] = moment * quadrant[0:1]
    for k, speed in enumerate((-x, x, -y, y)):
        moment_ref[4 * MOMENTS + k:4 * MOMENTS + k + 1, :] = jnp.maximum(speed, 0.0)[0:1]
    for l in range(span // LANES):
        cut = slice(l * LANES, (l + 1) * LANES)
        sums_ref[cut, :] = moment_ref[:, cut].T.astype(jnp.bfloat16)
    for k, v in enumerate((x, y)):
        courant = jnp.abs(v) * (HALF * TIME_STEP)
        half_square = 0.5 * courant * courant
        for n, value in enumerate((1.0 - 1.5 * courant + half_square, 2.0 * courant - 2.0 * half_square,
                                   half_square - 0.5 * courant, v)):
            stencil_ref[8 * (4 * k + n):8 * (4 * k + n + 1), :] = value
    row = lax.broadcasted_iota(jnp.int32, (COEF, 2 * LANES), 0)
    column = lax.broadcasted_iota(jnp.int32, (COEF, 2 * LANES), 1)
    want = jnp.where(column < LANES, B_E, B_W)
    hit = row % PART == want
    spread_ref[...] = jnp.where(hit, 1.0, 0.0).astype(jnp.bfloat16)


def setup(span, *given):
    groups = given[0].size // LANES
    whole = pl.BlockSpec(memory_space=pltpu.VMEM)
    table = jax.ShapeDtypeStruct((COEF, span), jnp.bfloat16)
    return pl.pallas_call(
        functools.partial(setup_kernel, span),
        out_shape=tuple(jax.ShapeDtypeStruct((groups, LANES), g.dtype) for g in given) + (table, table, table,
                   jax.ShapeDtypeStruct((span, LANES), jnp.bfloat16),
                   jax.ShapeDtypeStruct((64, span), jnp.float32),
                   jax.ShapeDtypeStruct((COEF, 2 * LANES), jnp.bfloat16)),
        in_specs=[whole] * 3,
        out_specs=(whole,) * 9,
        scratch_shapes=[pltpu.VMEM((PART, span), jnp.float32), pltpu.VMEM((LANES, span), jnp.float32)],
        name="setup",
    )(*given)


def turned(values, l, span, back=False):
    third = lax.axis_index("vel") * (span // WIDE) + l
    shift = NQ * (third % NQ)
    return pltpu.roll(values, (WIDE - shift) % WIDE if back else shift, 1)


def dot(a, b):
    return jnp.dot(a, b, preferred_element_type=jnp.float32)


def gas_kernel(count, size, *refs):
    part_refs = refs[:count]
    kind_ref, code_ref, temp_ref, out_ref = refs[count:]
    mine = pl.ds(pl.multiple_of(lax.axis_index("vel") * size, size), size)

    def read(k, scale):
        value = part_refs[0][pl.ds(k, size, stride=ROWS), :]
        for ref in part_refs[1:]:
            value = value + ref[pl.ds(k, size, stride=ROWS), :]
        return value * (WEIGHT * scale)

    kind = kind_ref[mine, :]
    code = code_ref[mine, :]
    wall = temp_ref[mine, :]
    s0 = s1 = s2 = s3 = jnp.zeros_like(wall)
    inverse = 1.0 / wall
    for j in range(NQ // 2):
        speed = HALF * (2 * j + 1)
        e = jnp.exp(inverse * (-0.5 * speed * speed))
        s0, s1, s2, s3 = s0 + e, s1 + speed * e, s2 + speed**2 * e, s3 + speed**3 * e
    scale = (WEIGHT * 2.0) * inverse * lax.rsqrt(wall)
    norm = 2.0 * scale * s1 * s0 * s0
    f_one = 2.0 * scale * s0 * s0 * s0
    f_nn = 2.0 * scale * s2 * s0 * s0
    f_tt = f_nn
    f_ns = 2.0 * scale * (s3 * s0 * s0 + 2.0 * s1 * s2 * s0)
    saturated = jnp.exp(LATENT * (1.0 - inverse)) * inverse
    incident = read(13, HALF)
    share = jnp.where(kind == 2, SIGMA, 0.0)
    emitted = share * saturated + (1.0 - share) * incident / norm
    boundary = kind > 0
    flux = jnp.where(boundary, emitted * norm - incident, 0.0)
    em = jnp.where(boundary, emitted, 0.0)
    along_x = code < 2
    sign = jnp.where((code == 0) | (code == 2), 1.0, -1.0)
    sx = jnp.where(along_x, sign, 0.0)
    sy = jnp.where(along_x, 0.0, sign)

    rho = read(0, 1.0) + em * f_one
    em_n = em * norm
    em_s = em * f_ns
    mx = read(1, HALF) + sx * em_n
    my = read(2, HALF) + sy * em_n
    mz = read(3, HALF)
    mxx = read(4, HALF**2) + em * f_nn
    myy = read(5, HALF**2) + em * f_tt
    mzz = read(6, HALF**2) + em * f_tt
    mxy = read(7, HALF**2)
    mxz = read(8, HALF**2)
    myz = read(9, HALF**2)
    mxs = read(10, HALF**3) + sx * em_s
    mys = read(11, HALF**3) + sy * em_s
    mzs = read(12, HALF**3)
    msq = mxx + myy + mzz
    per = 1.0 / rho
    ux, uy, uz = mx * per, my * per, mz * per
    uu = ux * ux + uy * uy + uz * uz
    temp = (msq * per - uu) * (1.0 / 3.0)
    dotted = ux * mx + uy * my + uz * mz

    def heat(third, u, m, second):
        return 0.5 * (third - 2.0 * (ux * second[0] + uy * second[1] + uz * second[2]) + uu * m
                      - u * msq + 2.0 * u * dotted - u * uu * rho)

    qx = heat(mxs, ux, mx, (mxx, mxy, mxz))
    qy = heat(mys, uy, my, (mxy, myy, myz))
    qz = heat(mzs, uz, mz, (mxz, myz, mzz))
    for k, value in enumerate((rho, ux, uy, uz, temp, qx, qy, qz, em, flux)):
        out_ref[k * size:(k + 1) * size, :] = value


def gas(parts, kind, code, temp):
    size = parts[0].shape[0] // ROWS
    whole = pl.BlockSpec(memory_space=pltpu.VMEM)
    return pl.pallas_call(
        functools.partial(gas_kernel, len(parts), size),
        out_shape=jax.ShapeDtypeStruct((GAS * size, LANES), jnp.float32),
        in_specs=[whole] * (len(parts) + 3),
        out_specs=whole,
        name="gas",
    )(*parts, kind, code, temp)


def state_kernel(count, groups, with_edges, *refs):
    piece_refs = refs[:count]
    kind_ref, code_ref, temp_ref, *refs = refs[count:]
    if with_edges:
        first_ref, last_ref, spread_ref, target_ref, factor_ref, wall_ref, coef_ref, low_ref, high_ref, *refs = refs
    else:
        coef_ref, flux_ref, *refs = refs
    stack_ref, field_ref = refs
    size = groups // count
    me = lax.axis_index("vel")
    for away, ref in enumerate(piece_refs):
        owner = lax.rem(me + (count - away), count)
        for k in range(GAS):
            field_ref[k, pl.ds(pl.multiple_of(owner * size, size), size), :] = ref[k * size:(k + 1) * size, :]
    kind = kind_ref[...]
    code = code_ref[...]
    wall = temp_ref[...]
    rho, ux, uy, uz, temp, qx, qy, qz, em, flux = (field_ref[k] for k in range(GAS))
    if not with_edges:
        flux_ref[...] = flux
    inverse = 1.0 / wall
    uu = ux * ux + uy * uy + uz * uz
    boundary = kind > 0
    pressure = rho * temp
    per_t = 1.0 / temp
    decay = jnp.exp((-TIME_STEP / SHEAR_EXPONENT) * pressure * jnp.exp(-0.72 * jnp.log(temp)))
    amount = (1.0 - decay) * rho * per_t * lax.rsqrt(temp)
    bend = amount * ((1.0 - PRANDTL) / 5.0) * per_t * per_t / pressure
    kappa = (0.5 * LOG2E) * per_t
    qu = qx * ux + qy * uy + qz * uz
    rest = uu - 5.0 * temp
    twice = -2.0 * bend * HALF**2
    kappa_sq = -kappa * HALF**2
    kappa_u = (2.0 * HALF) * kappa
    wall_sq = (-0.5 * LOG2E * HALF**2) * inverse
    bqu = bend * qu * HALF**2
    solid = jnp.where(boundary, OFF, 0.0)
    rows = {
        T_SQ_HI: kappa_sq, T_SQ_LO: kappa_sq,
        T_X: kappa_u * ux, T_Y: kappa_u * uy, T_Z: kappa_u * uz, T_ONE: -kappa * uu,
        P_ONE: amount - bend * qu * rest,
        P_X: bend * HALF * (qx * rest + 2.0 * qu * ux),
        P_Y: bend * HALF * (qy * rest + 2.0 * qu * uy),
        P_Z: bend * HALF * (qz * rest + 2.0 * qu * uz),
        P_XX: twice * qx * ux - bqu, P_YY: twice * qy * uy - bqu, P_ZZ: twice * qz * uz - bqu,
        P_XY: twice * (qx * uy + qy * ux), P_XZ: twice * (qx * uz + qz * ux),
        P_YZ: twice * (qy * uz + qz * uy),
        P_XS: bend * HALF**3 * qx, P_YS: bend * HALF**3 * qy, P_ZS: bend * HALF**3 * qz,
        W_SQ_HI: wall_sq, W_SQ_LO: wall_sq,
        W_ONE: jnp.where(boundary, 0.0, OFF),
        W_XP: jnp.where(code == 1, solid, 0.0), W_XN: jnp.where(code == 0, solid, 0.0),
        W_YP: jnp.where(code == 3, solid, 0.0), W_YN: jnp.where(code == 2, solid, 0.0),
        B_E: decay, B_W: em * decay * inverse * lax.rsqrt(wall),
    }
    rows[P_XSL], rows[P_YSL], rows[P_ZSL] = rows[P_XS], rows[P_YS], rows[P_ZS]
    zero = jnp.zeros_like(wall)
    for k in range(PART):
        value = rows.get(k)
        for part in range(2):
            if value is None:
                stack_ref[pl.ds(part * PART + k, groups, stride=STRIDE), :] = zero
                continue
            hi = value.astype(jnp.bfloat16).astype(jnp.float32)
            stack_ref[pl.ds(part * PART + k, groups, stride=STRIDE), :] = hi
            value = value - hi

    def turn(g, carry):
        block = stack_ref[pl.ds(g * STRIDE, COEF), :]
        coef_ref[pl.ds(pl.multiple_of(g * LANES, LANES), LANES), :] = block.T.astype(jnp.bfloat16)
        return carry

    lax.fori_loop(0, groups, turn, 0, unroll=8)
    if not with_edges:
        return
    size = low_ref.shape[0]
    for flat_ref, start, out_ref in ((first_ref, 0, low_ref), (last_ref, groups * LANES - size, high_ref)):
        coef = coef_ref[start:start + size, :]
        even = dot(coef, spread_ref[...])
        for l in range(flat_ref.shape[1] // WIDE):
            columns = slice(l * WIDE, (l + 1) * WIDE)
            out_ref[:, columns] = relaxed(coef, even, flat_ref[:, columns], target_ref[:, columns],
                                          factor_ref[:, columns], wall_ref[:, columns])


def state(with_edges, pieces, kind, code, temp, first, last, spread, tables):
    groups = kind.shape[0]
    whole = pl.BlockSpec(memory_space=pltpu.VMEM)
    operands = [*pieces, kind, code, temp]
    out_shape = (jax.ShapeDtypeStruct((groups * LANES, COEF), jnp.bfloat16),)
    if with_edges:
        operands += [first, last, spread, *tables]
        out_shape += (jax.ShapeDtypeStruct(first.shape, jnp.float32),) * 2
    else:
        out_shape += (jax.ShapeDtypeStruct((groups, LANES), jnp.float32),)
    return pl.pallas_call(
        functools.partial(state_kernel, len(pieces), groups, with_edges),
        out_shape=out_shape,
        in_specs=[whole] * len(operands),
        out_specs=(whole,) * len(out_shape),
        scratch_shapes=[pltpu.VMEM((groups * STRIDE + 7, LANES), jnp.float32),
                        pltpu.VMEM((GAS, groups, LANES), jnp.float32)],
        compiler_params=pltpu.CompilerParams(vmem_limit_bytes=SMALL_LIMIT),
        name="state",
    )(*operands)


WIDE = 256


def relaxed(coef, even, flat, target, factor, wall):
    exponent = dot(coef, target)
    factor = dot(coef, factor)
    wall = dot(coef, wall)
    decay, amount = even[:, :LANES], even[:, LANES:]
    parts = []
    for h in range(WIDE // LANES):
        cut = slice(h * LANES, (h + 1) * LANES)
        bounded = jnp.where(wall[:, cut] > 0.0, flat[:, cut] * decay, amount * jnp.exp2(wall[:, cut]))
        parts.append(bounded + jnp.exp2(exponent[:, cut]) * factor[:, cut])
    return jnp.concatenate(parts, axis=1)


def relax_block(spread_ref, tables, coef_ref, even_ref, flat_ref, store):
    even_ref[...] = dot(coef_ref[...], spread_ref[...])
    for l in range(flat_ref.shape[1] // WIDE):
        columns = slice(l * WIDE, (l + 1) * WIDE)
        target, factor, wall = (ref[:, columns] for ref in tables)
        store(l, relaxed(coef_ref[...], even_ref, flat_ref[:, columns], target, factor, wall))


PAD = 8
BLOCK = 8


def transport(exact, rows, field_ref, base, ncols, group, kind_ref, code_ref, sums_ref, stencil_ref,
              out_ref, parts_ref, strip_ref, half_ref):
    span = out_ref.shape[1]
    nothing = jnp.minimum(lax.axis_index("vel"), 0)
    shape = (ncols // 8, 8, LANES)
    unrolled = rows == BLOCK

    def lanes(l, carry):
        for h in range(WIDE // LANES):
            first = l * WIDE + h * LANES
            columns = slice(first, first + LANES) if unrolled else pl.ds(pl.multiple_of(first, LANES), LANES)
            x0, x1, x2, vx, y0, y1, y2, _ = (stencil_ref[8 * k:8 * k + 8, columns][None] for k in range(8))
            x_up = jnp.broadcast_to(vx > 0, shape)
            ahead = 1 if h == 0 else -1

            def field(k):
                start = pl.multiple_of(base + k * ncols, ncols)
                return field_ref[pl.ds(start, ncols), columns].reshape(shape)

            window = [field(k) for k in range(4)]
            for r in range(rows):
                window.append(field(r + 4))
                near = jnp.where(x_up, window[1], window[3])
                far = jnp.where(x_up, window[0], window[4])
                rowwise = x0 * window[2] + x1 * near + x2 * far
                window = window[1:]
                slot = h * BLOCK + r
                strip_ref[slot, PAD:PAD + ncols, :] = rowwise.reshape(ncols, LANES)

                def strip(k):
                    return strip_ref[slot, pl.ds(nothing + PAD + k, ncols), :].reshape(shape)

                value = y0 * rowwise + y1 * strip(ahead) + y2 * strip(2 * ahead)
                value = value.reshape(ncols, LANES)
                cut = slice(r * ncols, (r + 1) * ncols)
                out_ref[cut, columns] = value
                upper = value.astype(jnp.bfloat16)
                half_ref[0, cut, columns] = upper
                if exact:
                    half_ref[1, cut, columns] = (value - upper.astype(jnp.float32)).astype(jnp.bfloat16)
        return carry

    table = None
    if unrolled:
        for l in range(span // WIDE):
            lanes(l, 0)
            columns = slice(l * WIDE, (l + 1) * WIDE)
            for k in range(1 + exact):
                term = dot(half_ref[k, :, columns], sums_ref[columns, :])
                table = term if table is None else table + term
    else:
        lax.fori_loop(0, span // WIDE, lanes, 0)
        table = dot(half_ref[0], sums_ref[...])
        if exact:
            table = table + dot(half_ref[1], sums_ref[...])
    for g in range(rows * ncols // LANES):
        total = table[g * LANES:(g + 1) * LANES, :].T
        kind = kind_ref[pl.ds(group + g, 1), :]
        code = code_ref[pl.ds(group + g, 1), :]
        gas = kind == 0

        def keep(*codes):
            hit = (code == codes[0]) | (code == codes[1])
            return jnp.where(gas | jnp.logical_not(hit), 1.0, 0.0)

        kept = (keep(0, 2) * total[0:16] + keep(0, 3) * total[16:32]
                + keep(1, 2) * total[32:48] + keep(1, 3) * total[48:64])
        incident = jnp.where(code == 0, total[64:65], jnp.where(code == 1, total[65:66], jnp.where(
            code == 2, total[66:67], total[67:68])))
        parts_ref[pl.ds((group + g) * ROWS, ROWS), :] = jnp.concatenate(
            [kept[0:10], kept[10:13] + kept[13:16], incident], axis=0)


END = 2


def inner_kernel(relax, exact, blocks, ncols, flat_ref, kind_ref, code_ref, sums_ref, stencil_ref, *refs):
    if relax:
        coef_ref, spread_ref, target_ref, factor_ref, wall_ref, *refs = refs
    out_ref, parts_ref, head_ref, tail_ref, field_ref, even_ref, strip_ref, half_ref = refs
    i = pl.program_id(0)
    block = BLOCK * ncols
    span = flat_ref.shape[1]
    edge = END * ncols

    @pl.when(i == 0)
    def _():
        strip_ref[...] = jnp.zeros_like(strip_ref)
        blank = jnp.zeros((edge, span), jnp.float32)
        field_ref[:edge, :] = blank
        field_ref[field_ref.shape[0] - edge:, :] = blank

    @pl.when(i < blocks)
    def _():
        here = pl.ds(pl.multiple_of(edge + i * block, edge), block)

        if relax:
            def store(l, values):
                field_ref[here, l * WIDE:(l + 1) * WIDE] = values

            relax_block(spread_ref, (target_ref, factor_ref, wall_ref), coef_ref, even_ref, flat_ref, store)
        else:
            for l in range(span // WIDE):
                columns = slice(l * WIDE, (l + 1) * WIDE)
                for start in range(0, block, edge):
                    field_ref[pl.ds(pl.multiple_of(edge + i * block + start, edge), edge), columns] = turned(
                        flat_ref[start:start + edge, columns], l, span)

    @pl.when(i > 0)
    def _():
        transport(exact, BLOCK, field_ref, (i - 1) * block, ncols, (i - 1) * (block // LANES), kind_ref, code_ref,
                  sums_ref, stencil_ref, out_ref, parts_ref, strip_ref, half_ref)

    @pl.when(i == blocks)
    def _():
        size = head_ref.shape[0]
        last = field_ref.shape[0] - edge
        head_ref[...] = field_ref[edge:edge + size, :]
        tail_ref[...] = field_ref[last - size:last, :]


def outer_kernel(relax, exact, ncols, count, flat_ref, given_ref, head_ref, tail_ref, low_ref, high_ref,
                 kind_ref, code_ref, sums_ref, stencil_ref, out_ref, first_ref, last_ref, *refs):
    slot_refs = refs[:count]
    parts_ref, field_ref, strip_ref, half_ref, done_ref = refs[count:]
    edge = END * ncols
    size = head_ref.shape[0]
    span = first_ref.shape[1]
    groups = parts_ref.shape[0] // ROWS
    strip_ref[...] = jnp.zeros_like(strip_ref)
    parts_ref[...] = given_ref[...]

    def halo(ref, start):
        for l in range(span // WIDE):
            columns = slice(l * WIDE, (l + 1) * WIDE)
            values = ref[:, columns]
            field_ref[start:start + edge, columns] = values if relax else turned(values, l, span)

    halo(low_ref, 0)
    field_ref[edge:edge + size, :] = head_ref[...]
    field_ref[edge + size:edge + 2 * size, :] = tail_ref[...]
    halo(high_ref, edge + 2 * size)
    copies = []
    for k, (ref, base, group, start) in enumerate((
            (first_ref, 0, 0, 0), (last_ref, edge + size, groups - edge // LANES, out_ref.shape[0] - edge))):
        transport(exact, END, field_ref, base, ncols, group, kind_ref, code_ref,
                  sums_ref, stencil_ref, ref, parts_ref, strip_ref, half_ref)
        copies.append(pltpu.make_async_copy(ref, out_ref.at[pl.ds(start, edge), :], done_ref.at[k]))
        copies[-1].start()
    me = lax.axis_index("vel")
    rows = slot_refs[0].shape[0]
    for away, ref in enumerate(slot_refs):
        owner = lax.rem(me + away, count)
        ref[...] = parts_ref[pl.ds(pl.multiple_of(owner * rows, 4), rows), :]
    for copy in copies:
        copy.wait()


def inner(relax, exact, flat, coef, kind, code, spread, tables, sums, stencil, ncols):
    cells, span = flat.shape
    block = BLOCK * ncols
    blocks = cells // block
    groups = cells // LANES
    whole = pl.BlockSpec(memory_space=pltpu.VMEM)
    end = jax.ShapeDtypeStruct((2 * END * ncols, span), jnp.float32)
    operands = [flat, kind, code, sums, stencil]
    in_specs = [pl.BlockSpec((block, span), lambda i: (jnp.minimum(i, blocks - 1), 0))] + [whole] * 4
    if relax:
        operands += [coef, spread, *tables]
        in_specs += [pl.BlockSpec((block, COEF), lambda i: (jnp.minimum(i, blocks - 1), 0))] + [whole] * 4
    return pl.pallas_call(
        functools.partial(inner_kernel, relax, exact, blocks, ncols),
        grid=(blocks + 1,),
        out_shape=(jax.ShapeDtypeStruct((cells, span), jnp.float32),
                   jax.ShapeDtypeStruct((groups * ROWS, LANES), jnp.float32), end, end),
        in_specs=in_specs,
        out_specs=(pl.BlockSpec((block, span), lambda i: (jnp.maximum(i - 1, 0), 0)), whole, whole, whole),
        scratch_shapes=[pltpu.VMEM((cells + 2 * END * ncols, span), jnp.float32),
                        pltpu.VMEM((block, 2 * LANES), jnp.float32),
                        pltpu.VMEM((WIDE // LANES * BLOCK, ncols + 2 * PAD, LANES), jnp.float32),
                        pltpu.VMEM((1 + exact, block, span), jnp.bfloat16)],
        compiler_params=pltpu.CompilerParams(vmem_limit_bytes=VMEM_LIMIT),
        cost_estimate=pl.CostEstimate(flops=12 * cells * span * COEF, bytes_accessed=8 * cells * span,
                                      transcendentals=2 * cells * span),
        name="inner" if relax else "inner_first",
    )(*operands)


def outer(relax, exact, flat, parts, head, tail, low, high, kind, code, sums, stencil, ncols):
    cells, span = flat.shape
    edge = END * ncols
    count = lax.axis_size("vel")
    whole = pl.BlockSpec(memory_space=pltpu.VMEM)
    slot = jax.ShapeDtypeStruct((parts.shape[0] // count, LANES), jnp.float32)
    rim = jax.ShapeDtypeStruct((edge, span), jnp.float32)
    flat, first, last, *slots = pl.pallas_call(
        functools.partial(outer_kernel, relax, exact, ncols, count),
        out_shape=(jax.ShapeDtypeStruct((cells, span), jnp.float32), rim, rim) + (slot,) * count,
        in_specs=[pl.BlockSpec(memory_space=pl.ANY)] + [whole] * 9,
        out_specs=(pl.BlockSpec(memory_space=pl.ANY),) + (whole,) * (count + 2),
        scratch_shapes=[pltpu.VMEM(parts.shape, jnp.float32),
                        pltpu.VMEM((6 * edge, span), jnp.float32),
                        pltpu.VMEM((WIDE // LANES * BLOCK, ncols + 2 * PAD, LANES), jnp.float32),
                        pltpu.VMEM((1 + exact, edge, span), jnp.bfloat16),
                        pltpu.SemaphoreType.DMA((2,))],
        input_output_aliases={0: 0},
        compiler_params=pltpu.CompilerParams(vmem_limit_bytes=SMALL_LIMIT),
        name="outer" if relax else "outer_first",
    )(flat, parts, head, tail, low, high, kind, code, sums, stencil)
    return flat, first, last, slots


def last_kernel(flat_ref, coef_ref, spread_ref, target_ref, factor_ref, wall_ref, out_ref, even_ref):
    span = flat_ref.shape[1]

    def store(l, values):
        out_ref[:, l * WIDE:(l + 1) * WIDE] = turned(values, l, span, back=True)

    relax_block(spread_ref, (target_ref, factor_ref, wall_ref), coef_ref, even_ref, flat_ref, store)


def finish(flat, coef, spread, tables, ncols):
    cells, span = flat.shape
    block = 8 * ncols
    whole = pl.BlockSpec(memory_space=pltpu.VMEM)
    return pl.pallas_call(
        last_kernel,
        grid=(cells // block,),
        out_shape=jax.ShapeDtypeStruct((cells, span), jnp.float32),
        in_specs=[pl.BlockSpec((block, span), lambda i: (i, 0)),
                  pl.BlockSpec((block, COEF), lambda i: (i, 0)),
                  whole, whole, whole, whole],
        out_specs=pl.BlockSpec((block, span), lambda i: (i, 0)),
        scratch_shapes=[pltpu.VMEM((block, 2 * LANES), jnp.float32)],
        compiler_params=pltpu.CompilerParams(vmem_limit_bytes=VMEM_LIMIT),
        name="finish",
    )(flat, coef, spread, *tables)


def exchange(first, last):
    size = lax.axis_size("space")
    up = [(i, (i + 1) % size) for i in range(size - 1)]
    down = [(j, i) for i, j in up]
    return lax.ppermute(last, "space", up), lax.ppermute(first, "space", down)


def swap(slots):
    count = len(slots)
    return [slots[0]] + [lax.ppermute(slots[k], "vel", [(i, (i + k) % count) for i in range(count)])
                         for k in range(1, count)]


def shards(dist, cell_kind, normal_code, wall_temp):
    nrows, ncols, span = dist.shape
    cells = nrows * ncols
    flat = dist.reshape(cells, span)
    kind, code, temp, target, factor, wall, sums, stencil, spread = setup(span, cell_kind, normal_code, wall_temp)
    tables = (target, factor, wall)
    edge = 2 * ncols
    coef = None
    low, high = flat[:edge], flat[cells - edge:]
    for step in range(STEPS):
        final = step == STEPS - 1
        low, high = exchange(low, high)
        flat, parts, head, tail = inner(step > 0, final, flat, coef, kind, code, spread, tables, sums, stencil, ncols)
        flat, first, last, slots = outer(step > 0, final, flat, parts, head, tail, low, high, kind, code, sums, stencil, ncols)
        own = gas(swap(slots), kind, code, temp)
        coef, *others = state(not final, swap([own] * len(slots)), kind, code, temp, first, last, spread, tables)
        if not final:
            low, high = others
    flux = others[0]
    current = finish(flat, coef, spread, tables, ncols)
    columns = ncols // lax.axis_size("vel")
    own_flux = lax.dynamic_slice_in_dim(flux.reshape(nrows, ncols), lax.axis_index("vel") * columns, columns, 1)
    return current.reshape(nrows, ncols, span), own_flux


def solution(mesh):
    placed = (P("space", None, "vel"), P("space", None), P("space", None), P("space", None))
    return jax.shard_map(
        shards,
        mesh=mesh,
        in_specs=placed,
        out_specs=(P("space", None, "vel"), P("space", "vel")),
        check_vma=False,
    )
```

```python
import functools
import math

import jax
import jax.numpy as jnp
from jax import lax
from jax.experimental import pallas as pl
from jax.experimental.pallas import tpu as pltpu
from jax.sharding import PartitionSpec as P

NQ = 16
STEPS = 4
LIMIT = 5.0
TIME_STEP = 0.05
SIGMA = 0.8
LATENT = 5.0
PRANDTL = 2.0 / 3.0
SHEAR_EXPONENT = 0.1

SPACING = 2.0 * LIMIT / NQ
HALF = 0.5 * SPACING
WEIGHT = SPACING**3 / (2.0 * math.pi) ** 1.5
LOG2E = math.log2(math.e)
LANES = 128
MOMENTS = 16
ROWS = 14
GAS = 10
OFF = 1024.0

T_SQ_HI, T_SQ_LO, T_X, T_Y, T_Z, T_ONE = range(6)
P_ONE, P_X, P_Y, P_Z, P_XX, P_YY, P_ZZ, P_XY, P_XZ, P_YZ = range(6, 16)
P_XS, P_YS, P_ZS, P_XSL, P_YSL, P_ZSL = range(16, 22)
W_SQ_HI, W_SQ_LO, W_ONE, W_XP, W_XN, W_YP, W_YN = range(22, 29)
B_E, B_W = 29, 30
PART = 32
COEF = 2 * PART
STRIDE = COEF + 1

VMEM_LIMIT = 50 * 1024 * 1024
SMALL_LIMIT = 24 * 1024 * 1024


def setup_kernel(span, kind_in_ref, code_in_ref, temp_in_ref, kind_ref, code_ref, temp_ref, target_ref, factor_ref, wall_ref, sums_ref, stencil_ref, spread_ref,
                 feature_ref, moment_ref):
    for in_ref, ref in ((kind_in_ref, kind_ref), (code_in_ref, code_ref), (temp_in_ref, temp_ref)):
        ncols = in_ref.shape[1]
        joined = LANES // ncols
        for k in range(joined):
            ref[:, k * ncols:(k + 1) * ncols] = in_ref[pl.ds(k, ref.shape[0], stride=joined), :]
    shape = (8, span)
    place = lax.broadcasted_iota(jnp.int32, shape, 1)
    third = lax.axis_index("vel") * (span // WIDE) + place // WIDE
    first = place % NQ
    middle = place // NQ % NQ

    def odd(pick):
        return (2 * (pick % NQ) - (NQ - 1)).astype(jnp.float32)

    x, y, z = odd(first + third), odd(middle), odd(first + middle)
    one = jnp.ones(shape, jnp.float32)
    square = x * x + y * y + z * z
    square_hi = jnp.floor(square * (1.0 / 16.0)) * 16.0
    square_lo = square - square_hi

    def split(v):
        hi = jnp.floor(v * (1.0 / 128.0)) * 128.0
        return hi, v - hi

    xs, xsl = split(x * square)
    ys, ysl = split(y * square)
    zs, zsl = split(z * square)
    xp = jnp.where(x > 0, 1.0, 0.0)
    yp = jnp.where(y > 0, 1.0, 0.0)
    features = [square_hi, square_lo, x, y, z, one,
                one, x, y, z, x * x, y * y, z * z, x * y, x * z, y * z, xs, ys, zs, xsl, ysl, zsl,
                square_hi, square_lo, one, xp, one - xp, yp, one - yp]
    feature_ref[...] = jnp.zeros_like(feature_ref)
    for k, feature in enumerate(features):
        feature_ref[k:k + 1, :] = feature[0:1]
    row = lax.broadcasted_iota(jnp.int32, (PART, span), 0)
    for ref, low, high in ((target_ref, T_SQ_HI, P_ONE), (factor_ref, P_ONE, W_SQ_HI),
                           (wall_ref, W_SQ_HI, B_E)):
        chosen = jnp.where((row >= low) & (row < high), feature_ref[...], 0.0)
        ref[...] = jnp.concatenate([chosen, chosen], axis=0).astype(jnp.bfloat16)
    quadrants = (xp * yp, xp * (one - yp), (one - xp) * yp, (one - xp) * (one - yp))
    moment = feature_ref[P_ONE:W_SQ_HI, :]
    moment_ref[...] = jnp.zeros_like(moment_ref)
    for k, quadrant in enumerate(quadrants):
        moment_ref[MOMENTS * k:MOMENTS * (k + 1), :] = moment * quadrant[0:1]
    for k, speed in enumerate((-x, x, -y, y)):
        moment_ref[4 * MOMENTS + k:4 * MOMENTS + k + 1, :] = jnp.maximum(speed, 0.0)[0:1]
    for l in range(span // LANES):
        cut = slice(l * LANES, (l + 1) * LANES)
        sums_ref[cut, :] = moment_ref[:, cut].T.astype(jnp.bfloat16)
    for k, v in enumerate((x, y)):
        courant = jnp.abs(v) * (HALF * TIME_STEP)
        half_square = 0.5 * courant * courant
        for n, value in enumerate((1.0 - 1.5 * courant + half_square, 2.0 * courant - 2.0 * half_square,
                                   half_square - 0.5 * courant, v)):
            stencil_ref[8 * (4 * k + n):8 * (4 * k + n + 1), :] = value
    row = lax.broadcasted_iota(jnp.int32, (COEF, 2 * LANES), 0)
    column = lax.broadcasted_iota(jnp.int32, (COEF, 2 * LANES), 1)
    want = jnp.where(column < LANES, B_E, B_W)
    hit = row % PART == want
    spread_ref[...] = jnp.where(hit, 1.0, 0.0).astype(jnp.bfloat16)


def setup(span, *given):
    groups = given[0].size // LANES
    whole = pl.BlockSpec(memory_space=pltpu.VMEM)
    table = jax.ShapeDtypeStruct((COEF, span), jnp.bfloat16)
    return pl.pallas_call(
        functools.partial(setup_kernel, span),
        out_shape=tuple(jax.ShapeDtypeStruct((groups, LANES), g.dtype) for g in given) + (table, table, table,
                   jax.ShapeDtypeStruct((span, LANES), jnp.bfloat16),
                   jax.ShapeDtypeStruct((64, span), jnp.float32),
                   jax.ShapeDtypeStruct((COEF, 2 * LANES), jnp.bfloat16)),
        in_specs=[whole] * 3,
        out_specs=(whole,) * 9,
        scratch_shapes=[pltpu.VMEM((PART, span), jnp.float32), pltpu.VMEM((LANES, span), jnp.float32)],
        name="setup",
    )(*given)


def turned(values, l, span, back=False):
    third = lax.axis_index("vel") * (span // WIDE) + l
    shift = NQ * (third % NQ)
    return pltpu.roll(values, (WIDE - shift) % WIDE if back else shift, 1)


def dot(a, b):
    return jnp.dot(a, b, preferred_element_type=jnp.float32)


def gas_kernel(count, size, *refs):
    part_refs = refs[:count]
    kind_ref, code_ref, temp_ref, out_ref = refs[count:]
    mine = pl.ds(pl.multiple_of(lax.axis_index("vel") * size, size), size)

    def read(k, scale):
        value = part_refs[0][pl.ds(k, size, stride=ROWS), :]
        for ref in part_refs[1:]:
            value = value + ref[pl.ds(k, size, stride=ROWS), :]
        return value * (WEIGHT * scale)

    kind = kind_ref[mine, :]
    code = code_ref[mine, :]
    wall = temp_ref[mine, :]
    s0 = s1 = s2 = s3 = jnp.zeros_like(wall)
    inverse = 1.0 / wall
    for j in range(NQ // 2):
        speed = HALF * (2 * j + 1)
        e = jnp.exp(inverse * (-0.5 * speed * speed))
        s0, s1, s2, s3 = s0 + e, s1 + speed * e, s2 + speed**2 * e, s3 + speed**3 * e
    scale = (WEIGHT * 2.0) * inverse * lax.rsqrt(wall)
    norm = 2.0 * scale * s1 * s0 * s0
    f_one = 2.0 * scale * s0 * s0 * s0
    f_nn = 2.0 * scale * s2 * s0 * s0
    f_tt = f_nn
    f_ns = 2.0 * scale * (s3 * s0 * s0 + 2.0 * s1 * s2 * s0)
    saturated = jnp.exp(LATENT * (1.0 - inverse)) * inverse
    incident = read(13, HALF)
    share = jnp.where(kind == 2, SIGMA, 0.0)
    emitted = share * saturated + (1.0 - share) * incident / norm
    boundary = kind > 0
    flux = jnp.where(boundary, emitted * norm - incident, 0.0)
    em = jnp.where(boundary, emitted, 0.0)
    along_x = code < 2
    sign = jnp.where((code == 0) | (code == 2), 1.0, -1.0)
    sx = jnp.where(along_x, sign, 0.0)
    sy = jnp.where(along_x, 0.0, sign)

    rho = read(0, 1.0) + em * f_one
    em_n = em * norm
    em_s = em * f_ns
    mx = read(1, HALF) + sx * em_n
    my = read(2, HALF) + sy * em_n
    mz = read(3, HALF)
    mxx = read(4, HALF**2) + em * f_nn
    myy = read(5, HALF**2) + em * f_tt
    mzz = read(6, HALF**2) + em * f_tt
    mxy = read(7, HALF**2)
    mxz = read(8, HALF**2)
    myz = read(9, HALF**2)
    mxs = read(10, HALF**3) + sx * em_s
    mys = read(11, HALF**3) + sy * em_s
    mzs = read(12, HALF**3)
    msq = mxx + myy + mzz
    per = 1.0 / rho
    ux, uy, uz = mx * per, my * per, mz * per
    uu = ux * ux + uy * uy + uz * uz
    temp = (msq * per - uu) * (1.0 / 3.0)
    dotted = ux * mx + uy * my + uz * mz

    def heat(third, u, m, second):
        return 0.5 * (third - 2.0 * (ux * second[0] + uy * second[1] + uz * second[2]) + uu * m
                      - u * msq + 2.0 * u * dotted - u * uu * rho)

    qx = heat(mxs, ux, mx, (mxx, mxy, mxz))
    qy = heat(mys, uy, my, (mxy, myy, myz))
    qz = heat(mzs, uz, mz, (mxz, myz, mzz))
    for k, value in enumerate((rho, ux, uy, uz, temp, qx, qy, qz, em, flux)):
        out_ref[k * size:(k + 1) * size, :] = value


def gas(parts, kind, code, temp):
    size = parts[0].shape[0] // ROWS
    whole = pl.BlockSpec(memory_space=pltpu.VMEM)
    return pl.pallas_call(
        functools.partial(gas_kernel, len(parts), size),
        out_shape=jax.ShapeDtypeStruct((GAS * size, LANES), jnp.float32),
        in_specs=[whole] * (len(parts) + 3),
        out_specs=whole,
        name="gas",
    )(*parts, kind, code, temp)


def state_kernel(count, groups, with_edges, *refs):
    piece_refs = refs[:count]
    kind_ref, code_ref, temp_ref, *refs = refs[count:]
    if with_edges:
        first_ref, last_ref, spread_ref, target_ref, factor_ref, wall_ref, coef_ref, low_ref, high_ref, *refs = refs
    else:
        coef_ref, flux_ref, *refs = refs
    stack_ref, field_ref = refs
    size = groups // count
    me = lax.axis_index("vel")
    for away, ref in enumerate(piece_refs):
        owner = lax.rem(me + (count - away), count)
        for k in range(GAS):
            field_ref[k, pl.ds(pl.multiple_of(owner * size, size), size), :] = ref[k * size:(k + 1) * size, :]
    kind = kind_ref[...]
    code = code_ref[...]
    wall = temp_ref[...]
    rho, ux, uy, uz, temp, qx, qy, qz, em, flux = (field_ref[k] for k in range(GAS))
    if not with_edges:
        flux_ref[...] = flux
    inverse = 1.0 / wall
    uu = ux * ux + uy * uy + uz * uz
    boundary = kind > 0
    pressure = rho * temp
    per_t = 1.0 / temp
    decay = jnp.exp((-TIME_STEP / SHEAR_EXPONENT) * pressure * jnp.exp(-0.72 * jnp.log(temp)))
    amount = (1.0 - decay) * rho * per_t * lax.rsqrt(temp)
    bend = amount * ((1.0 - PRANDTL) / 5.0) * per_t * per_t / pressure
    kappa = (0.5 * LOG2E) * per_t
    qu = qx * ux + qy * uy + qz * uz
    rest = uu - 5.0 * temp
    twice = -2.0 * bend * HALF**2
    kappa_sq = -kappa * HALF**2
    kappa_u = (2.0 * HALF) * kappa
    wall_sq = (-0.5 * LOG2E * HALF**2) * inverse
    bqu = bend * qu * HALF**2
    solid = jnp.where(boundary, OFF, 0.0)
    rows = {
        T_SQ_HI: kappa_sq, T_SQ_LO: kappa_sq,
        T_X: kappa_u * ux, T_Y: kappa_u * uy, T_Z: kappa_u * uz, T_ONE: -kappa * uu,
        P_ONE: amount - bend * qu * rest,
        P_X: bend * HALF * (qx * rest + 2.0 * qu * ux),
        P_Y: bend * HALF * (qy * rest + 2.0 * qu * uy),
        P_Z: bend * HALF * (qz * rest + 2.0 * qu * uz),
        P_XX: twice * qx * ux - bqu, P_YY: twice * qy * uy - bqu, P_ZZ: twice * qz * uz - bqu,
        P_XY: twice * (qx * uy + qy * ux), P_XZ: twice * (qx * uz + qz * ux),
        P_YZ: twice * (qy * uz + qz * uy),
        P_XS: bend * HALF**3 * qx, P_YS: bend * HALF**3 * qy, P_ZS: bend * HALF**3 * qz,
        W_SQ_HI: wall_sq, W_SQ_LO: wall_sq,
        W_ONE: jnp.where(boundary, 0.0, OFF),
        W_XP: jnp.where(code == 1, solid, 0.0), W_XN: jnp.where(code == 0, solid, 0.0),
        W_YP: jnp.where(code == 3, solid, 0.0), W_YN: jnp.where(code == 2, solid, 0.0),
        B_E: decay, B_W: em * decay * inverse * lax.rsqrt(wall),
    }
    rows[P_XSL], rows[P_YSL], rows[P_ZSL] = rows[P_XS], rows[P_YS], rows[P_ZS]
    zero = jnp.zeros_like(wall)
    for k in range(PART):
        value = rows.get(k)
        for part in range(2):
            if value is None:
                stack_ref[pl.ds(part * PART + k, groups, stride=STRIDE), :] = zero
                continue
            hi = value.astype(jnp.bfloat16).astype(jnp.float32)
            stack_ref[pl.ds(part * PART + k, groups, stride=STRIDE), :] = hi
            value = value - hi

    def turn(g, carry):
        block = stack_ref[pl.ds(g * STRIDE, COEF), :]
        coef_ref[pl.ds(pl.multiple_of(g * LANES, LANES), LANES), :] = block.T.astype(jnp.bfloat16)
        return carry

    lax.fori_loop(0, groups, turn, 0, unroll=8)
    if not with_edges:
        return
    size = low_ref.shape[0]
    for flat_ref, start, out_ref in ((first_ref, 0, low_ref), (last_ref, groups * LANES - size, high_ref)):
        coef = coef_ref[start:start + size, :]
        even = dot(coef, spread_ref[...])
        for l in range(flat_ref.shape[1] // WIDE):
            columns = slice(l * WIDE, (l + 1) * WIDE)
            out_ref[:, columns] = relaxed(coef, even, flat_ref[:, columns], target_ref[:, columns],
                                          factor_ref[:, columns], wall_ref[:, columns])


def state(with_edges, pieces, kind, code, temp, first, last, spread, tables):
    groups = kind.shape[0]
    whole = pl.BlockSpec(memory_space=pltpu.VMEM)
    operands = [*pieces, kind, code, temp]
    out_shape = (jax.ShapeDtypeStruct((groups * LANES, COEF), jnp.bfloat16),)
    if with_edges:
        operands += [first, last, spread, *tables]
        out_shape += (jax.ShapeDtypeStruct(first.shape, jnp.float32),) * 2
    else:
        out_shape += (jax.ShapeDtypeStruct((groups, LANES), jnp.float32),)
    return pl.pallas_call(
        functools.partial(state_kernel, len(pieces), groups, with_edges),
        out_shape=out_shape,
        in_specs=[whole] * len(operands),
        out_specs=(whole,) * len(out_shape),
        scratch_shapes=[pltpu.VMEM((groups * STRIDE + 7, LANES), jnp.float32),
                        pltpu.VMEM((GAS, groups, LANES), jnp.float32)],
        compiler_params=pltpu.CompilerParams(vmem_limit_bytes=SMALL_LIMIT),
        name="state",
    )(*operands)


WIDE = 256


def relaxed(coef, even, flat, target, factor, wall):
    exponent = dot(coef, target)
    factor = dot(coef, factor)
    wall = dot(coef, wall)
    decay, amount = even[:, :LANES], even[:, LANES:]
    parts = []
    for h in range(WIDE // LANES):
        cut = slice(h * LANES, (h + 1) * LANES)
        bounded = jnp.where(wall[:, cut] > 0.0, flat[:, cut] * decay, amount * jnp.exp2(wall[:, cut]))
        parts.append(bounded + jnp.exp2(exponent[:, cut]) * factor[:, cut])
    return jnp.concatenate(parts, axis=1)


CELLS = 512


def relax_tiles(cells, spread_ref, tables, coef_ref, even_ref, flat_ref, store):
    target_ref, factor_ref, wall_ref = tables
    span = flat_ref.shape[1]

    def block(b, carry):
        start = pl.multiple_of(b * CELLS, CELLS)
        coef = coef_ref[pl.ds(start, CELLS), :]
        even_ref[...] = dot(coef, spread_ref[...])
        for l in range(span // WIDE):
            columns = slice(l * WIDE, (l + 1) * WIDE)
            store(start, l, relaxed(coef, even_ref, flat_ref[pl.ds(start, CELLS), columns],
                                    target_ref[:, columns], factor_ref[:, columns], wall_ref[:, columns]))
        return carry

    lax.fori_loop(0, cells // CELLS, block, 0)


PAD = 8
BLOCK = 8


def transport(exact, rows, field_ref, base, ncols, group, kind_ref, code_ref, sums_ref, stencil_ref,
              out_ref, parts_ref, strip_ref, half_ref):
    span = out_ref.shape[1]
    nothing = jnp.minimum(pl.program_id(0) if rows == BLOCK else lax.axis_index("vel"), 0)
    shape = (ncols // 8, 8, LANES)
    unrolled = rows == BLOCK

    def lanes(l, carry):
        for h in range(WIDE // LANES):
            first = l * WIDE + h * LANES
            columns = slice(first, first + LANES) if unrolled else pl.ds(pl.multiple_of(first, LANES), LANES)
            x0, x1, x2, vx, y0, y1, y2, _ = (stencil_ref[8 * k:8 * k + 8, columns][None] for k in range(8))
            x_up = jnp.broadcast_to(vx > 0, shape)
            ahead = 1 if h == 0 else -1

            def field(k):
                start = pl.multiple_of(base + k * ncols, ncols)
                return field_ref[pl.ds(start, ncols), columns].reshape(shape)

            window = [field(k) for k in range(4)]
            for r in range(rows):
                window.append(field(r + 4))
                near = jnp.where(x_up, window[1], window[3])
                far = jnp.where(x_up, window[0], window[4])
                rowwise = x0 * window[2] + x1 * near + x2 * far
                window = window[1:]
                slot = h * BLOCK + r
                strip_ref[slot, PAD:PAD + ncols, :] = rowwise.reshape(ncols, LANES)

                def strip(k):
                    return strip_ref[slot, pl.ds(nothing + PAD + k, ncols), :].reshape(shape)

                value = y0 * rowwise + y1 * strip(ahead) + y2 * strip(2 * ahead)
                value = value.reshape(ncols, LANES)
                cut = slice(r * ncols, (r + 1) * ncols)
                out_ref[cut, columns] = value
                upper = value.astype(jnp.bfloat16)
                half_ref[0, cut, columns] = upper
                if exact:
                    half_ref[1, cut, columns] = (value - upper.astype(jnp.float32)).astype(jnp.bfloat16)
        return carry

    table = None
    if unrolled:
        for l in range(span // WIDE):
            lanes(l, 0)
            columns = slice(l * WIDE, (l + 1) * WIDE)
            for k in range(1 + exact):
                term = dot(half_ref[k, :, columns], sums_ref[columns, :])
                table = term if table is None else table + term
    else:
        lax.fori_loop(0, span // WIDE, lanes, 0)
        table = dot(half_ref[0], sums_ref[...])
        if exact:
            table = table + dot(half_ref[1], sums_ref[...])
    for g in range(rows * ncols // LANES):
        total = table[g * LANES:(g + 1) * LANES, :].T
        kind = kind_ref[pl.ds(group + g, 1), :]
        code = code_ref[pl.ds(group + g, 1), :]
        gas = kind == 0

        def keep(*codes):
            hit = (code == codes[0]) | (code == codes[1])
            return jnp.where(gas | jnp.logical_not(hit), 1.0, 0.0)

        kept = (keep(0, 2) * total[0:16] + keep(0, 3) * total[16:32]
                + keep(1, 2) * total[32:48] + keep(1, 3) * total[48:64])
        incident = jnp.where(code == 0, total[64:65], jnp.where(code == 1, total[65:66], jnp.where(
            code == 2, total[66:67], total[67:68])))
        parts_ref[pl.ds((group + g) * ROWS, ROWS), :] = jnp.concatenate(
            [kept[0:10], kept[10:13] + kept[13:16], incident], axis=0)


END = 2


def patch(i, blocks, flat_ref, first_ref, last_ref):
    edge = first_ref.shape[0]

    @pl.when(i == 0)
    def _():
        flat_ref[:edge, :] = first_ref[...]

    @pl.when(i == blocks - 1)
    def _():
        flat_ref[flat_ref.shape[0] - edge:, :] = last_ref[...]


def inner_kernel(relax, exact, blocks, ncols, flat_ref, kind_ref, code_ref, sums_ref, stencil_ref, *refs):
    if relax:
        coef_ref, spread_ref, target_ref, factor_ref, wall_ref, first_ref, last_ref, *refs = refs
    out_ref, parts_ref, head_ref, tail_ref, field_ref, even_ref, strip_ref, half_ref = refs
    i = pl.program_id(0)
    block = BLOCK * ncols
    span = flat_ref.shape[1]
    edge = END * ncols

    @pl.when(i == 0)
    def _():
        strip_ref[...] = jnp.zeros_like(strip_ref)
        blank = jnp.zeros((edge, span), jnp.float32)
        field_ref[:edge, :] = blank
        field_ref[field_ref.shape[0] - edge:, :] = blank

    @pl.when(i < blocks)
    def _():
        if relax:
            def store(start, l, values):
                cells = pl.ds(pl.multiple_of(edge + i * block + start, edge), CELLS)
                field_ref[cells, l * WIDE:(l + 1) * WIDE] = values

            patch(i, blocks, flat_ref, first_ref, last_ref)
            relax_tiles(block, spread_ref, (target_ref, factor_ref, wall_ref), coef_ref, even_ref, flat_ref, store)
        else:
            for l in range(span // WIDE):
                columns = slice(l * WIDE, (l + 1) * WIDE)
                for start in range(0, block, edge):
                    field_ref[pl.ds(pl.multiple_of(edge + i * block + start, edge), edge), columns] = turned(
                        flat_ref[start:start + edge, columns], l, span)

    @pl.when(i > 0)
    def _():
        transport(exact, BLOCK, field_ref, (i - 1) * block, ncols, (i - 1) * (block // LANES), kind_ref, code_ref,
                  sums_ref, stencil_ref, out_ref, parts_ref, strip_ref, half_ref)

    @pl.when(i == blocks)
    def _():
        size = head_ref.shape[0]
        last = field_ref.shape[0] - edge
        head_ref[...] = field_ref[edge:edge + size, :]
        tail_ref[...] = field_ref[last - size:last, :]


def outer_kernel(relax, exact, ncols, count, given_ref, head_ref, tail_ref, low_ref, high_ref,
                 kind_ref, code_ref, sums_ref, stencil_ref, first_ref, last_ref, *refs):
    slot_refs = refs[:count]
    parts_ref, field_ref, strip_ref, half_ref = refs[count:]
    edge = END * ncols
    size = head_ref.shape[0]
    span = first_ref.shape[1]
    groups = parts_ref.shape[0] // ROWS
    strip_ref[...] = jnp.zeros_like(strip_ref)
    parts_ref[...] = given_ref[...]

    def halo(ref, start):
        for l in range(span // WIDE):
            columns = slice(l * WIDE, (l + 1) * WIDE)
            values = ref[:, columns]
            field_ref[start:start + edge, columns] = values if relax else turned(values, l, span)

    halo(low_ref, 0)
    field_ref[edge:edge + size, :] = head_ref[...]
    field_ref[edge + size:edge + 2 * size, :] = tail_ref[...]
    halo(high_ref, edge + 2 * size)
    for ref, base, group in ((first_ref, 0, 0), (last_ref, edge + size, groups - edge // LANES)):
        transport(exact, END, field_ref, base, ncols, group, kind_ref, code_ref,
                  sums_ref, stencil_ref, ref, parts_ref, strip_ref, half_ref)
    me = lax.axis_index("vel")
    rows = slot_refs[0].shape[0]
    for away, ref in enumerate(slot_refs):
        owner = lax.rem(me + away, count)
        ref[...] = parts_ref[pl.ds(pl.multiple_of(owner * rows, 4), rows), :]


def inner(relax, exact, flat, first, last, coef, kind, code, spread, tables, sums, stencil, ncols):
    cells, span = flat.shape
    block = BLOCK * ncols
    blocks = cells // block
    groups = cells // LANES
    whole = pl.BlockSpec(memory_space=pltpu.VMEM)
    end = jax.ShapeDtypeStruct((2 * END * ncols, span), jnp.float32)
    operands = [flat, kind, code, sums, stencil]
    in_specs = [pl.BlockSpec((block, span), lambda i: (jnp.minimum(i, blocks - 1), 0))] + [whole] * 4
    if relax:
        operands += [coef, spread, *tables, first, last]
        in_specs += [pl.BlockSpec((block, COEF), lambda i: (jnp.minimum(i, blocks - 1), 0))] + [whole] * 6
    return pl.pallas_call(
        functools.partial(inner_kernel, relax, exact, blocks, ncols),
        grid=(blocks + 1,),
        out_shape=(jax.ShapeDtypeStruct((cells, span), jnp.float32),
                   jax.ShapeDtypeStruct((groups * ROWS, LANES), jnp.float32), end, end),
        in_specs=in_specs,
        out_specs=(pl.BlockSpec((block, span), lambda i: (jnp.maximum(i - 1, 0), 0)), whole, whole, whole),
        scratch_shapes=[pltpu.VMEM((cells + 2 * END * ncols, span), jnp.float32),
                        pltpu.VMEM((block, 2 * LANES), jnp.float32),
                        pltpu.VMEM((WIDE // LANES * BLOCK, ncols + 2 * PAD, LANES), jnp.float32),
                        pltpu.VMEM((1 + exact, block, span), jnp.bfloat16)],
        compiler_params=pltpu.CompilerParams(vmem_limit_bytes=VMEM_LIMIT),
        cost_estimate=pl.CostEstimate(flops=12 * cells * span * COEF, bytes_accessed=8 * cells * span,
                                      transcendentals=2 * cells * span),
        name="inner" if relax else "inner_first",
    )(*operands)


def outer(relax, exact, parts, head, tail, low, high, kind, code, sums, stencil, ncols):
    span = head.shape[1]
    edge = END * ncols
    count = lax.axis_size("vel")
    whole = pl.BlockSpec(memory_space=pltpu.VMEM)
    slot = jax.ShapeDtypeStruct((parts.shape[0] // count, LANES), jnp.float32)
    rim = jax.ShapeDtypeStruct((edge, span), jnp.float32)
    first, last, *slots = pl.pallas_call(
        functools.partial(outer_kernel, relax, exact, ncols, count),
        out_shape=(rim, rim) + (slot,) * count,
        in_specs=[whole] * 9,
        out_specs=(whole,) * (count + 2),
        scratch_shapes=[pltpu.VMEM(parts.shape, jnp.float32),
                        pltpu.VMEM((6 * edge, span), jnp.float32),
                        pltpu.VMEM((WIDE // LANES * BLOCK, ncols + 2 * PAD, LANES), jnp.float32),
                        pltpu.VMEM((1 + exact, edge, span), jnp.bfloat16)],
        compiler_params=pltpu.CompilerParams(vmem_limit_bytes=SMALL_LIMIT),
        name="outer" if relax else "outer_first",
    )(parts, head, tail, low, high, kind, code, sums, stencil)
    return first, last, slots


def last_kernel(blocks, flat_ref, coef_ref, spread_ref, target_ref, factor_ref, wall_ref, first_ref, last_ref,
                out_ref, even_ref):
    span = flat_ref.shape[1]

    def store(start, l, values):
        out_ref[pl.ds(start, CELLS), l * WIDE:(l + 1) * WIDE] = turned(values, l, span, back=True)

    patch(pl.program_id(0), blocks, flat_ref, first_ref, last_ref)
    relax_tiles(flat_ref.shape[0], spread_ref, (target_ref, factor_ref, wall_ref), coef_ref, even_ref,
                flat_ref, store)


def finish(flat, first, last, coef, spread, tables, ncols):
    cells, span = flat.shape
    block = 8 * ncols
    whole = pl.BlockSpec(memory_space=pltpu.VMEM)
    return pl.pallas_call(
        functools.partial(last_kernel, cells // block),
        grid=(cells // block,),
        out_shape=jax.ShapeDtypeStruct((cells, span), jnp.float32),
        in_specs=[pl.BlockSpec((block, span), lambda i: (i, 0)),
                  pl.BlockSpec((block, COEF), lambda i: (i, 0)),
                  whole, whole, whole, whole, whole, whole],
        out_specs=pl.BlockSpec((block, span), lambda i: (i, 0)),
        scratch_shapes=[pltpu.VMEM((block, 2 * LANES), jnp.float32)],
        compiler_params=pltpu.CompilerParams(vmem_limit_bytes=VMEM_LIMIT),
        name="finish",
    )(flat, coef, spread, *tables, first, last)


def exchange(first, last):
    size = lax.axis_size("space")
    up = [(i, (i + 1) % size) for i in range(size - 1)]
    down = [(j, i) for i, j in up]
    return lax.ppermute(last, "space", up), lax.ppermute(first, "space", down)


def swap(slots):
    count = len(slots)
    return [slots[0]] + [lax.ppermute(slots[k], "vel", [(i, (i + k) % count) for i in range(count)])
                         for k in range(1, count)]


def shards(dist, cell_kind, normal_code, wall_temp):
    nrows, ncols, span = dist.shape
    cells = nrows * ncols
    flat = dist.reshape(cells, span)
    kind, code, temp, target, factor, wall, sums, stencil, spread = setup(span, cell_kind, normal_code, wall_temp)
    tables = (target, factor, wall)
    edge = 2 * ncols
    coef = first = last = None
    low, high = flat[:edge], flat[cells - edge:]
    for step in range(STEPS):
        final = step == STEPS - 1
        low, high = exchange(low, high)
        flat, parts, head, tail = inner(step > 0, final, flat, first, last, coef, kind, code, spread, tables, sums, stencil, ncols)
        first, last, slots = outer(step > 0, final, parts, head, tail, low, high, kind, code, sums, stencil, ncols)
        own = gas(swap(slots), kind, code, temp)
        coef, *others = state(not final, swap([own] * len(slots)), kind, code, temp, first, last, spread, tables)
        if not final:
            low, high = others
    flux = others[0]
    current = finish(flat, first, last, coef, spread, tables, ncols)
    columns = ncols // lax.axis_size("vel")
    own_flux = lax.dynamic_slice_in_dim(flux.reshape(nrows, ncols), lax.axis_index("vel") * columns, columns, 1)
    return current.reshape(nrows, ncols, span), own_flux


def solution(mesh):
    placed = (P("space", None, "vel"), P("space", None), P("space", None), P("space", None))
    return jax.shard_map(
        shards,
        mesh=mesh,
        in_specs=placed,
        out_specs=(P("space", None, "vel"), P("space", "vel")),
        check_vma=False,
    )
```
